256 devices in a mesh: space: 64 (over z_hi, y, x, core), band: 4 (over z_lo).
Axes of the slice: x: 4, y: 4, z: 8 (z_hi: 2, z_lo: 4; z = z_hi * 4 + z_lo), core: 2. Of those that a mesh axis runs over, the one named last changes fastest.
Arguments:
- phonon_deviation: float32 [24, 96, 32768], P('band', None, 'space'), may hold values from -6 to 6
- thermal_field: float32 [128, 128, 128], P('space'), may hold values from -6 to 6
- bulk_generation: float32 [128, 128, 128], P('space'), may hold values from -6 to 6
- ambient_coupling: float32 [128, 128, 128], P('space'), may hold values from 0.5 to 1
- substance_label: int32 [128, 128, 128], P('space'), may hold values from 0 to 7
- material_conductance_table: float32 [8], replicated, may hold values from 2 to 4
- mode_specific_warmth: float32 [24], replicated, may hold values from 0.3 to 3
- mode_lifetime: float32 [24], replicated, may hold values from 0.2 to 5
- mode_velocity_ratio: float32 [24], replicated, may hold values from 0.5 to 5
- angular_cosine_factor: float32 [6, 96], replicated, may hold values from -0.05 to 0.05
- region_mesh_node: int32 [32768], P('space'), may hold values from 0 to 32767
- upstream_neighbour: int32 [8, 32768], P(None, 'space'), may hold values from -1 to 511, as said below
- interior_local_node: int32 [16384], P('space'), may hold values from 0 to 511
- boundary_orientation: int32 [16384], P('space'), may hold values from 0 to 5
- neighbour_partition: int32 [16384, 1], P('space'), may hold values from 0 to 63; in each aligned block of 256 rows (0 to 255, 256 to 511, ...) at most 8 rows name the same one
- exterior_local_node: int32 [16384], P('space'), may hold values from 0 to 32767
Outputs:
- temperature_out: float32 [128, 128, 128], P('space')
- intensity_out: float32 [24, 96, 32768], P('band', None, 'space')
The draws below stay inside these ranges and needn't reach their ends.
Inputs may be any that keep to these rules, and one draw needn't show every extreme that they name: `upstream_neighbour`: -1 marks an inflow cell; other values are patch cells of the same tile. `neighbour_partition`: among the 256 faces of one tile, at most 8 name the same owner.
All inputs are finite; a program needn't handle non-finite values.
Results may differ from the reference program's by a relative error of at most 0.0001.
Values sent between devices are 32-bit elements; how exact they have to be, the bound alone decides.
No kernel may reach another device: no remote copies, remote signals or barrier semaphores. Data moves between devices by JAX's collectives and lax.ppermute only.
A program may use at most 64 MiB of HBM per device.

```python
import math
import jax
import jax.numpy as jnp
import numpy as np

BANDS = 24
NDIR = 96
DBLK = 8
SWEEPS = 2
ITERS = 20
NMAT = 8
PATCH = 512
NFACE = 256
NODES_MIDDLE_AX = 128
NODES_TRAILING_AX = 128
CAP = 8
NODES_EACH_BLOCK = 32768
NODES_LEADING_AX = 128
PATCH_TOTAL = 32768
FACE_TOTAL = 16384
N_SPACE = 64


def draw_upstream_neighbour(key, part):
    key = jax.random.fold_in(key, 11)
    first_key, second_key = jax.random.split(key)
    cells = jax.random.randint(first_key, (DBLK, PATCH_TOTAL), 0, PATCH)
    inflow = jax.random.randint(second_key, (DBLK, PATCH_TOTAL), 0, 4) == 0
    result = jnp.where(inflow, -1, cells).astype(jnp.int32)
    result = result.at[:, 0].set(-1)
    result = result.at[:, 1].set(PATCH - 1)
    return result


def draw_thermal_field(key, part):
    key = jax.random.fold_in(key, 17)
    shape = (NODES_LEADING_AX, NODES_MIDDLE_AX, NODES_TRAILING_AX)
    rows = jnp.arange(NODES_LEADING_AX, dtype=jnp.int32)
    parity = (rows % 2).astype(jnp.float32)
    alternating = (1.0 - 2.0 * parity)[:, None, None]
    magnitude = jax.random.uniform(key, shape, jnp.float32, 1.5, 6.0)
    return (alternating * magnitude).astype(jnp.float32)


def with_ends(values, own_key, least, high):
    longest = values.shape.index(max(values.shape))
    spots = []
    for shift in (0, 1):
        where = [jax.random.randint(jax.random.fold_in(own_key, axis), (), 0, length) for axis, length in enumerate(values.shape)]
        where[longest] = (where[longest] + shift) % values.shape[longest]
        spots.append(tuple(where))
    return values.at[spots[0]].set(least).at[spots[1]].set(high)


def shard_levels(stream_key, dims, pieces, smallest, largest):
    level = 1.0
    for dim, shards_of in pieces:
        heights = jax.random.uniform(jax.random.fold_in(jax.random.fold_in(stream_key, 6), dim), (shards_of,), jnp.float32, smallest / len(pieces), largest / len(pieces))
        level = level * jnp.repeat(jnp.exp(heights), dims[dim] // shards_of).reshape((-1,) + (1,) * (len(dims) - 1 - dim))
    return level


def deal_out(key, own, number, rows, count, top, reach, lean):
    ranking = jax.random.permutation(key, count)
    crowded, usual = shares(count, rows * top, reach, lean, True), shares(count, rows * top, reach, lean, False)
    places = jnp.arange(count)

    def named(lengths, offset_by):
        used = int((lengths > 0).sum())
        fixed = max(1, used // 4)
        passed = fixed + (places - fixed + offset_by * (used - fixed)) % max(1, count - fixed)
        return jnp.zeros((count,), jnp.int32).at[ranking[jnp.where(places < fixed, places, passed)]].set(jnp.asarray(lengths, jnp.int32))

    lengths = jnp.where(number % 4 == 0, named(crowded, number // 4), named(usual, number - number // 4 - 1))
    mixed = jax.random.permutation(jax.random.fold_in(own, 3), count)
    giver, taker = mixed[0:count // 2 * 2:2], mixed[1:count // 2 * 2:2]
    room = jnp.minimum(lengths[giver] - 1, reach - lengths[taker]) // 2
    room = jnp.where((giver == ranking[0]) | (taker == ranking[0]) | (lengths[taker] == 0), 0, jnp.maximum(room, 0))
    passed = jax.random.randint(jax.random.fold_in(own, 4), (count // 2,), 0, 1 << 20) % (room + 1)
    lengths = lengths.at[giver].add(-passed).at[taker].add(passed)
    items = jnp.searchsorted(jnp.cumsum(lengths), jnp.arange(rows * top), side="right").astype(jnp.int32)
    grid = items.reshape(top, rows).T
    grid = grid[jax.random.permutation(jax.random.fold_in(own, 1), rows)]
    offset_by = jax.random.randint(jax.random.fold_in(own, 2), (rows, 1), 0, top)
    return jnp.take_along_axis(grid, (jnp.arange(top)[None, :] + offset_by) % top, axis=1)


def shares(count, total, reach, slope, full):
    portions = [(1 << 20) // math.isqrt(standing ** slope) + 1 for standing in range(1, count + 1)]
    largest = reach if full else min(reach, max(-(-total // count), total * portions[0] // sum(portions)))
    least = 1 if total - largest >= count - 1 else 0
    holding, spare = [largest] + [least] * (count - 1), total - largest - least * (count - 1)
    while spare > 0:
        free = [i for i in range(1, count) if holding[i] < largest] or [i for i in range(1, count) if holding[i] < reach]
        mass, left = sum([portions[i] for i in free]), spare
        for i in free:
            addition = min(reach - holding[i], max(1, left * portions[i] // mass), spare)
            holding[i] = holding[i] + addition
            spare = spare - addition
    return np.array(holding)


def gaussian(key, extent, deviation, limit, shards=(), kind=jnp.bfloat16):
    values = deviation * jax.random.normal(key, extent, jnp.float32)
    if shards:
        values = values * shard_levels(key, extent, shards, -0.22, 0.18)
    return jnp.clip(values, -limit, limit).astype(kind)


def setup_inputs(seed: int = 0) -> dict:
    arg_keys = jax.random.split(jax.random.key(seed), 17)
    phonon_deviation = gaussian(arg_keys[0], (BANDS, NDIR, PATCH_TOTAL), 1.0, 6.0, ((0, 4), (2, 64)), jnp.float32)
    thermal_field = draw_thermal_field(jax.random.fold_in(arg_keys[16], 71), 0)
    bulk_generation = gaussian(arg_keys[2], (NODES_LEADING_AX, NODES_MIDDLE_AX, NODES_TRAILING_AX), 1.0, 6.0, ((0, 64),), jnp.float32)
    ambient_coupling = jnp.clip(0.5 + 0.5 * jax.random.uniform(arg_keys[3], (NODES_LEADING_AX, NODES_MIDDLE_AX, NODES_TRAILING_AX), jnp.float32) ** shard_levels(arg_keys[3], (NODES_LEADING_AX, NODES_MIDDLE_AX, NODES_TRAILING_AX), ((0, 64),), -0.2, 0.2), 0.5, 1.0)
    substance_label = with_ends(jax.random.randint(arg_keys[4], (NODES_LEADING_AX, NODES_MIDDLE_AX, NODES_TRAILING_AX), 0, NMAT), jax.random.fold_in(arg_keys[4], 1), 0, NMAT - 1).astype(jnp.int32)
    material_conductance_table = jnp.clip(jnp.exp(jax.random.uniform(arg_keys[5], (NMAT,), jnp.float32, math.log(2.0), math.log(4.0))), 2.0, 4.0)
    mode_specific_warmth = jnp.clip(jnp.exp(jax.random.uniform(arg_keys[6], (BANDS,), jnp.float32, math.log(0.3), math.log(3.0))), 0.3, 3.0)
    mode_lifetime = jnp.clip(jnp.exp(jax.random.uniform(arg_keys[7], (BANDS,), jnp.float32, math.log(0.2), math.log(5.0))), 0.2, 5.0)
    mode_velocity_ratio = jnp.clip(jnp.exp(jax.random.uniform(arg_keys[8], (BANDS,), jnp.float32, math.log(0.5), math.log(5.0))), 0.5, 5.0)
    angular_cosine_factor = jnp.clip(jax.random.uniform(arg_keys[9], (6, NDIR), jnp.float32, -0.05, 0.05), -0.05, 0.05)
    region_mesh_node = with_ends(jax.random.randint(arg_keys[10], (PATCH_TOTAL,), 0, NODES_EACH_BLOCK), jax.random.fold_in(arg_keys[10], 1), 0, NODES_EACH_BLOCK - 1).astype(jnp.int32)
    upstream_neighbour = draw_upstream_neighbour(jax.random.fold_in(arg_keys[16], 71), 0)
    interior_local_node = with_ends(jax.random.randint(arg_keys[12], (FACE_TOTAL,), 0, PATCH), jax.random.fold_in(arg_keys[12], 1), 0, PATCH - 1).astype(jnp.int32)
    boundary_orientation = with_ends(jax.random.randint(arg_keys[13], (FACE_TOTAL,), 0, 6), jax.random.fold_in(arg_keys[13], 1), 0, 5).astype(jnp.int32)
    neighbour_partition_keys = jax.random.split(jax.random.fold_in(arg_keys[14], 1), FACE_TOTAL // NFACE)
    neighbour_partition_turns = jax.random.permutation(jax.random.fold_in(arg_keys[14], 3), FACE_TOTAL // NFACE)
    neighbour_partition = jax.vmap(lambda own, number: deal_out(jax.random.fold_in(arg_keys[14], 2), own, number, NFACE, N_SPACE, 1, CAP, 2))(neighbour_partition_keys, neighbour_partition_turns).reshape((FACE_TOTAL, 1))
    exterior_local_node = with_ends(jax.random.randint(arg_keys[15], (FACE_TOTAL,), 0, NODES_EACH_BLOCK), jax.random.fold_in(arg_keys[15], 1), 0, NODES_EACH_BLOCK - 1).astype(jnp.int32)
    return dict(phonon_deviation=phonon_deviation, thermal_field=thermal_field, bulk_generation=bulk_generation, ambient_coupling=ambient_coupling, substance_label=substance_label, material_conductance_table=material_conductance_table, mode_specific_warmth=mode_specific_warmth, mode_lifetime=mode_lifetime, mode_velocity_ratio=mode_velocity_ratio, angular_cosine_factor=angular_cosine_factor, region_mesh_node=region_mesh_node, upstream_neighbour=upstream_neighbour, interior_local_node=interior_local_node, boundary_orientation=boundary_orientation, neighbour_partition=neighbour_partition, exterior_local_node=exterior_local_node)


lowest = 0.5
highest = 50.0


def chebyshev_table(count):
    centre = (highest + lowest) / 2.0
    spread = (highest - lowest) / 2.0
    ratio = centre / spread
    rho_prev = 1.0 / ratio
    table = [(0.0, 1.0 / centre)]
    for number in range(1, count):
        rho_next = 1.0 / (2.0 * ratio - rho_prev)
        table.append((rho_next * rho_prev, 2.0 * rho_next / spread))
        rho_prev = rho_next
    return table


def conductance(substance_label, material_conductance_table):
    result = jnp.zeros(substance_label.shape, jnp.float32)
    for mat_no in range(material_conductance_table.shape[0]):
        result = result + jnp.where(substance_label == mat_no, material_conductance_table[mat_no], jnp.float32(0.0))
    return result


def operate(padded, kpadded, sink_here):
    centre = padded[1:-1, 1:-1, 1:-1]
    kcentre = kpadded[1:-1, 1:-1, 1:-1]
    pairs = [
        (padded[2:, 1:-1, 1:-1], kpadded[2:, 1:-1, 1:-1]),
        (padded[:-2, 1:-1, 1:-1], kpadded[:-2, 1:-1, 1:-1]),
        (padded[1:-1, 2:, 1:-1], kpadded[1:-1, 2:, 1:-1]),
        (padded[1:-1, :-2, 1:-1], kpadded[1:-1, :-2, 1:-1]),
        (padded[1:-1, 1:-1, 2:], kpadded[1:-1, 1:-1, 2:]),
        (padded[1:-1, 1:-1, :-2], kpadded[1:-1, 1:-1, :-2]),
    ]
    total = sink_here * centre
    for values, kvalues in pairs:
        total = total + 0.5 * (kcentre + kvalues) * (centre - values)
    return total


def relaxed(thermal_storage, rate, speeds, moment, upstream):
    return (thermal_storage * moment / rate + speeds * upstream) / (speeds + 1.0 / rate)


def face_table(angular_cosine_factor, boundary_orientation):
    table = jnp.zeros((angular_cosine_factor.shape[1], boundary_orientation.shape[0]), jnp.float32)
    for side_no in range(6):
        table = table + jnp.where(boundary_orientation[None, :] == side_no, angular_cosine_factor[side_no][:, None], jnp.float32(0.0))
    return table


def reference(phonon_deviation, thermal_field, bulk_generation, ambient_coupling, substance_label, material_conductance_table, mode_specific_warmth, mode_lifetime, mode_velocity_ratio, angular_cosine_factor, region_mesh_node, upstream_neighbour, interior_local_node, boundary_orientation, neighbour_partition, exterior_local_node):
    partition_table = (jnp.arange(PATCH_TOTAL) // PATCH).astype(jnp.int32)
    region_thermal_field = thermal_field.reshape(-1)[partition_table * NODES_EACH_BLOCK + region_mesh_node]
    thermal_storage = mode_specific_warmth[:, None, None]
    rate = mode_lifetime[:, None, None]
    speeds = mode_velocity_ratio[:, None, None]
    capacity_sum = jnp.sum(mode_specific_warmth / mode_lifetime)
    per_block = NDIR // DBLK
    energy = phonon_deviation
    for sweep_no in range(SWEEPS):
        moment = jnp.sum(jnp.mean(energy, axis=1) / mode_lifetime[:, None], axis=0) / capacity_sum
        fragments = []
        for partition_number in range(DBLK):
            emission_term = upstream_neighbour[partition_number]
            columns = partition_table * PATCH + jnp.maximum(emission_term, 0)
            collected_values = energy[:, partition_number * per_block:(partition_number + 1) * per_block][:, :, columns]
            fragments.append(jnp.where(emission_term < 0, thermal_storage * region_thermal_field, collected_values))
        energy = relaxed(thermal_storage, rate, speeds, moment, jnp.concatenate(fragments, axis=1))
    face_cols = (jnp.arange(FACE_TOTAL) // NFACE).astype(jnp.int32) * PATCH + interior_local_node
    summed = jnp.sum(energy[:, :, face_cols], axis=0)
    flux = jnp.sum(face_table(angular_cosine_factor, boundary_orientation) * summed, axis=0)
    targets = neighbour_partition.reshape(-1) * NODES_EACH_BLOCK + exterior_local_node
    accumulate_absorbed = jnp.zeros((NODES_LEADING_AX * NODES_MIDDLE_AX * NODES_TRAILING_AX,), jnp.float32).at[targets].add(flux).reshape(NODES_LEADING_AX, NODES_MIDDLE_AX, NODES_TRAILING_AX)
    linear_forcing = bulk_generation + accumulate_absorbed
    kpadded = jnp.pad(conductance(substance_label, material_conductance_table), 1)
    iterative_status = thermal_field
    angular_advance = jnp.zeros(thermal_field.shape, jnp.float32)
    for first, second in chebyshev_table(ITERS):
        resid = linear_forcing - operate(jnp.pad(iterative_status, 1), kpadded, ambient_coupling)
        angular_advance = first * angular_advance + second * resid
        iterative_status = iterative_status + angular_advance
    return (iterative_status, energy)
```

```python
import jax
import jax.numpy as jnp
from jax import lax
from jax.experimental import pallas as pl
from jax.experimental.pallas import tpu as pltpu
from jax.sharding import PartitionSpec as P

ITERS = 20
BOTH = ("space", "band")
F32 = jnp.float32
BF16 = jnp.bfloat16
VMEM_BYTES = 24 * 1024 * 1024
VMEM_MOST = 56 * 1024 * 1024

DMAX = 12
LATER = ITERS - DMAX
OWN = 4
EXT = OWN + 2 * DMAX
BODY = 8
OWNERS = EXT // 2
TILES = 7
WIN = 8 * TILES

lowest = 0.5
highest = 50.0


def chebyshev_table(count):
    centre = (highest + lowest) / 2.0
    spread = (highest - lowest) / 2.0
    ratio = centre / spread
    rho_prev = 1.0 / ratio
    table = [(0.0, 1.0 / centre)]
    for number in range(1, count):
        rho_next = 1.0 / (2.0 * ratio - rho_prev)
        table.append((rho_next * rho_prev, 2.0 * rho_next / spread))
        rho_prev = rho_next
    return table


PATH = (
    (0, 0), (1, 0), (1, 1), (0, 1), (0, 2), (1, 2), (1, 3), (2, 3),
    (2, 0), (3, 0), (3, 1), (2, 1), (2, 2), (3, 2), (3, 3), (0, 3),
)


def spot_of(m):
    x, y = PATH[m // 2]
    return (y * 4 + x) * 2 + m % 2


def flat(z, spot):
    return ((z // 4) * 32 + spot) * 4 + z % 4


def along(move):
    return [
        (flat(z, spot_of(m)), flat(z, spot_of(move(m))))
        for z in range(8)
        for m in range(32)
        if 0 <= move(m) < 32
    ]


NEXT = along(lambda m: m + 1 if m % 2 else m - 1)
SECOND = along(lambda m: m - 2 if m % 2 else m + 2)
THIRD = along(lambda m: m + 3 if m % 2 else m - 3)
SIBLING = along(lambda m: m ^ 1)


def deal_perm(which):
    pairs = []
    for z in range(8):
        for tile in range((z // 4) * 32, (z // 4) * 32 + 32):
            stays = (tile % 2) == which
            target = z if stays else 7 - z
            pairs.append((flat(z, tile % 32), flat(target, spot_of(tile // 2))))
    return pairs


def call(body, outs, *, ins, scratch=(), flops=0, moved=0, space=pltpu.VMEM, grant=VMEM_BYTES):
    return pl.pallas_call(
        body,
        out_shape=outs,
        in_specs=ins,
        out_specs=jax.tree.map(lambda _: pl.BlockSpec(memory_space=space), outs),
        scratch_shapes=list(scratch),
        compiler_params=pltpu.CompilerParams(vmem_limit_bytes=grant),
        cost_estimate=pl.CostEstimate(flops=flops, bytes_accessed=moved, transcendentals=0),
    )


IN_VMEM = pl.BlockSpec(memory_space=pltpu.VMEM)
IN_SMEM = pl.BlockSpec(memory_space=pltpu.SMEM)
ANYWHERE = pl.BlockSpec(memory_space=pl.ANY)


def sds(*shape):
    return jax.ShapeDtypeStruct(shape, F32)


def halves(values):
    high = values.astype(BF16)
    low = (values - high.astype(F32)).astype(BF16)
    return high, low


def dot(a, b):
    return jnp.dot(a, b, preferred_element_type=F32)


def dot_nt(a, b):
    return lax.dot_general(a, b, (((1,), (1,)), ((), ())), preferred_element_type=F32)


def iota(shape, axis):
    return lax.broadcasted_iota(jnp.int32, shape, axis)


def fetch(sources, targets, sems):
    copies = [pltpu.make_async_copy(a, b, sems.at[n]) for n, (a, b) in enumerate(zip(sources, targets))]
    for copy in copies:
        copy.start()
    return copies


def full(value, width=128):
    return jnp.full((1, width), value, F32)


def wide(row):
    return jnp.concatenate([row] * 4, axis=1)


def transport_body(
    where, warmth, lifetime, velocity, *refs
):
    sources, outs, (vscr, cscr, *targets), sems = refs[:9], refs[9:14], refs[14:25], refs[25]
    phonon, field, node, upwind, behind, side, owners, beyond, cosines = targets
    again_out, sums_out, cells_out, inflow_out, rates_out = outs
    copies = fetch(sources, targets, sems)
    nb, nd, _ = phonon.shape
    first_band = where[3]

    capacity, sum_alpha, sum_ab, carry = full(0.0), full(0.0), full(0.0), full(0.0)
    for b in range(warmth.shape[0]):
        storage, speed, weight = full(warmth[b]), full(velocity[b]), 1.0 / full(lifetime[b])
        scale = 1.0 / (speed + weight)
        alpha, beta = storage * weight * scale, speed * scale
        capacity = capacity + storage * weight
        sum_alpha = sum_alpha + alpha
        sum_ab = sum_ab + alpha * beta
        carry = carry + alpha * weight
    unit = 1.0 / (nd * capacity)
    carry, sum_alpha, sum_ab = wide(carry / capacity), wide(sum_alpha), wide(sum_ab)
    alphas, betas, stores, means = [], [], [], []
    for b in range(nb):
        storage = full(warmth[first_band + b])
        speed, weight = full(velocity[first_band + b]), 1.0 / full(lifetime[first_band + b])
        scale = 1.0 / (speed + weight)
        alphas.append(wide(storage * weight * scale))
        betas.append(wide(speed * scale))
        stores.append(wide(storage))
        means.append(wide(weight * unit))
        rates_out[b : b + 1, :] = alphas[b]
        rates_out[nb + b : nb + b + 1, :] = betas[b]
        rates_out[2 * nb + b : 2 * nb + b + 1, :] = stores[b]

    for copy in copies[1:]:
        copy.wait()
    cell = node[...]
    rows_hot = jnp.where(iota((256, 512), 0) == (cell >> 7), 1.0, 0.0).astype(BF16)
    turned = field[...].T
    high, low = halves(turned)
    picked = dot(high, rows_hot) + dot(low, rows_hot)
    patch = jnp.sum(jnp.where(iota((128, 512), 0) == (cell & 127), picked, 0.0), axis=0, keepdims=True)

    copies[0].wait()
    m0 = jnp.zeros((1, 512), F32)
    for b in range(nb):
        m0 = m0 + means[b] * jnp.sum(phonon[b], axis=0, keepdims=True)
    m0h, m0l = halves(m0)
    m0_rows = jnp.where(
        iota((16, 512), 0) == 0, m0h.astype(F32), jnp.where(iota((16, 512), 0) == 1, m0l.astype(F32), 0.0)
    ).astype(BF16)

    first_half = iota((24, 512), 0) < 12
    mid_first = iota((1, 8, 512), 1) < 4
    share = jnp.zeros((1, 512), F32)
    for pair in range(4):
        hots, blanks = [], []
        for odd in range(2):
            source = upwind[2 * pair + odd : 2 * pair + odd + 1, :]
            hots.append(jnp.where(iota((512, 512), 0) == source, 1.0, 0.0).astype(BF16))
            blanks.append(jnp.where(source < 0, patch, 0.0))
        inflow = jnp.where(first_half, blanks[0], blanks[1])
        inflow_out[pair * 24 : pair * 24 + 24, :] = inflow

        def gather(values, extra):
            parts = []
            moms = []
            for odd in range(2):
                chunk = values[:, 8 * odd : 8 * odd + 16, :].reshape(nb * 16, 512)
                h, l = halves(chunk)
                pieces = [h, l] + ([m0_rows] if extra else [])
                got = dot(jnp.concatenate(pieces, axis=0), hots[odd])
                parts.append((got[: nb * 16] + got[nb * 16 : nb * 32]).reshape(nb, 16, 512))
                if extra:
                    moms.append(got[nb * 32 : nb * 32 + 1] + got[nb * 32 + 1 : nb * 32 + 2])
            a, b = parts
            middle = jnp.where(mid_first, a[:, 8:16], b[:, 0:8])
            return jnp.concatenate([a[:, 0:8], middle, b[:, 8:16]], axis=1), moms

        first, moms = gather(phonon[:, pair * 24 : pair * 24 + 24, :], True)
        for odd in range(2):
            sums_out[2 * pair + odd : 2 * pair + odd + 1, :] = moms[odd]
        ups = []
        for b in range(nb):
            up = first[b] + stores[b] * inflow
            share = share + (means[b] * betas[b]) * jnp.sum(up, axis=0, keepdims=True)
            ups.append(up[None])
        second, _ = gather(jnp.concatenate(ups, axis=0), False)
        again_out[:, pair * 24 : pair * 24 + 24, :] = second
        total = jnp.zeros((24, 512), F32)
        for b in range(nb):
            total = total + (betas[b] * betas[b]) * second[b] + (betas[b] * stores[b]) * inflow
        vscr[pair * 24 : pair * 24 + 24, :] = total + sum_ab * jnp.where(first_half, moms[0], moms[1])

    m1 = carry * m0 + share
    sums_out[8:16, :] = jnp.zeros((8, 512), F32)
    sums_out[8:9, :] = m1
    field_sum = vscr[...] + sum_alpha * m1
    cscr[...] = jnp.zeros((8, 128), F32)
    cscr[0:6, 0:96] = cosines[...]
    by_side = jnp.dot(
        cscr[:, 0:96], field_sum, precision=lax.Precision.HIGHEST, preferred_element_type=F32
    )

    hot = jnp.where(iota((512, 256), 0) == behind[...], 1.0, 0.0).astype(BF16)
    h, l = halves(by_side)
    at_face = dot(jnp.concatenate([h.astype(F32), l.astype(F32)], axis=0).astype(BF16), hot)
    at_face = at_face[0:8] + at_face[8:16]
    flux = jnp.sum(jnp.where(iota((8, 256), 0) == side[...], at_face, 0.0), axis=0, keepdims=True)
    owner_row = owners[...]
    column = jnp.broadcast_to(owner_row.astype(F32), (128, 256)).T
    column = jnp.concatenate([column, column], axis=1)
    same = (column == owner_row.astype(F32)) & (iota((256, 256), 0) < iota((256, 256), 1))
    place = jnp.sum(jnp.where(same, 1.0, 0.0), axis=0, keepdims=True).astype(jnp.int32)
    slot = owner_row * 8 + place
    slots = jnp.where(iota((512, 256), 0) == slot, 1.0, 0.0).astype(BF16)
    h, l = halves(flux)
    line = iota((16, 256), 0)
    target = beyond[...]
    rows = jnp.where(line == 0, h.astype(F32), 0.0)
    rows = jnp.where(line == 1, l.astype(F32), rows)
    rows = jnp.where(line == 2, (target >> 7).astype(F32), rows)
    rows = jnp.where(line == 3, (target & 127).astype(F32), rows)
    packed = dot_nt(rows.astype(BF16), slots)
    sums_out[9:10, :] = packed[0:1] + packed[1:2]
    cells_out[...] = packed[2:3] * 128.0 + packed[3:4]


def deal_body(*refs):
    shares, cells, out, scr, held, held_cells, sems = refs[:4], *refs[4:]
    sources = [share.at[pl.ds(8, 8)] for share in shares] + [cells]
    targets = [held.at[n] for n in range(4)] + [held_cells]
    copies = fetch(sources, targets, sems)
    scr[...] = jnp.zeros(scr.shape, F32)
    for copy in copies:
        copy.wait()
    scr[0:1, 128:640] = (held[0, 1:2] + held[1, 1:2]) + (held[2, 1:2] + held[3, 1:2])
    scr[1:2, 128:640] = held_cells[...]
    lead = 128 - 8 * (DMAX // 2)
    for q, (x, y) in enumerate(PATH):
        at = lead + 32 * q
        base = at // 128 * 128
        rolled = pltpu.roll(scr[:, base : base + 256], (256 - (at - base)) % 256, 1)[0:2, 0:128]
        out[4 * y + x] = rolled
        out[16 + 4 * y + x] = rolled


def finish_body(rates, again, sums_a, sums_b, sums_c, sums_d, inflow, energy_out):
    nb = again.shape[0]
    first_half = iota((24, 512), 0) < 12
    sums = (sums_a[...] + sums_b[...]) + (sums_c[...] + sums_d[...])
    m1 = sums[8:9, :]
    for pair in range(4):
        span = slice(pair * 24, pair * 24 + 24)
        mom = jnp.where(first_half, sums[2 * pair : 2 * pair + 1, :], sums[2 * pair + 1 : 2 * pair + 2, :])
        blank = inflow[span, :]
        for b in range(nb):
            alpha = rates[b : b + 1, :]
            beta = rates[nb + b : nb + b + 1, :]
            storage = rates[2 * nb + b : 2 * nb + b + 1, :]
            upstream = beta * again[b, span, :] + alpha * mom + storage * blank
            energy_out[b, span, :] = alpha * m1 + beta * upstream


def pack_body(where, table, *refs):
    (first_out, second_out), (thermal, label, sink, bulk), sems = refs[4:6], refs[6:10], refs[10]
    for copy in fetch(refs[:4], refs[6:10], sems):
        copy.wait()
    for number, out in ((6, first_out), (7, second_out)):
        start = where[number]
        for row in range(2):
            for t in range(TILES):
                at = pl.ds(start + t, 8, stride=TILES)
                out[0, row, t] = thermal[row, at, :]
                kinds = label[row, at, :]
                k = jnp.zeros((8, 128), F32)
                for mat in range(8):
                    k = jnp.where(kinds == mat, table[mat], k)
                out[1, row, t] = k
                out[2, row, t] = sink[row, at, :]
                out[3, row, t] = bulk[row, at, :]


def join_body(where, first, second, block_out, sems):
    swap = where[4]
    copies = [
        pltpu.make_async_copy(piece, block_out.at[:, pl.ds(2 * at, 2)], sems.at[number])
        for number, (piece, at) in enumerate(((first, swap), (second, 1 - swap)))
    ]
    for copy in copies:
        copy.start()
    for copy in copies:
        copy.wait()


def next_sublane(v):
    return pltpu.roll(v, 7, 0)


def last_sublane(v):
    return pltpu.roll(v, 1, 0)


def lane_ahead(v):
    return pltpu.roll(v, 127, 1)


def lane_behind(v):
    return pltpu.roll(v, 1, 1)


def assemble(core, lefts, own, rights, others, numbers, outs):
    for this, (before, after) in ((0, (lefts, others)), (1, (others, rights))):

        @pl.when(core == this)
        def _(before=before, after=after):
            for number, out in zip(numbers, outs):
                out[DMAX : DMAX + OWN] = own[number]
                for n, piece in enumerate(before):
                    at = DMAX - OWN * (n + 1)
                    out[at : at + OWN] = piece[number]
                for n, piece in enumerate(after):
                    at = DMAX + OWN * (n + 1)
                    out[at : at + OWN] = piece[number]


def faces_body(where, arrived, other, out, amounts, targets):
    start, core = where[1], where[5]
    for number, scr in ((0, amounts), (1, targets)):
        scr[:, 0:32] = arrived[:, number, :].T
        scr[:, 32:64] = other[:, number, :].T
    for o in range(OWNERS):
        at = pl.ds(pl.multiple_of(8 * o + 16 * core, 8), 8)
        slots = amounts[at, 0:64]
        amount = jnp.concatenate([slots[q : q + 1] for q in range(8)], axis=1)
        slots = targets[at, 0:64]
        target = jnp.concatenate([slots[q : q + 1] for q in range(8)], axis=1).astype(jnp.int32)
        y = ((target >> 7) & 127) - start
        inside = (y >= 0) & (y < WIN)
        s = (y * 37) >> 8
        place = jnp.where(inside, (target >> 14) * WIN + (y - TILES * s) * 8 + s, -1)
        hit = iota((2 * WIN, 512), 0) == place
        high = amount.astype(BF16).astype(F32)
        low = amount - high
        left = jnp.concatenate([jnp.where(hit, high, 0.0), jnp.where(hit, low, 0.0)], axis=0).astype(BF16)
        lanes = jnp.where(iota((128, 512), 0) == (target & 127), 1.0, 0.0).astype(BF16)
        got = dot_nt(left, lanes)
        out[2 * o : 2 * o + 2] = (got[: 2 * WIN] + got[2 * WIN :]).reshape(2, TILES, 8, 128)


def coefficients(where, k_in, faces, wx, wy, wz, wb, diag, rhs):
    first_row, start = where[0], where[1]
    shape = (8, 128)
    lane = iota(shape, 1)
    z_edge = jnp.where((lane == 0) | (lane == 127), 0.5, 0.0)
    z_half = jnp.where(lane == 127, 0.0, 0.5)
    b_half = jnp.where(lane == 0, 0.0, 0.5)
    last_half = jnp.where(iota(shape, 0) == 7, 0.0, 0.5)

    def link(row):
        return jnp.where((row >= 0) & (row < 127), 0.5, 0.0).astype(F32)

    def one(i):
        row = first_row + i
        after, before = link(row), link(row - 1)
        at_end = jnp.where((row == 0) | (row == 127), 0.5, 0.0).astype(F32)
        up, down = jnp.minimum(i + 1, EXT - 1), jnp.maximum(i - 1, 0)
        ks = [k_in[i, t] for t in range(TILES)]
        ys = [0.5 * (ks[t] + ks[t + 1]) for t in range(TILES - 1)]
        ys.append(last_half * (ks[TILES - 1] + next_sublane(ks[0])))
        for t in range(TILES):
            k = ks[t]
            column = TILES * iota(shape, 0) + (start + t)
            edge = z_edge + at_end + jnp.where((column == 0) | (column == 127), 0.5, 0.0)
            x_after = after * (k + k_in[up, t])
            x_before = before * (k + k_in[down, t])
            z_after = z_half * (k + lane_ahead(k))
            z_before = b_half * (k + lane_behind(k))
            y_before = ys[t - 1] if t else last_sublane(ys[TILES - 1])
            wx[i, t] = x_after
            wy[i, t] = ys[t]
            wz[i, t] = z_after
            wb[i, t] = z_before
            links = (x_after + x_before) + (ys[t] + y_before) + (z_after + z_before)
            diag[i, t] = (diag[i, t] + edge * k) + links
            rhs[i, t] = rhs[i, t] + faces[i, t]

    def four(n, _):
        for q in range(4):
            one(4 * n + q)
        return 0

    lax.fori_loop(0, EXT // 4, four, 0)


def steps(depth, rates, first, x_even, x_odd, d, wx, wy, wz, wb, diag, rhs):
    shift = DMAX - depth

    def rows(i, count, c1, c2, old, new):
        columns = [[old[i - 1 + q, t] for q in range(count + 2)] for t in (TILES - 1, 0)]
        before = [last_sublane(columns[0][q + 1]) for q in range(count)]
        after_end = [next_sublane(columns[1][q + 1]) for q in range(count)]
        y_before = [last_sublane(wy[i + q, TILES - 1]) for q in range(count)]
        here = columns[1]
        for t in range(TILES):
            ahead = [old[i - 1 + q, t + 1] for q in range(count + 2)] if t < TILES - 1 else None
            x_before = wx[i - 1, t]
            for q in range(count):
                v = here[q + 1]
                y_here, x_here = wy[i + q, t], wx[i + q, t]
                total = rhs[i + q, t] - diag[i + q, t] * v
                total = total + (x_here * here[q + 2] + x_before * here[q])
                total = total + (y_here * (ahead[q + 1] if ahead else after_end[q]) + y_before[q] * before[q])
                total = total + (wz[i + q, t] * lane_ahead(v) + wb[i + q, t] * lane_behind(v))
                step = c2 * total + c1 * d[i + q, t]
                d[i + q, t] = step
                new[i + q, t] = v + step
                before[q], y_before[q], x_before = v, y_here, x_here
            here = ahead

    def one(k, old, new):
        c1, c2 = rates[first + k, 0], rates[first + k, 1]
        low = shift + k + 1
        count = OWN + 2 * (depth - 1 - k)

        def several(n, _):
            rows(low + BODY * n, BODY, c1, c2, old, new)
            return 0

        bodies = count // BODY
        lax.fori_loop(0, bodies, several, 0)
        for tail in (2, 4, 6):

            @pl.when(count % BODY == tail)
            def _(tail=tail):
                rows(low + BODY * bodies, tail, c1, c2, old, new)

    def both(n, _):
        one(2 * n, x_even, x_odd)
        one(2 * n + 1, x_odd, x_even)
        return 0

    lax.fori_loop(0, depth // 2, both, 0)


def first_round_body(where, rates, *refs):
    own, near, far, third, other_own, other_near, other_far, faces = refs[:8]
    out, wx, wy, wz, wb, diag, rhs, xa, xb, d = refs[8:]
    mine = (near, far, third)
    assemble(
        where[5], mine, own, mine, (other_own, other_near, other_far), (0, 1, 2, 3), (xa, xb, diag, rhs)
    )
    coefficients(where, xb, faces, wx, wy, wz, wb, diag, rhs)
    d[...] = jnp.zeros(d.shape, F32)
    steps(DMAX, rates, 0, xa, xb, d, wx, wy, wz, wb, diag, rhs)
    for number, ref in ((0, xa), (1, d)):
        out[number] = ref[DMAX : DMAX + OWN]


def last_round_body(where, rates, wx, wy, wz, wb, diag, rhs, own, near, far, other_own, other_near, *rest):
    *outs, xa, xb, d = rest
    assemble(where[5], (near, far), own, (near, far), (other_own, other_near), (0, 1), (xa, d))
    steps(LATER, rates, DMAX, xa, xb, d, wx, wy, wz, wb, diag, rhs)
    offset, swap = where[2], where[4]
    for number, out in enumerate(outs):
        for j in range(16):
            y = offset + j
            s = (y * 37) >> 8
            t = y - TILES * s
            for row in range(2):
                source = DMAX + 2 * ((swap + number) % 2) + row
                out[row, j : j + 1, :] = xa[source, t, pl.ds(s, 1), :]


def place_body(where, *refs):
    out = refs[4]
    band, flip, half = where[8], where[9], where[10]
    for n in range(4):
        source = (band + (4 - n)) % 4
        for number in range(2):
            side = (number + flip) % 2
            block = 4 * side + jnp.where(side == half, source, 3 - source)
            out[:, pl.ds(pl.multiple_of(16 * block, 16), 16), :] = refs[n][number]


def on_device(
    phonon_deviation,
    thermal_field,
    bulk_generation,
    ambient_coupling,
    substance_label,
    material_conductance_table,
    mode_specific_warmth,
    mode_lifetime,
    mode_velocity_ratio,
    angular_cosine_factor,
    region_mesh_node,
    upstream_neighbour,
    interior_local_node,
    boundary_orientation,
    neighbour_partition,
    exterior_local_node,
):
    nb, nd, cells = phonon_deviation.shape
    tile = lax.axis_index("space")
    band = lax.axis_index("band")
    half = tile // 32
    plane = half * 4 + band
    other = 7 - plane
    chip = (tile % 32) // 2
    order = jnp.int32(0)
    for q, (x, y) in enumerate(PATH):
        order = jnp.where(chip == 4 * y + x, q, order)
    place = 2 * order + tile % 2
    away = jnp.where((place // 16) == half, 0, 1)
    stays = tile % 2 == 0

    def start_of(z):
        return jnp.clip(16 * z - 20, 0, 128 - WIN)

    start = start_of(plane)
    flip = jnp.where(stays == (half == 0), 0, 1)
    where = jnp.stack(
        [
            4 * place - DMAX,
            start,
            16 * plane - start,
            band * nb,
            away,
            tile % 2,
            jnp.where(stays, start, start_of(other)),
            jnp.where(stays, start_of(other), start),
            band,
            flip,
            half,
        ]
    ).astype(jnp.int32)
    ext = sds(EXT, TILES, 8, 128)

    pack_shape = sds(4, 2, TILES, 8, 128)
    fields = (thermal_field, substance_label, ambient_coupling, bulk_generation)
    first, second = call(
        pack_body,
        [pack_shape, pack_shape],
        ins=[IN_SMEM, IN_SMEM] + [ANYWHERE] * 4,
        scratch=[pltpu.VMEM(x.shape, x.dtype) for x in fields] + [pltpu.SemaphoreType.DMA((4,))],
        moved=3 << 20,
        grant=VMEM_MOST,
    )(where, material_conductance_table, *fields)
    first, second, where = lax.optimization_barrier((first, second, where))
    got_first = lax.ppermute(first, BOTH, deal_perm(0))
    got_second = lax.ppermute(second, BOTH, deal_perm(1))

    held = (
        phonon_deviation,
        thermal_field.reshape(256, 128),
        region_mesh_node.reshape(1, -1),
        upstream_neighbour,
        interior_local_node.reshape(1, -1),
        boundary_orientation.reshape(1, -1),
        neighbour_partition.reshape(1, -1),
        exterior_local_node.reshape(1, -1),
        angular_cosine_factor,
    )
    again, sums, targets, inflow, rates = call(
        transport_body,
        [sds(nb, nd, cells), sds(16, cells), sds(1, cells), sds(nd, cells), sds(3 * nb, cells)],
        ins=[IN_SMEM] * 4 + [ANYWHERE] * 9,
        scratch=[pltpu.VMEM((nd, cells), F32), pltpu.VMEM((8, 128), F32)]
        + [pltpu.VMEM(x.shape, x.dtype) for x in held]
        + [pltpu.SemaphoreType.DMA((9,))],
        flops=2 * 1600 * 512 * 512 * 4,
        moved=4 << 20,
        grant=VMEM_MOST,
    )(where, mode_specific_warmth, mode_lifetime, mode_velocity_ratio, *held)
    shares = [sums] + [
        lax.ppermute(sums, "band", [(i, (i + turn) % 4) for i in range(4)]) for turn in (1, 2, 3)
    ]

    packets = call(
        deal_body,
        sds(32, 2, 128),
        ins=[ANYWHERE] * 5,
        scratch=[
            pltpu.VMEM((8, 768), F32),
            pltpu.VMEM((4, 8, cells), F32),
            pltpu.VMEM((1, cells), F32),
            pltpu.SemaphoreType.DMA((5,)),
        ],
        moved=1 << 18,
        grant=VMEM_MOST,
    )(*shares, targets)

    packets, got_first, got_second = lax.optimization_barrier((packets, got_first, got_second))
    block = call(
        join_body,
        sds(4, OWN, TILES, 8, 128),
        ins=[IN_SMEM, ANYWHERE, ANYWHERE],
        scratch=[pltpu.SemaphoreType.DMA((2,))],
        moved=2 << 20,
        space=pl.ANY,
    )(where, got_first, got_second)
    packets, block = lax.optimization_barrier((packets, block))
    near = lax.ppermute(block, BOTH, NEXT)
    far = lax.ppermute(block, BOTH, SECOND)
    third = lax.ppermute(block, BOTH, THIRD)
    other_own = lax.ppermute(block, BOTH, SIBLING)
    arrived = lax.all_to_all(
        packets, "space", split_axis=0, concat_axis=0, tiled=True,
        axis_index_groups=[list(range(0, 64, 2)), list(range(1, 64, 2))],
    )
    near, far, third, other_own, arrived = lax.optimization_barrier((near, far, third, other_own, arrived))
    other_near = lax.ppermute(near, BOTH, SIBLING)
    other_far = lax.ppermute(far, BOTH, SIBLING)
    faces = call(
        faces_body,
        ext,
        ins=[IN_SMEM, IN_VMEM, IN_VMEM],
        scratch=[pltpu.VMEM((128, 128), F32)] * 2,
        flops=1 << 30,
        moved=1 << 20,
    )(where, arrived, lax.ppermute(arrived, BOTH, SIBLING))

    factors = jnp.array(chebyshev_table(ITERS), F32)
    work = 25 * DMAX * (OWN + DMAX) * 8192
    scratch = [pltpu.VMEM((EXT, TILES, 8, 128), F32)] * 3
    state, *operator = call(
        first_round_body,
        [sds(2, OWN, TILES, 8, 128)] + [ext] * 6,
        ins=[IN_SMEM] * 2 + [IN_VMEM] * 8,
        scratch=scratch,
        flops=work,
        moved=8 << 20,
    )(where, factors, block, near, far, third, other_own, other_near, other_far, faces)
    near = lax.ppermute(state, BOTH, NEXT)
    far = lax.ppermute(state, BOTH, SECOND)
    other_own = lax.ppermute(state, BOTH, SIBLING)
    energy = call(
        finish_body,
        sds(nb, nd, cells),
        ins=[IN_VMEM] * 7,
        flops=8 * nb * nd * cells,
        moved=3 << 20,
    )(rates, again, *shares, inflow)
    near, far, other_own, energy = lax.optimization_barrier((near, far, other_own, energy))
    other_near = lax.ppermute(near, BOTH, SIBLING)
    state = call(
        last_round_body,
        [sds(2, 16, 128)] * 2,
        ins=[IN_SMEM] * 2 + [IN_VMEM] * 11,
        scratch=scratch,
        flops=work,
        moved=8 << 20,
    )(where, factors, *operator, state, near, far, other_own, other_near)

    back = [[(b, a) for a, b in deal_perm(which)] for which in (0, 1)]
    blocks = jnp.stack([lax.ppermute(state[which], BOTH, back[which]) for which in (0, 1)])
    pieces = [blocks] + [
        lax.ppermute(blocks, "band", [(i, (i + turn) % 4) for i in range(4)]) for turn in (1, 2, 3)
    ]
    temperature = call(place_body, sds(2, 128, 128), ins=[IN_SMEM] + [IN_VMEM] * 4, moved=1 << 18)(
        where, *pieces
    )
    return temperature, energy


def solution(mesh):
    return jax.shard_map(
        on_device,
        mesh=mesh,
        in_specs=(
            P("band", None, "space"),
            P("space", None, None),
            P("space", None, None),
            P("space", None, None),
            P("space", None, None),
            P(),
            P(),
            P(),
            P(),
            P(),
            P("space"),
            P(None, "space"),
            P("space"),
            P("space"),
            P("space", None),
            P("space"),
        ),
        out_specs=(P("space", None, None), P("band", None, "space")),
        check_vma=False,
    )
```

```python
import jax
import jax.numpy as jnp
from jax import lax
from jax.experimental import pallas as pl
from jax.experimental.pallas import tpu as pltpu
from jax.sharding import PartitionSpec as P

ITERS = 20
BOTH = ("space", "band")
F32 = jnp.float32
BF16 = jnp.bfloat16
VMEM_BYTES = 24 * 1024 * 1024
VMEM_MOST = 56 * 1024 * 1024

DMAX = 12
LATER = ITERS - DMAX
OWN = 4
EXT = OWN + 2 * DMAX
BODY = 8
OWNERS = EXT // 2
TILES = 7
WIN = 8 * TILES

lowest = 0.5
highest = 50.0


def chebyshev_table(count):
    centre = (highest + lowest) / 2.0
    spread = (highest - lowest) / 2.0
    ratio = centre / spread
    rho_prev = 1.0 / ratio
    table = [(0.0, 1.0 / centre)]
    for number in range(1, count):
        rho_next = 1.0 / (2.0 * ratio - rho_prev)
        table.append((rho_next * rho_prev, 2.0 * rho_next / spread))
        rho_prev = rho_next
    return table


PATH = (
    (3, 0), (2, 0), (2, 1), (3, 1), (3, 2), (3, 3), (2, 3), (2, 2),
    (1, 1), (1, 0), (0, 0), (0, 1), (0, 2), (1, 2), (1, 3), (0, 3),
)


def spot_of(m):
    x, y = PATH[m // 2]
    return (y * 4 + x) * 2 + m % 2


def flat(z, spot):
    return ((z // 4) * 32 + spot) * 4 + z % 4


def along(move):
    return [
        (flat(z, spot_of(m)), flat(z, spot_of(move(m))))
        for z in range(8)
        for m in range(32)
        if 0 <= move(m) < 32
    ]


NEXT = along(lambda m: m + 1 if m % 2 else m - 1)
SECOND = along(lambda m: m - 2 if m % 2 else m + 2)
THIRD = along(lambda m: m + 3 if m % 2 else m - 3)
SIBLING = along(lambda m: m ^ 1)


def chip_perm(cores):
    pairs = []
    for z in range(8):
        for chip in range(16):
            place = spot_of(chip + 16 * (z // 4))
            for core, target in zip(cores, (z, (z + 4) % 8)):
                pairs.append((flat(z, 2 * chip + core), flat(target, place)))
    return pairs


def call(body, outs, *, ins, scratch=(), flops=0, moved=0, space=pltpu.VMEM, grant=VMEM_BYTES):
    return pl.pallas_call(
        body,
        out_shape=outs,
        in_specs=ins,
        out_specs=jax.tree.map(lambda _: pl.BlockSpec(memory_space=space), outs),
        scratch_shapes=list(scratch),
        compiler_params=pltpu.CompilerParams(vmem_limit_bytes=grant),
        cost_estimate=pl.CostEstimate(flops=flops, bytes_accessed=moved, transcendentals=0),
    )


IN_VMEM = pl.BlockSpec(memory_space=pltpu.VMEM)
IN_SMEM = pl.BlockSpec(memory_space=pltpu.SMEM)
ANYWHERE = pl.BlockSpec(memory_space=pl.ANY)


def sds(*shape):
    return jax.ShapeDtypeStruct(shape, F32)


def halves(values):
    high = values.astype(BF16)
    low = (values - high.astype(F32)).astype(BF16)
    return high, low


def dot(a, b):
    return jnp.dot(a, b, preferred_element_type=F32)


def dot_nt(a, b):
    return lax.dot_general(a, b, (((1,), (1,)), ((), ())), preferred_element_type=F32)


def iota(shape, axis):
    return lax.broadcasted_iota(jnp.int32, shape, axis)


def full(value, width=128):
    return jnp.full((1, width), value, F32)


def wide(row):
    return jnp.concatenate([row] * 4, axis=1)


def transport_body(
    where, warmth, lifetime, velocity, phonon, field, node, upwind, behind, side, owners, beyond, cosines,
    again_out, sums_out, cells_out, inflow_out, rates_out, vscr, cscr,
):
    nb, nd, _ = phonon.shape
    first_band = where[3]

    capacity, sum_alpha, sum_ab, carry = full(0.0), full(0.0), full(0.0), full(0.0)
    for b in range(warmth.shape[0]):
        storage, speed, weight = full(warmth[b]), full(velocity[b]), 1.0 / full(lifetime[b])
        scale = 1.0 / (speed + weight)
        alpha, beta = storage * weight * scale, speed * scale
        capacity = capacity + storage * weight
        sum_alpha = sum_alpha + alpha
        sum_ab = sum_ab + alpha * beta
        carry = carry + alpha * weight
    unit = 1.0 / (nd * capacity)
    carry, sum_alpha, sum_ab = wide(carry / capacity), wide(sum_alpha), wide(sum_ab)
    alphas, betas, stores, means = [], [], [], []
    for b in range(nb):
        storage = full(warmth[first_band + b])
        speed, weight = full(velocity[first_band + b]), 1.0 / full(lifetime[first_band + b])
        scale = 1.0 / (speed + weight)
        alphas.append(wide(storage * weight * scale))
        betas.append(wide(speed * scale))
        stores.append(wide(storage))
        means.append(wide(weight * unit))
        rates_out[b : b + 1, :] = alphas[b]
        rates_out[nb + b : nb + b + 1, :] = betas[b]
        rates_out[2 * nb + b : 2 * nb + b + 1, :] = stores[b]

    cell = node[...]
    rows_hot = jnp.where(iota((256, 512), 0) == (cell >> 7), 1.0, 0.0).astype(BF16)
    turned = field[...].T
    high, low = halves(turned)
    picked = dot(high, rows_hot) + dot(low, rows_hot)
    patch = jnp.sum(jnp.where(iota((128, 512), 0) == (cell & 127), picked, 0.0), axis=0, keepdims=True)

    m0 = jnp.zeros((1, 512), F32)
    for b in range(nb):
        m0 = m0 + means[b] * jnp.sum(phonon[b], axis=0, keepdims=True)
    m0h, m0l = halves(m0)
    m0_rows = jnp.where(
        iota((16, 512), 0) == 0, m0h.astype(F32), jnp.where(iota((16, 512), 0) == 1, m0l.astype(F32), 0.0)
    ).astype(BF16)

    first_half = iota((24, 512), 0) < 12
    mid_first = iota((1, 8, 512), 1) < 4
    share = jnp.zeros((1, 512), F32)
    for pair in range(4):
        hots, blanks = [], []
        for odd in range(2):
            source = upwind[2 * pair + odd : 2 * pair + odd + 1, :]
            hots.append(jnp.where(iota((512, 512), 0) == source, 1.0, 0.0).astype(BF16))
            blanks.append(jnp.where(source < 0, patch, 0.0))
        inflow = jnp.where(first_half, blanks[0], blanks[1])
        inflow_out[pair * 24 : pair * 24 + 24, :] = inflow

        def gather(values, extra):
            parts = []
            moms = []
            for odd in range(2):
                chunk = values[:, 8 * odd : 8 * odd + 16, :].reshape(nb * 16, 512)
                h, l = halves(chunk)
                pieces = [h, l] + ([m0_rows] if extra else [])
                got = dot(jnp.concatenate(pieces, axis=0), hots[odd])
                parts.append((got[: nb * 16] + got[nb * 16 : nb * 32]).reshape(nb, 16, 512))
                if extra:
                    moms.append(got[nb * 32 : nb * 32 + 1] + got[nb * 32 + 1 : nb * 32 + 2])
            a, b = parts
            middle = jnp.where(mid_first, a[:, 8:16], b[:, 0:8])
            return jnp.concatenate([a[:, 0:8], middle, b[:, 8:16]], axis=1), moms

        first, moms = gather(phonon[:, pair * 24 : pair * 24 + 24, :], True)
        for odd in range(2):
            sums_out[2 * pair + odd : 2 * pair + odd + 1, :] = moms[odd]
        ups = []
        for b in range(nb):
            up = first[b] + stores[b] * inflow
            share = share + (means[b] * betas[b]) * jnp.sum(up, axis=0, keepdims=True)
            ups.append(up[None])
        second, _ = gather(jnp.concatenate(ups, axis=0), False)
        again_out[:, pair * 24 : pair * 24 + 24, :] = second
        total = jnp.zeros((24, 512), F32)
        for b in range(nb):
            total = total + (betas[b] * betas[b]) * second[b] + (betas[b] * stores[b]) * inflow
        vscr[pair * 24 : pair * 24 + 24, :] = total + sum_ab * jnp.where(first_half, moms[0], moms[1])

    m1 = carry * m0 + share
    sums_out[8:9, :] = m1
    field_sum = vscr[...] + sum_alpha * m1
    cscr[...] = jnp.zeros((8, 128), F32)
    cscr[0:6, 0:96] = cosines[...]
    by_side = jnp.dot(
        cscr[:, 0:96], field_sum, precision=lax.Precision.HIGHEST, preferred_element_type=F32
    )

    hot = jnp.where(iota((512, 256), 0) == behind[...], 1.0, 0.0).astype(BF16)
    h, l = halves(by_side)
    at_face = dot(jnp.concatenate([h.astype(F32), l.astype(F32)], axis=0).astype(BF16), hot)
    at_face = at_face[0:8] + at_face[8:16]
    flux = jnp.sum(jnp.where(iota((8, 256), 0) == side[...], at_face, 0.0), axis=0, keepdims=True)
    owner_row = owners[...]
    column = jnp.broadcast_to(owner_row.astype(F32), (128, 256)).T
    column = jnp.concatenate([column, column], axis=1)
    same = (column == owner_row.astype(F32)) & (iota((256, 256), 0) < iota((256, 256), 1))
    place = jnp.sum(jnp.where(same, 1.0, 0.0), axis=0, keepdims=True).astype(jnp.int32)
    slot = owner_row * 8 + place
    slots = jnp.where(iota((512, 256), 0) == slot, 1.0, 0.0).astype(BF16)
    h, l = halves(flux)
    line = iota((16, 256), 0)
    target = beyond[...]
    rows = jnp.where(line == 0, h.astype(F32), 0.0)
    rows = jnp.where(line == 1, l.astype(F32), rows)
    rows = jnp.where(line == 2, (target >> 7).astype(F32), rows)
    rows = jnp.where(line == 3, (target & 127).astype(F32), rows)
    packed = dot_nt(rows.astype(BF16), slots)
    sums_out[9:10, :] = packed[0:1] + packed[1:2]
    cells_out[...] = packed[2:3] * 128.0 + packed[3:4]


def deal_body(sums_a, sums_b, sums_c, sums_d, cells, out, scr):
    scr[...] = jnp.zeros(scr.shape, F32)
    scr[0:1, 128:640] = (sums_a[9:10, :] + sums_b[9:10, :]) + (sums_c[9:10, :] + sums_d[9:10, :])
    scr[1:2, 128:640] = cells[...]
    lead = 128 - 8 * (DMAX // 2)
    for q, (x, y) in enumerate(PATH):
        at = lead + 32 * q
        base = at // 128 * 128
        rolled = pltpu.roll(scr[:, base : base + 256], (256 - (at - base)) % 256, 1)[0:2, 0:128]
        for device in (2 * (4 * y + x), 2 * (4 * y + x) + 1):
            out[device] = rolled
            out[32 + device] = rolled


def finish_body(rates, again, sums_a, sums_b, sums_c, sums_d, inflow, energy_out):
    nb = again.shape[0]
    first_half = iota((24, 512), 0) < 12
    sums = (sums_a[...] + sums_b[...]) + (sums_c[...] + sums_d[...])
    m1 = sums[8:9, :]
    for pair in range(4):
        span = slice(pair * 24, pair * 24 + 24)
        mom = jnp.where(first_half, sums[2 * pair : 2 * pair + 1, :], sums[2 * pair + 1 : 2 * pair + 2, :])
        blank = inflow[span, :]
        for b in range(nb):
            alpha = rates[b : b + 1, :]
            beta = rates[nb + b : nb + b + 1, :]
            storage = rates[2 * nb + b : 2 * nb + b + 1, :]
            upstream = beta * again[b, span, :] + alpha * mom + storage * blank
            energy_out[b, span, :] = alpha * m1 + beta * upstream


def pack_body(where, table, thermal, label, sink, bulk, first_out, second_out):
    for number, out in ((6, first_out), (7, second_out)):
        start = where[number]
        for row in range(2):
            for t in range(TILES):
                at = pl.ds(start + t, 8, stride=TILES)
                out[0, row, t] = thermal[row, at, :]
                kinds = label[row, at, :]
                k = jnp.zeros((8, 128), F32)
                for mat in range(8):
                    k = jnp.where(kinds == mat, table[mat], k)
                out[1, row, t] = k
                out[2, row, t] = sink[row, at, :]
                out[3, row, t] = bulk[row, at, :]


def join_body(where, first, second, block_out, sems):
    swap = where[4]
    copies = [
        pltpu.make_async_copy(piece, block_out.at[:, pl.ds(2 * at, 2)], sems.at[number])
        for number, (piece, at) in enumerate(((first, swap), (second, 1 - swap)))
    ]
    for copy in copies:
        copy.start()
    for copy in copies:
        copy.wait()


def next_sublane(v):
    return pltpu.roll(v, 7, 0)


def last_sublane(v):
    return pltpu.roll(v, 1, 0)


def lane_ahead(v):
    return pltpu.roll(v, 127, 1)


def lane_behind(v):
    return pltpu.roll(v, 1, 1)


def assemble(core, lefts, own, rights, others, numbers, outs):
    for this, (before, after) in ((0, (lefts, others)), (1, (others, rights))):

        @pl.when(core == this)
        def _(before=before, after=after):
            for number, out in zip(numbers, outs):
                out[DMAX : DMAX + OWN] = own[number]
                for n, piece in enumerate(before):
                    at = DMAX - OWN * (n + 1)
                    out[at : at + OWN] = piece[number]
                for n, piece in enumerate(after):
                    at = DMAX + OWN * (n + 1)
                    out[at : at + OWN] = piece[number]


def faces_body(where, arrived, out, amounts, targets):
    start, core = where[1], where[5]
    for number, scr in ((0, amounts), (1, targets)):
        scr[:, 0:64] = arrived[:, number, :].T
    for o in range(OWNERS):
        at = pl.ds(pl.multiple_of(8 * o + 16 * core, 8), 8)
        slots = amounts[at, 0:64]
        amount = jnp.concatenate([slots[q : q + 1] for q in range(8)], axis=1)
        slots = targets[at, 0:64]
        target = jnp.concatenate([slots[q : q + 1] for q in range(8)], axis=1).astype(jnp.int32)
        y = ((target >> 7) & 127) - start
        inside = (y >= 0) & (y < WIN)
        s = (y * 37) >> 8
        place = jnp.where(inside, (target >> 14) * WIN + (y - TILES * s) * 8 + s, -1)
        hit = iota((2 * WIN, 512), 0) == place
        high = amount.astype(BF16).astype(F32)
        low = amount - high
        left = jnp.concatenate([jnp.where(hit, high, 0.0), jnp.where(hit, low, 0.0)], axis=0).astype(BF16)
        lanes = jnp.where(iota((128, 512), 0) == (target & 127), 1.0, 0.0).astype(BF16)
        got = dot_nt(left, lanes)
        out[2 * o : 2 * o + 2] = (got[: 2 * WIN] + got[2 * WIN :]).reshape(2, TILES, 8, 128)


def coefficients(where, k_in, faces, wx, wy, wz, wb, diag, rhs):
    first_row, start = where[0], where[1]
    shape = (8, 128)
    lane = iota(shape, 1)
    z_edge = jnp.where((lane == 0) | (lane == 127), 0.5, 0.0)
    z_half = jnp.where(lane == 127, 0.0, 0.5)
    b_half = jnp.where(lane == 0, 0.0, 0.5)
    last_half = jnp.where(iota(shape, 0) == 7, 0.0, 0.5)

    def link(row):
        return jnp.where((row >= 0) & (row < 127), 0.5, 0.0).astype(F32)

    def one(i):
        row = first_row + i
        after, before = link(row), link(row - 1)
        at_end = jnp.where((row == 0) | (row == 127), 0.5, 0.0).astype(F32)
        up, down = jnp.minimum(i + 1, EXT - 1), jnp.maximum(i - 1, 0)
        ks = [k_in[i, t] for t in range(TILES)]
        ys = [0.5 * (ks[t] + ks[t + 1]) for t in range(TILES - 1)]
        ys.append(last_half * (ks[TILES - 1] + next_sublane(ks[0])))
        for t in range(TILES):
            k = ks[t]
            column = TILES * iota(shape, 0) + (start + t)
            edge = z_edge + at_end + jnp.where((column == 0) | (column == 127), 0.5, 0.0)
            x_after = after * (k + k_in[up, t])
            x_before = before * (k + k_in[down, t])
            z_after = z_half * (k + lane_ahead(k))
            z_before = b_half * (k + lane_behind(k))
            y_before = ys[t - 1] if t else last_sublane(ys[TILES - 1])
            wx[i, t] = x_after
            wy[i, t] = ys[t]
            wz[i, t] = z_after
            wb[i, t] = z_before
            links = (x_after + x_before) + (ys[t] + y_before) + (z_after + z_before)
            diag[i, t] = (diag[i, t] + edge * k) + links
            rhs[i, t] = rhs[i, t] + faces[i, t]

    def four(n, _):
        for q in range(4):
            one(4 * n + q)
        return 0

    lax.fori_loop(0, EXT // 4, four, 0)


def steps(depth, rates, first, x_even, x_odd, d, wx, wy, wz, wb, diag, rhs):
    shift = DMAX - depth

    def rows(i, count, c1, c2, old, new):
        columns = [[old[i - 1 + q, t] for q in range(count + 2)] for t in (TILES - 1, 0)]
        before = [last_sublane(columns[0][q + 1]) for q in range(count)]
        after_end = [next_sublane(columns[1][q + 1]) for q in range(count)]
        y_before = [last_sublane(wy[i + q, TILES - 1]) for q in range(count)]
        here = columns[1]
        for t in range(TILES):
            ahead = [old[i - 1 + q, t + 1] for q in range(count + 2)] if t < TILES - 1 else None
            x_before = wx[i - 1, t]
            for q in range(count):
                v = here[q + 1]
                y_here, x_here = wy[i + q, t], wx[i + q, t]
                total = rhs[i + q, t] - diag[i + q, t] * v
                total = total + (x_here * here[q + 2] + x_before * here[q])
                total = total + (y_here * (ahead[q + 1] if ahead else after_end[q]) + y_before[q] * before[q])
                total = total + (wz[i + q, t] * lane_ahead(v) + wb[i + q, t] * lane_behind(v))
                step = c2 * total + c1 * d[i + q, t]
                d[i + q, t] = step
                new[i + q, t] = v + step
                before[q], y_before[q], x_before = v, y_here, x_here
            here = ahead

    def one(k, old, new):
        c1, c2 = rates[first + k, 0], rates[first + k, 1]
        low = shift + k + 1
        count = OWN + 2 * (depth - 1 - k)

        def several(n, _):
            rows(low + BODY * n, BODY, c1, c2, old, new)
            return 0

        bodies = count // BODY
        lax.fori_loop(0, bodies, several, 0)
        for tail in (2, 4, 6):

            @pl.when(count % BODY == tail)
            def _(tail=tail):
                rows(low + BODY * bodies, tail, c1, c2, old, new)

    def both(n, _):
        one(2 * n, x_even, x_odd)
        one(2 * n + 1, x_odd, x_even)
        return 0

    lax.fori_loop(0, depth // 2, both, 0)


def first_round_body(where, rates, *refs):
    own, near, far, third, other_own, other_near, other_far, faces = refs[:8]
    out, wx, wy, wz, wb, diag, rhs, xa, xb, d = refs[8:]
    mine = (near, far, third)
    assemble(
        where[5], mine, own, mine, (other_own, other_near, other_far), (0, 1, 2, 3), (xa, xb, diag, rhs)
    )
    coefficients(where, xb, faces, wx, wy, wz, wb, diag, rhs)
    d[...] = jnp.zeros(d.shape, F32)
    steps(DMAX, rates, 0, xa, xb, d, wx, wy, wz, wb, diag, rhs)
    for number, ref in ((0, xa), (1, d)):
        out[number] = ref[DMAX : DMAX + OWN]


def last_round_body(where, rates, wx, wy, wz, wb, diag, rhs, own, near, far, other_own, other_near, *rest):
    out, xa, xb, d = rest
    assemble(where[5], (near, far), own, (near, far), (other_own, other_near), (0, 1), (xa, d))
    steps(LATER, rates, DMAX, xa, xb, d, wx, wy, wz, wb, diag, rhs)
    offset = where[2]
    for j in range(16):
        y = offset + j
        s = (y * 37) >> 8
        t = y - TILES * s
        for row in range(OWN):
            out[row, j : j + 1, :] = xa[DMAX + row, t, pl.ds(s, 1), :]


def place_body(where, *refs):
    out = refs[4]
    core, band, half = where[5], where[8], where[9]
    for n in range(4):
        source = (band + (4 - n)) % 4
        for other in range(2):
            block = 4 * ((half + core + other) % 2) + source
            out[:, pl.ds(pl.multiple_of(16 * block, 16), 16), :] = refs[n][other, pl.ds(2 * core, 2)]


def on_device(
    phonon_deviation,
    thermal_field,
    bulk_generation,
    ambient_coupling,
    substance_label,
    material_conductance_table,
    mode_specific_warmth,
    mode_lifetime,
    mode_velocity_ratio,
    angular_cosine_factor,
    region_mesh_node,
    upstream_neighbour,
    interior_local_node,
    boundary_orientation,
    neighbour_partition,
    exterior_local_node,
):
    nb, nd, cells = phonon_deviation.shape
    tile = lax.axis_index("space")
    band = lax.axis_index("band")
    half = tile // 32
    plane = half * 4 + band
    other = (plane + 4) % 8
    chip = (tile % 32) // 2
    order = jnp.int32(0)
    for q, (x, y) in enumerate(PATH):
        order = jnp.where(chip == 4 * y + x, q, order)
    place = 2 * order + tile % 2
    stays = tile % 2 == 0

    def start_of(z):
        return jnp.clip(16 * z - 20, 0, 128 - WIN)

    start = start_of(plane)
    where = jnp.stack(
        [
            4 * place - DMAX,
            start,
            16 * plane - start,
            band * nb,
            jnp.where(place // 16 == half, 0, 1),
            tile % 2,
            jnp.where(stays, start, start_of(other)),
            jnp.where(stays, start_of(other), start),
            band,
            half,
        ]
    ).astype(jnp.int32)
    ext = sds(EXT, TILES, 8, 128)

    pack_shape = sds(4, 2, TILES, 8, 128)
    first, second = call(
        pack_body, [pack_shape, pack_shape], ins=[IN_SMEM, IN_SMEM] + [IN_VMEM] * 4, moved=3 << 20,
        grant=VMEM_MOST,
    )(where, material_conductance_table, thermal_field, substance_label, ambient_coupling, bulk_generation)
    first, second, where = lax.optimization_barrier((first, second, where))
    got_first = lax.ppermute(first, BOTH, chip_perm((0, 1)))
    got_second = lax.ppermute(second, BOTH, chip_perm((1, 0)))

    again, sums, targets, inflow, rates = call(
        transport_body,
        [sds(nb, nd, cells), sds(10, cells), sds(1, cells), sds(nd, cells), sds(3 * nb, cells)],
        ins=[IN_SMEM] * 4 + [IN_VMEM] * 9,
        scratch=[pltpu.VMEM((nd, cells), F32), pltpu.VMEM((8, 128), F32)],
        flops=2 * 1600 * 512 * 512 * 4,
        moved=4 << 20,
        grant=VMEM_MOST,
    )(
        where,
        mode_specific_warmth,
        mode_lifetime,
        mode_velocity_ratio,
        phonon_deviation,
        thermal_field.reshape(256, 128),
        region_mesh_node.reshape(1, -1),
        upstream_neighbour,
        interior_local_node.reshape(1, -1),
        boundary_orientation.reshape(1, -1),
        neighbour_partition.reshape(1, -1),
        exterior_local_node.reshape(1, -1),
        angular_cosine_factor,
    )
    shares = [sums] + [
        lax.ppermute(sums, "band", [(i, (i + turn) % 4) for i in range(4)]) for turn in (1, 2, 3)
    ]

    packets = call(
        deal_body,
        sds(64, 2, 128),
        ins=[IN_VMEM] * 5,
        scratch=[pltpu.VMEM((8, 768), F32)],
        moved=1 << 18,
    )(*shares, targets)

    packets, got_first, got_second = lax.optimization_barrier((packets, got_first, got_second))
    block = call(
        join_body,
        sds(4, OWN, TILES, 8, 128),
        ins=[IN_SMEM, ANYWHERE, ANYWHERE],
        scratch=[pltpu.SemaphoreType.DMA((2,))],
        moved=2 << 20,
        space=pl.ANY,
    )(where, got_first, got_second)
    packets, block = lax.optimization_barrier((packets, block))
    near = lax.ppermute(block, BOTH, NEXT)
    far = lax.ppermute(block, BOTH, SECOND)
    third = lax.ppermute(block, BOTH, THIRD)
    other_own = lax.ppermute(block, BOTH, SIBLING)
    arrived = lax.all_to_all(packets, "space", split_axis=0, concat_axis=0, tiled=True)
    near, far, third, other_own, arrived = lax.optimization_barrier((near, far, third, other_own, arrived))
    other_near = lax.ppermute(near, BOTH, SIBLING)
    other_far = lax.ppermute(far, BOTH, SIBLING)
    faces = call(
        faces_body,
        ext,
        ins=[IN_SMEM, IN_VMEM],
        scratch=[pltpu.VMEM((128, 128), F32)] * 2,
        flops=1 << 30,
        moved=1 << 20,
    )(where, arrived)

    factors = jnp.array(chebyshev_table(ITERS), F32)
    work = 25 * DMAX * (OWN + DMAX) * 8192
    scratch = [pltpu.VMEM((EXT, TILES, 8, 128), F32)] * 3
    state, *operator = call(
        first_round_body,
        [sds(2, OWN, TILES, 8, 128)] + [ext] * 6,
        ins=[IN_SMEM] * 2 + [IN_VMEM] * 8,
        scratch=scratch,
        flops=work,
        moved=8 << 20,
    )(where, factors, block, near, far, third, other_own, other_near, other_far, faces)
    near = lax.ppermute(state, BOTH, NEXT)
    far = lax.ppermute(state, BOTH, SECOND)
    other_own = lax.ppermute(state, BOTH, SIBLING)
    energy = call(
        finish_body,
        sds(nb, nd, cells),
        ins=[IN_VMEM] * 7,
        flops=8 * nb * nd * cells,
        moved=3 << 20,
    )(rates, again, *shares, inflow)
    near, far, other_own, energy = lax.optimization_barrier((near, far, other_own, energy))
    other_near = lax.ppermute(near, BOTH, SIBLING)
    state = call(
        last_round_body,
        sds(OWN, 16, 128),
        ins=[IN_SMEM] * 2 + [IN_VMEM] * 11,
        scratch=scratch,
        flops=work,
        moved=8 << 20,
    )(where, factors, *operator, state, near, far, other_own, other_near)

    rows = lax.ppermute(state, BOTH, [(b, a) for a, b in chip_perm((0, 1))])
    rows = jnp.stack([rows, lax.ppermute(rows, BOTH, SIBLING)])
    pieces = [rows] + [
        lax.ppermute(rows, "band", [(i, (i + turn) % 4) for i in range(4)]) for turn in (1, 2, 3)
    ]
    temperature = call(place_body, sds(2, 128, 128), ins=[IN_SMEM] + [IN_VMEM] * 4, moved=1 << 18)(
        where, *pieces
    )
    return temperature, energy


def solution(mesh):
    return jax.shard_map(
        on_device,
        mesh=mesh,
        in_specs=(
            P("band", None, "space"),
            P("space", None, None),
            P("space", None, None),
            P("space", None, None),
            P("space", None, None),
            P(),
            P(),
            P(),
            P(),
            P(),
            P("space"),
            P(None, "space"),
            P("space"),
            P("space"),
            P("space", None),
            P("space"),
        ),
        out_specs=(P("space", None, None), P("band", None, "space")),
        check_vma=False,
    )
```

```python
import jax
import jax.numpy as jnp
from jax import lax
from jax.experimental import pallas as pl
from jax.experimental.pallas import tpu as pltpu
from jax.sharding import PartitionSpec as P

ITERS = 20
BOTH = ("space", "band")
F32 = jnp.float32
BF16 = jnp.bfloat16
VMEM_BYTES = 24 * 1024 * 1024
VMEM_MOST = 56 * 1024 * 1024

DMAX = 12
LATER = ITERS - DMAX
OWN = 4
EXT = OWN + 2 * DMAX
BODY = 8
OWNERS = EXT // 2
TILES = 9
WIN = 8 * TILES

lowest = 0.5
highest = 50.0


def chebyshev_table(count):
    centre = (highest + lowest) / 2.0
    spread = (highest - lowest) / 2.0
    ratio = centre / spread
    rho_prev = 1.0 / ratio
    table = [(0.0, 1.0 / centre)]
    for number in range(1, count):
        rho_next = 1.0 / (2.0 * ratio - rho_prev)
        table.append((rho_next * rho_prev, 2.0 * rho_next / spread))
        rho_prev = rho_next
    return table


PATH = (
    (3, 0), (2, 0), (2, 1), (3, 1), (3, 2), (3, 3), (2, 3), (2, 2),
    (1, 1), (1, 0), (0, 0), (0, 1), (0, 2), (1, 2), (1, 3), (0, 3),
)


def spot_of(m):
    x, y = PATH[m // 2]
    return (y * 4 + x) * 2 + m % 2


def flat(z, spot):
    return ((z // 4) * 32 + spot) * 4 + z % 4


def along(move):
    return [
        (flat(z, spot_of(m)), flat(z, spot_of(move(m))))
        for z in range(8)
        for m in range(32)
        if 0 <= move(m) < 32
    ]


NEXT = along(lambda m: m + 1 if m % 2 else m - 1)
SECOND = along(lambda m: m - 2 if m % 2 else m + 2)
THIRD = along(lambda m: m + 3 if m % 2 else m - 3)
SIBLING = along(lambda m: m ^ 1)


def chip_perm(cores):
    pairs = []
    for z in range(8):
        for chip in range(16):
            place = spot_of(chip + 16 * (z // 4))
            for core, target in zip(cores, (z, (z + 4) % 8)):
                pairs.append((flat(z, 2 * chip + core), flat(target, place)))
    return pairs


HOME = [
    [(flat(z, spot_of(chip + 16 * (z // 4))), flat(z, 2 * chip + core)) for z in range(8) for chip in range(16)]
    for core in range(2)
]


def call(body, outs, *, ins, scratch=(), flops=0, moved=0, space=pltpu.VMEM, grant=VMEM_BYTES):
    return pl.pallas_call(
        body,
        out_shape=outs,
        in_specs=ins,
        out_specs=jax.tree.map(lambda _: pl.BlockSpec(memory_space=space), outs),
        scratch_shapes=list(scratch),
        compiler_params=pltpu.CompilerParams(vmem_limit_bytes=grant),
        cost_estimate=pl.CostEstimate(flops=flops, bytes_accessed=moved, transcendentals=0),
    )


IN_VMEM = pl.BlockSpec(memory_space=pltpu.VMEM)
IN_SMEM = pl.BlockSpec(memory_space=pltpu.SMEM)
ANYWHERE = pl.BlockSpec(memory_space=pl.ANY)


def sds(*shape):
    return jax.ShapeDtypeStruct(shape, F32)


def halves(values):
    high = values.astype(BF16)
    low = (values - high.astype(F32)).astype(BF16)
    return high, low


def dot(a, b):
    return jnp.dot(a, b, preferred_element_type=F32)


def dot_nt(a, b):
    return lax.dot_general(a, b, (((1,), (1,)), ((), ())), preferred_element_type=F32)


def iota(shape, axis):
    return lax.broadcasted_iota(jnp.int32, shape, axis)


def full(value, width=128):
    return jnp.full((1, width), value, F32)


def wide(row):
    return jnp.concatenate([row] * 4, axis=1)


def transport_body(
    where, warmth, lifetime, velocity, phonon, field, node, upwind, behind, side, owners, beyond, cosines,
    again_out, sums_out, inflow_out, rates_out, vscr, cscr,
):
    nb, nd, _ = phonon.shape
    first_band = where[3]

    capacity, sum_alpha, sum_ab, carry = full(0.0), full(0.0), full(0.0), full(0.0)
    for b in range(warmth.shape[0]):
        storage, speed, weight = full(warmth[b]), full(velocity[b]), 1.0 / full(lifetime[b])
        scale = 1.0 / (speed + weight)
        alpha, beta = storage * weight * scale, speed * scale
        capacity = capacity + storage * weight
        sum_alpha = sum_alpha + alpha
        sum_ab = sum_ab + alpha * beta
        carry = carry + alpha * weight
    unit = 1.0 / (nd * capacity)
    carry, sum_alpha, sum_ab = wide(carry / capacity), wide(sum_alpha), wide(sum_ab)
    alphas, betas, stores, means = [], [], [], []
    for b in range(nb):
        storage = full(warmth[first_band + b])
        speed, weight = full(velocity[first_band + b]), 1.0 / full(lifetime[first_band + b])
        scale = 1.0 / (speed + weight)
        alphas.append(wide(storage * weight * scale))
        betas.append(wide(speed * scale))
        stores.append(wide(storage))
        means.append(wide(weight * unit))
        rates_out[b : b + 1, :] = alphas[b]
        rates_out[nb + b : nb + b + 1, :] = betas[b]
        rates_out[2 * nb + b : 2 * nb + b + 1, :] = stores[b]

    cell = node[...]
    rows_hot = jnp.where(iota((256, 512), 0) == (cell >> 7), 1.0, 0.0).astype(BF16)
    turned = field[...].T
    high, low = halves(turned)
    picked = dot(high, rows_hot) + dot(low, rows_hot)
    patch = jnp.sum(jnp.where(iota((128, 512), 0) == (cell & 127), picked, 0.0), axis=0, keepdims=True)

    m0 = jnp.zeros((1, 512), F32)
    for b in range(nb):
        m0 = m0 + means[b] * jnp.sum(phonon[b], axis=0, keepdims=True)
    m0h, m0l = halves(m0)
    m0_rows = jnp.where(
        iota((16, 512), 0) == 0, m0h.astype(F32), jnp.where(iota((16, 512), 0) == 1, m0l.astype(F32), 0.0)
    ).astype(BF16)

    first_half = iota((24, 512), 0) < 12
    mid_first = iota((1, 8, 512), 1) < 4
    share = jnp.zeros((1, 512), F32)
    for pair in range(4):
        hots, blanks = [], []
        for odd in range(2):
            source = upwind[2 * pair + odd : 2 * pair + odd + 1, :]
            hots.append(jnp.where(iota((512, 512), 0) == source, 1.0, 0.0).astype(BF16))
            blanks.append(jnp.where(source < 0, patch, 0.0))
        inflow = jnp.where(first_half, blanks[0], blanks[1])
        inflow_out[pair * 24 : pair * 24 + 24, :] = inflow

        def gather(values, extra):
            parts = []
            moms = []
            for odd in range(2):
                chunk = values[:, 8 * odd : 8 * odd + 16, :].reshape(nb * 16, 512)
                h, l = halves(chunk)
                pieces = [h, l] + ([m0_rows] if extra else [])
                got = dot(jnp.concatenate(pieces, axis=0), hots[odd])
                parts.append((got[: nb * 16] + got[nb * 16 : nb * 32]).reshape(nb, 16, 512))
                if extra:
                    moms.append(got[nb * 32 : nb * 32 + 1] + got[nb * 32 + 1 : nb * 32 + 2])
            a, b = parts
            middle = jnp.where(mid_first, a[:, 8:16], b[:, 0:8])
            return jnp.concatenate([a[:, 0:8], middle, b[:, 8:16]], axis=1), moms

        first, moms = gather(phonon[:, pair * 24 : pair * 24 + 24, :], True)
        for odd in range(2):
            sums_out[2 * pair + odd : 2 * pair + odd + 1, :] = moms[odd]
        ups = []
        for b in range(nb):
            up = first[b] + stores[b] * inflow
            share = share + (means[b] * betas[b]) * jnp.sum(up, axis=0, keepdims=True)
            ups.append(up[None])
        second, _ = gather(jnp.concatenate(ups, axis=0), False)
        again_out[:, pair * 24 : pair * 24 + 24, :] = second
        total = jnp.zeros((24, 512), F32)
        for b in range(nb):
            total = total + (betas[b] * betas[b]) * second[b] + (betas[b] * stores[b]) * inflow
        vscr[pair * 24 : pair * 24 + 24, :] = total + sum_ab * jnp.where(first_half, moms[0], moms[1])

    m1 = carry * m0 + share
    sums_out[8:9, :] = m1
    field_sum = vscr[...] + sum_alpha * m1
    cscr[...] = jnp.zeros((8, 128), F32)
    cscr[0:6, 0:96] = cosines[...]
    by_side = jnp.dot(
        cscr[:, 0:96], field_sum, precision=lax.Precision.HIGHEST, preferred_element_type=F32
    )

    hot = jnp.where(iota((512, 256), 0) == behind[...], 1.0, 0.0).astype(BF16)
    h, l = halves(by_side)
    at_face = dot(jnp.concatenate([h.astype(F32), l.astype(F32)], axis=0).astype(BF16), hot)
    at_face = at_face[0:8] + at_face[8:16]
    flux = jnp.sum(jnp.where(iota((8, 256), 0) == side[...], at_face, 0.0), axis=0, keepdims=True)
    owner_row = owners[...]
    column = jnp.broadcast_to(owner_row.astype(F32), (128, 256)).T
    column = jnp.concatenate([column, column], axis=1)
    same = (column == owner_row.astype(F32)) & (iota((256, 256), 0) < iota((256, 256), 1))
    place = jnp.sum(jnp.where(same, 1.0, 0.0), axis=0, keepdims=True).astype(jnp.int32)
    slot = owner_row * 8 + place
    slots = jnp.where(iota((512, 256), 0) == slot, 1.0, 0.0).astype(BF16)
    h, l = halves(flux)
    line = iota((16, 256), 0)
    target = beyond[...]
    rows = jnp.where(line == 0, h.astype(F32), 0.0)
    rows = jnp.where(line == 1, l.astype(F32), rows)
    rows = jnp.where(line == 2, (target >> 7).astype(F32), rows)
    rows = jnp.where(line == 3, (target & 127).astype(F32), rows)
    packed = dot_nt(rows.astype(BF16), slots)
    sums_out[9:10, :] = packed[0:1] + packed[1:2]
    sums_out[10:11, :] = packed[2:3] * 128.0 + packed[3:4]


def deal_body(sums_a, sums_b, sums_c, sums_d, out, scr):
    scr[...] = jnp.zeros(scr.shape, F32)
    scr[0:1, 128:640] = (sums_a[9:10, :] + sums_b[9:10, :]) + (sums_c[9:10, :] + sums_d[9:10, :])
    scr[1:2, 128:640] = sums_a[10:11, :]
    lead = 128 - 8 * (DMAX // 2)
    for q, (x, y) in enumerate(PATH):
        at = lead + 32 * q
        base = at // 128 * 128
        rolled = pltpu.roll(scr[:, base : base + 256], (256 - (at - base)) % 256, 1)[0:2, 0:128]
        for device in (2 * (4 * y + x), 2 * (4 * y + x) + 1):
            out[device] = rolled
            out[32 + device] = rolled


def finish_body(rates, again, sums_a, sums_b, sums_c, sums_d, inflow, energy_out):
    nb = again.shape[0]
    first_half = iota((24, 512), 0) < 12
    sums = (sums_a[...] + sums_b[...]) + (sums_c[...] + sums_d[...])
    m1 = sums[8:9, :]
    for pair in range(4):
        span = slice(pair * 24, pair * 24 + 24)
        mom = jnp.where(first_half, sums[2 * pair : 2 * pair + 1, :], sums[2 * pair + 1 : 2 * pair + 2, :])
        blank = inflow[span, :]
        for b in range(nb):
            alpha = rates[b : b + 1, :]
            beta = rates[nb + b : nb + b + 1, :]
            storage = rates[2 * nb + b : 2 * nb + b + 1, :]
            upstream = beta * again[b, span, :] + alpha * mom + storage * blank
            energy_out[b, span, :] = alpha * m1 + beta * upstream


def pack_body(where, table, thermal, label, sink, bulk, out):
    start = where[1]
    for row in range(2):
        for t in range(TILES):
            at = pl.ds(start + t, 8, stride=TILES)
            out[0, row, t] = thermal[row, at, :]
            kinds = label[row, at, :]
            k = jnp.zeros((8, 128), F32)
            for mat in range(8):
                k = jnp.where(kinds == mat, table[mat], k)
            out[1, row, t] = k
            out[2, row, t] = sink[row, at, :]
            out[3, row, t] = bulk[row, at, :]


def join_body(where, first, second, block_out, sems):
    swap = where[4]
    copies = [
        pltpu.make_async_copy(piece, block_out.at[:, pl.ds(2 * at, 2)], sems.at[number])
        for number, (piece, at) in enumerate(((first, swap), (second, 1 - swap)))
    ]
    for copy in copies:
        copy.start()
    for copy in copies:
        copy.wait()


def next_sublane(v):
    return pltpu.roll(v, 7, 0)


def last_sublane(v):
    return pltpu.roll(v, 1, 0)


def lane_ahead(v):
    return pltpu.roll(v, 127, 1)


def lane_behind(v):
    return pltpu.roll(v, 1, 1)


def assemble(core, lefts, own, rights, others, numbers, outs):
    for this, (before, after) in ((0, (lefts, others)), (1, (others, rights))):

        @pl.when(core == this)
        def _(before=before, after=after):
            for number, out in zip(numbers, outs):
                out[DMAX : DMAX + OWN] = own[number]
                for n, piece in enumerate(before):
                    at = DMAX - OWN * (n + 1)
                    out[at : at + OWN] = piece[number]
                for n, piece in enumerate(after):
                    at = DMAX + OWN * (n + 1)
                    out[at : at + OWN] = piece[number]


def faces_body(where, arrived, out, amounts, targets):
    start, core = where[1], where[5]
    for number, scr in ((0, amounts), (1, targets)):
        scr[:, 0:64] = arrived[:, number, :].T
    for o in range(OWNERS):
        at = pl.ds(pl.multiple_of(8 * o + 16 * core, 8), 8)
        slots = amounts[at, 0:64]
        amount = jnp.concatenate([slots[q : q + 1] for q in range(8)], axis=1)
        slots = targets[at, 0:64]
        target = jnp.concatenate([slots[q : q + 1] for q in range(8)], axis=1).astype(jnp.int32)
        y = ((target >> 7) & 127) - start
        inside = (y >= 0) & (y < WIN)
        s = (y * 57) >> 9
        place = jnp.where(inside, (target >> 14) * WIN + (y - TILES * s) * 8 + s, -1)
        hit = iota((2 * WIN, 512), 0) == place
        high = amount.astype(BF16).astype(F32)
        low = amount - high
        left = jnp.concatenate([jnp.where(hit, high, 0.0), jnp.where(hit, low, 0.0)], axis=0).astype(BF16)
        lanes = jnp.where(iota((128, 512), 0) == (target & 127), 1.0, 0.0).astype(BF16)
        got = dot_nt(left, lanes)
        out[2 * o : 2 * o + 2] = (got[: 2 * WIN] + got[2 * WIN :]).reshape(2, TILES, 8, 128)


def coefficients(where, k_in, faces, wx, wy, wz, wb, diag, rhs):
    first_row, start = where[0], where[1]
    shape = (8, 128)
    lane = iota(shape, 1)
    z_edge = jnp.where((lane == 0) | (lane == 127), 0.5, 0.0)
    z_half = jnp.where(lane == 127, 0.0, 0.5)
    b_half = jnp.where(lane == 0, 0.0, 0.5)
    last_half = jnp.where(iota(shape, 0) == 7, 0.0, 0.5)

    def link(row):
        return jnp.where((row >= 0) & (row < 127), 0.5, 0.0).astype(F32)

    def one(i):
        row = first_row + i
        after, before = link(row), link(row - 1)
        at_end = jnp.where((row == 0) | (row == 127), 0.5, 0.0).astype(F32)
        up, down = jnp.minimum(i + 1, EXT - 1), jnp.maximum(i - 1, 0)
        ks = [k_in[i, t] for t in range(TILES)]
        ys = [0.5 * (ks[t] + ks[t + 1]) for t in range(TILES - 1)]
        ys.append(last_half * (ks[TILES - 1] + next_sublane(ks[0])))
        for t in range(TILES):
            k = ks[t]
            column = TILES * iota(shape, 0) + (start + t)
            edge = z_edge + at_end + jnp.where((column == 0) | (column == 127), 0.5, 0.0)
            x_after = after * (k + k_in[up, t])
            x_before = before * (k + k_in[down, t])
            z_after = z_half * (k + lane_ahead(k))
            z_before = b_half * (k + lane_behind(k))
            y_before = ys[t - 1] if t else last_sublane(ys[TILES - 1])
            wx[i, t] = x_after
            wy[i, t] = ys[t]
            wz[i, t] = z_after
            wb[i, t] = z_before
            links = (x_after + x_before) + (ys[t] + y_before) + (z_after + z_before)
            diag[i, t] = (diag[i, t] + edge * k) + links
            rhs[i, t] = rhs[i, t] + faces[i, t]

    def four(n, _):
        for q in range(4):
            one(4 * n + q)
        return 0

    lax.fori_loop(0, EXT // 4, four, 0)


def steps(depth, rates, first, x_even, x_odd, d, wx, wy, wz, wb, diag, rhs):
    shift = DMAX - depth

    def rows(i, count, c1, c2, old, new):
        columns = [[old[i - 1 + q, t] for q in range(count + 2)] for t in (TILES - 1, 0)]
        before = [last_sublane(columns[0][q + 1]) for q in range(count)]
        after_end = [next_sublane(columns[1][q + 1]) for q in range(count)]
        y_before = [last_sublane(wy[i + q, TILES - 1]) for q in range(count)]
        here = columns[1]
        for t in range(TILES):
            ahead = [old[i - 1 + q, t + 1] for q in range(count + 2)] if t < TILES - 1 else None
            x_before = wx[i - 1, t]
            for q in range(count):
                v = here[q + 1]
                y_here, x_here = wy[i + q, t], wx[i + q, t]
                total = rhs[i + q, t] - diag[i + q, t] * v
                total = total + (x_here * here[q + 2] + x_before * here[q])
                total = total + (y_here * (ahead[q + 1] if ahead else after_end[q]) + y_before[q] * before[q])
                total = total + (wz[i + q, t] * lane_ahead(v) + wb[i + q, t] * lane_behind(v))
                step = c2 * total + c1 * d[i + q, t]
                d[i + q, t] = step
                new[i + q, t] = v + step
                before[q], y_before[q], x_before = v, y_here, x_here
            here = ahead

    def one(k, old, new):
        c1, c2 = rates[first + k, 0], rates[first + k, 1]
        low = shift + k + 1
        count = OWN + 2 * (depth - 1 - k)

        def several(n, _):
            rows(low + BODY * n, BODY, c1, c2, old, new)
            return 0

        bodies = count // BODY
        lax.fori_loop(0, bodies, several, 0)
        for tail in (2, 4, 6):

            @pl.when(count % BODY == tail)
            def _(tail=tail):
                rows(low + BODY * bodies, tail, c1, c2, old, new)

    def both(n, _):
        one(2 * n, x_even, x_odd)
        one(2 * n + 1, x_odd, x_even)
        return 0

    lax.fori_loop(0, depth // 2, both, 0)


def first_round_body(where, rates, *refs):
    own, near, far, third, other_own, other_near, other_far, faces = refs[:8]
    out, wx, wy, wz, wb, diag, rhs, xa, xb, d = refs[8:]
    mine = (near, far, third)
    assemble(
        where[5], mine, own, mine, (other_own, other_near, other_far), (0, 1, 2, 3), (xa, xb, diag, rhs)
    )
    coefficients(where, xb, faces, wx, wy, wz, wb, diag, rhs)
    d[...] = jnp.zeros(d.shape, F32)
    steps(DMAX, rates, 0, xa, xb, d, wx, wy, wz, wb, diag, rhs)
    for number, ref in ((0, xa), (1, d)):
        out[number] = ref[DMAX : DMAX + OWN]


def last_round_body(where, rates, wx, wy, wz, wb, diag, rhs, own, near, far, other_own, other_near, *rest):
    *outs, xa, xb, d = rest
    assemble(where[5], (near, far), own, (near, far), (other_own, other_near), (0, 1), (xa, d))
    steps(LATER, rates, DMAX, xa, xb, d, wx, wy, wz, wb, diag, rhs)
    offset = where[2]
    for j in range(32):
        y = offset + j
        s = (y * 57) >> 9
        t = y - TILES * s
        for row in range(OWN):
            outs[row // 2][row % 2, j : j + 1, :] = xa[DMAX + row, t, pl.ds(s, 1), :]


def place_body(where, *refs):
    out = refs[4]
    for n in range(4):
        source = (where[6] + (4 - n)) % 4
        out[:, pl.ds(pl.multiple_of(32 * source, 32), 32), :] = refs[n][...]


def on_device(
    phonon_deviation,
    thermal_field,
    bulk_generation,
    ambient_coupling,
    substance_label,
    material_conductance_table,
    mode_specific_warmth,
    mode_lifetime,
    mode_velocity_ratio,
    angular_cosine_factor,
    region_mesh_node,
    upstream_neighbour,
    interior_local_node,
    boundary_orientation,
    neighbour_partition,
    exterior_local_node,
):
    nb, nd, cells = phonon_deviation.shape
    tile = lax.axis_index("space")
    band = lax.axis_index("band")
    half = tile // 32
    chip = (tile % 32) // 2
    order = jnp.int32(0)
    for q, (x, y) in enumerate(PATH):
        order = jnp.where(chip == 4 * y + x, q, order)
    place = 2 * order + tile % 2
    start = jnp.clip(32 * band - 20, 0, 128 - WIN)
    away = jnp.where(place // 16 == half, 0, 1)
    where = jnp.stack(
        [4 * place - DMAX, start, 32 * band - start, band * nb, away, tile % 2, band]
    ).astype(jnp.int32)
    ext = sds(EXT, TILES, 8, 128)

    window = call(
        pack_body,
        sds(4, 2, TILES, 8, 128),
        ins=[IN_SMEM, IN_SMEM] + [IN_VMEM] * 4,
        moved=3 << 20,
        grant=VMEM_MOST,
    )(where, material_conductance_table, thermal_field, substance_label, ambient_coupling, bulk_generation)
    window, where = lax.optimization_barrier((window, where))
    got_first = lax.ppermute(window, BOTH, chip_perm((0, 1)))
    got_second = lax.ppermute(window, BOTH, chip_perm((1, 0)))

    again, sums, inflow, rates = call(
        transport_body,
        [sds(nb, nd, cells), sds(11, cells), sds(nd, cells), sds(3 * nb, cells)],
        ins=[IN_SMEM] * 4 + [IN_VMEM] * 9,
        scratch=[pltpu.VMEM((nd, cells), F32), pltpu.VMEM((8, 128), F32)],
        flops=2 * 1600 * 512 * 512 * 4,
        moved=4 << 20,
        grant=VMEM_MOST,
    )(
        where,
        mode_specific_warmth,
        mode_lifetime,
        mode_velocity_ratio,
        phonon_deviation,
        thermal_field.reshape(256, 128),
        region_mesh_node.reshape(1, -1),
        upstream_neighbour,
        interior_local_node.reshape(1, -1),
        boundary_orientation.reshape(1, -1),
        neighbour_partition.reshape(1, -1),
        exterior_local_node.reshape(1, -1),
        angular_cosine_factor,
    )
    shares = [sums] + [
        lax.ppermute(sums, "band", [(i, (i + turn) % 4) for i in range(4)]) for turn in (1, 2, 3)
    ]

    packets = call(
        deal_body,
        sds(64, 2, 128),
        ins=[IN_VMEM] * 4,
        scratch=[pltpu.VMEM((8, 768), F32)],
        moved=1 << 18,
    )(*shares)

    packets, got_first, got_second = lax.optimization_barrier((packets, got_first, got_second))
    block = call(
        join_body,
        sds(4, OWN, TILES, 8, 128),
        ins=[IN_SMEM, ANYWHERE, ANYWHERE],
        scratch=[pltpu.SemaphoreType.DMA((2,))],
        moved=2 << 20,
        space=pl.ANY,
    )(where, got_first, got_second)
    packets, block = lax.optimization_barrier((packets, block))
    near = lax.ppermute(block, BOTH, NEXT)
    far = lax.ppermute(block, BOTH, SECOND)
    third = lax.ppermute(block, BOTH, THIRD)
    other_own = lax.ppermute(block, BOTH, SIBLING)
    arrived = lax.all_to_all(packets, "space", split_axis=0, concat_axis=0, tiled=True)
    near, far, third, other_own, arrived = lax.optimization_barrier((near, far, third, other_own, arrived))
    other_near = lax.ppermute(near, BOTH, SIBLING)
    other_far = lax.ppermute(far, BOTH, SIBLING)
    faces = call(
        faces_body,
        ext,
        ins=[IN_SMEM, IN_VMEM],
        scratch=[pltpu.VMEM((128, 128), F32)] * 2,
        flops=1 << 30,
        moved=1 << 20,
    )(where, arrived)

    factors = jnp.array(chebyshev_table(ITERS), F32)
    work = 25 * DMAX * (OWN + DMAX) * 8192
    scratch = [pltpu.VMEM((EXT, TILES, 8, 128), F32)] * 3
    state, *operator = call(
        first_round_body,
        [sds(2, OWN, TILES, 8, 128)] + [ext] * 6,
        ins=[IN_SMEM] * 2 + [IN_VMEM] * 8,
        scratch=scratch,
        flops=work,
        moved=8 << 20,
    )(where, factors, block, near, far, third, other_own, other_near, other_far, faces)
    near = lax.ppermute(state, BOTH, NEXT)
    far = lax.ppermute(state, BOTH, SECOND)
    other_own = lax.ppermute(state, BOTH, SIBLING)
    energy = call(
        finish_body,
        sds(nb, nd, cells),
        ins=[IN_VMEM] * 7,
        flops=8 * nb * nd * cells,
        moved=3 << 20,
    )(rates, again, *shares, inflow)
    near, far, other_own, energy = lax.optimization_barrier((near, far, other_own, energy))
    other_near = lax.ppermute(near, BOTH, SIBLING)
    state = call(
        last_round_body,
        [sds(2, 32, 128)] * 2,
        ins=[IN_SMEM] * 2 + [IN_VMEM] * 11,
        scratch=scratch,
        flops=work,
        moved=8 << 20,
    )(where, factors, *operator, state, near, far, other_own, other_near)

    rows = sum(lax.ppermute(state[core], BOTH, HOME[core]) for core in range(2))
    pieces = [rows] + [
        lax.ppermute(rows, "band", [(i, (i + turn) % 4) for i in range(4)]) for turn in (1, 2, 3)
    ]
    temperature = call(place_body, sds(2, 128, 128), ins=[IN_SMEM] + [IN_VMEM] * 4, moved=1 << 18)(
        where, *pieces
    )
    return temperature, energy


def solution(mesh):
    return jax.shard_map(
        on_device,
        mesh=mesh,
        in_specs=(
            P("band", None, "space"),
            P("space", None, None),
            P("space", None, None),
            P("space", None, None),
            P("space", None, None),
            P(),
            P(),
            P(),
            P(),
            P(),
            P("space"),
            P(None, "space"),
            P("space"),
            P("space"),
            P("space", None),
            P("space"),
        ),
        out_specs=(P("space", None, None), P("band", None, "space")),
        check_vma=False,
    )
```

```python
import jax
import jax.numpy as jnp
from jax import lax
from jax.experimental import pallas as pl
from jax.experimental.pallas import tpu as pltpu
from jax.sharding import PartitionSpec as P

ITERS = 20
BOTH = ("space", "band")
F32 = jnp.float32
BF16 = jnp.bfloat16
VMEM_BYTES = 24 * 1024 * 1024
VMEM_MOST = 56 * 1024 * 1024

DMAX = 12
LATER = ITERS - DMAX
OWN = 4
EXT = OWN + 2 * DMAX
BODY = 8
OWNERS = EXT // 2
TILES = 7
WIN = 8 * TILES

lowest = 0.5
highest = 50.0


def chebyshev_table(count):
    centre = (highest + lowest) / 2.0
    spread = (highest - lowest) / 2.0
    ratio = centre / spread
    rho_prev = 1.0 / ratio
    table = [(0.0, 1.0 / centre)]
    for number in range(1, count):
        rho_next = 1.0 / (2.0 * ratio - rho_prev)
        table.append((rho_next * rho_prev, 2.0 * rho_next / spread))
        rho_prev = rho_next
    return table


PATH = (
    (3, 0), (2, 0), (2, 1), (3, 1), (3, 2), (3, 3), (2, 3), (2, 2),
    (1, 1), (1, 0), (0, 0), (0, 1), (0, 2), (1, 2), (1, 3), (0, 3),
)


def spot_of(m):
    x, y = PATH[m // 2]
    return (y * 4 + x) * 2 + m % 2


def flat(z, spot):
    return ((z // 4) * 32 + spot) * 4 + z % 4


def along(move):
    return [
        (flat(z, spot_of(m)), flat(z, spot_of(move(m))))
        for z in range(8)
        for m in range(32)
        if 0 <= move(m) < 32
    ]


NEXT = along(lambda m: m + 1 if m % 2 else m - 1)
SECOND = along(lambda m: m - 2 if m % 2 else m + 2)
THIRD = along(lambda m: m + 3 if m % 2 else m - 3)
SIBLING = along(lambda m: m ^ 1)


def chip_perm(cores):
    pairs = []
    for z in range(8):
        for chip in range(16):
            place = spot_of(chip + 16 * (z // 4))
            for core, target in zip(cores, (z, (z + 4) % 8)):
                pairs.append((flat(z, 2 * chip + core), flat(target, place)))
    return pairs


def call(body, outs, *, ins, scratch=(), flops=0, moved=0, space=pltpu.VMEM, grant=VMEM_BYTES):
    return pl.pallas_call(
        body,
        out_shape=outs,
        in_specs=ins,
        out_specs=jax.tree.map(lambda _: pl.BlockSpec(memory_space=space), outs),
        scratch_shapes=list(scratch),
        compiler_params=pltpu.CompilerParams(vmem_limit_bytes=grant),
        cost_estimate=pl.CostEstimate(flops=flops, bytes_accessed=moved, transcendentals=0),
    )


IN_VMEM = pl.BlockSpec(memory_space=pltpu.VMEM)
IN_SMEM = pl.BlockSpec(memory_space=pltpu.SMEM)
ANYWHERE = pl.BlockSpec(memory_space=pl.ANY)


def sds(*shape):
    return jax.ShapeDtypeStruct(shape, F32)


def halves(values):
    high = values.astype(BF16)
    low = (values - high.astype(F32)).astype(BF16)
    return high, low


def dot(a, b):
    return jnp.dot(a, b, preferred_element_type=F32)


def dot_nt(a, b):
    return lax.dot_general(a, b, (((1,), (1,)), ((), ())), preferred_element_type=F32)


def iota(shape, axis):
    return lax.broadcasted_iota(jnp.int32, shape, axis)


def full(value, width=128):
    return jnp.full((1, width), value, F32)


def wide(row):
    return jnp.concatenate([row] * 4, axis=1)


def transport_body(
    where, warmth, lifetime, velocity, phonon, field, node, upwind, behind, side, owners, beyond, cosines,
    again_out, sums_out, inflow_out, rates_out, vscr, cscr,
):
    nb, nd, _ = phonon.shape
    first_band = where[3]

    capacity, sum_alpha, sum_ab, carry = full(0.0), full(0.0), full(0.0), full(0.0)
    for b in range(warmth.shape[0]):
        storage, speed, weight = full(warmth[b]), full(velocity[b]), 1.0 / full(lifetime[b])
        scale = 1.0 / (speed + weight)
        alpha, beta = storage * weight * scale, speed * scale
        capacity = capacity + storage * weight
        sum_alpha = sum_alpha + alpha
        sum_ab = sum_ab + alpha * beta
        carry = carry + alpha * weight
    unit = 1.0 / (nd * capacity)
    carry, sum_alpha, sum_ab = wide(carry / capacity), wide(sum_alpha), wide(sum_ab)
    alphas, betas, stores, means = [], [], [], []
    for b in range(nb):
        storage = full(warmth[first_band + b])
        speed, weight = full(velocity[first_band + b]), 1.0 / full(lifetime[first_band + b])
        scale = 1.0 / (speed + weight)
        alphas.append(wide(storage * weight * scale))
        betas.append(wide(speed * scale))
        stores.append(wide(storage))
        means.append(wide(weight * unit))
        rates_out[b : b + 1, :] = alphas[b]
        rates_out[nb + b : nb + b + 1, :] = betas[b]
        rates_out[2 * nb + b : 2 * nb + b + 1, :] = stores[b]

    cell = node[...]
    rows_hot = jnp.where(iota((256, 512), 0) == (cell >> 7), 1.0, 0.0).astype(BF16)
    turned = field[...].T
    high, low = halves(turned)
    picked = dot(high, rows_hot) + dot(low, rows_hot)
    patch = jnp.sum(jnp.where(iota((128, 512), 0) == (cell & 127), picked, 0.0), axis=0, keepdims=True)

    m0 = jnp.zeros((1, 512), F32)
    for b in range(nb):
        m0 = m0 + means[b] * jnp.sum(phonon[b], axis=0, keepdims=True)
    m0h, m0l = halves(m0)
    m0_rows = jnp.where(
        iota((16, 512), 0) == 0, m0h.astype(F32), jnp.where(iota((16, 512), 0) == 1, m0l.astype(F32), 0.0)
    ).astype(BF16)

    first_half = iota((24, 512), 0) < 12
    mid_first = iota((1, 8, 512), 1) < 4
    share = jnp.zeros((1, 512), F32)
    for pair in range(4):
        hots, blanks = [], []
        for odd in range(2):
            source = upwind[2 * pair + odd : 2 * pair + odd + 1, :]
            hots.append(jnp.where(iota((512, 512), 0) == source, 1.0, 0.0).astype(BF16))
            blanks.append(jnp.where(source < 0, patch, 0.0))
        inflow = jnp.where(first_half, blanks[0], blanks[1])
        inflow_out[pair * 24 : pair * 24 + 24, :] = inflow

        def gather(values, extra):
            parts = []
            moms = []
            for odd in range(2):
                chunk = values[:, 8 * odd : 8 * odd + 16, :].reshape(nb * 16, 512)
                h, l = halves(chunk)
                pieces = [h, l] + ([m0_rows] if extra else [])
                got = dot(jnp.concatenate(pieces, axis=0), hots[odd])
                parts.append((got[: nb * 16] + got[nb * 16 : nb * 32]).reshape(nb, 16, 512))
                if extra:
                    moms.append(got[nb * 32 : nb * 32 + 1] + got[nb * 32 + 1 : nb * 32 + 2])
            a, b = parts
            middle = jnp.where(mid_first, a[:, 8:16], b[:, 0:8])
            return jnp.concatenate([a[:, 0:8], middle, b[:, 8:16]], axis=1), moms

        first, moms = gather(phonon[:, pair * 24 : pair * 24 + 24, :], True)
        for odd in range(2):
            sums_out[2 * pair + odd : 2 * pair + odd + 1, :] = moms[odd]
        ups = []
        for b in range(nb):
            up = first[b] + stores[b] * inflow
            share = share + (means[b] * betas[b]) * jnp.sum(up, axis=0, keepdims=True)
            ups.append(up[None])
        second, _ = gather(jnp.concatenate(ups, axis=0), False)
        again_out[:, pair * 24 : pair * 24 + 24, :] = second
        total = jnp.zeros((24, 512), F32)
        for b in range(nb):
            total = total + (betas[b] * betas[b]) * second[b] + (betas[b] * stores[b]) * inflow
        vscr[pair * 24 : pair * 24 + 24, :] = total + sum_ab * jnp.where(first_half, moms[0], moms[1])

    m1 = carry * m0 + share
    sums_out[8:9, :] = m1
    field_sum = vscr[...] + sum_alpha * m1
    cscr[...] = jnp.zeros((8, 128), F32)
    cscr[0:6, 0:96] = cosines[...]
    by_side = jnp.dot(
        cscr[:, 0:96], field_sum, precision=lax.Precision.HIGHEST, preferred_element_type=F32
    )

    hot = jnp.where(iota((512, 256), 0) == behind[...], 1.0, 0.0).astype(BF16)
    h, l = halves(by_side)
    at_face = dot(jnp.concatenate([h.astype(F32), l.astype(F32)], axis=0).astype(BF16), hot)
    at_face = at_face[0:8] + at_face[8:16]
    flux = jnp.sum(jnp.where(iota((8, 256), 0) == side[...], at_face, 0.0), axis=0, keepdims=True)
    owner_row = owners[...]
    column = jnp.broadcast_to(owner_row.astype(F32), (128, 256)).T
    column = jnp.concatenate([column, column], axis=1)
    same = (column == owner_row.astype(F32)) & (iota((256, 256), 0) < iota((256, 256), 1))
    place = jnp.sum(jnp.where(same, 1.0, 0.0), axis=0, keepdims=True).astype(jnp.int32)
    slot = owner_row * 8 + place
    slots = jnp.where(iota((512, 256), 0) == slot, 1.0, 0.0).astype(BF16)
    h, l = halves(flux)
    line = iota((16, 256), 0)
    target = beyond[...]
    rows = jnp.where(line == 0, h.astype(F32), 0.0)
    rows = jnp.where(line == 1, l.astype(F32), rows)
    rows = jnp.where(line == 2, (target >> 7).astype(F32), rows)
    rows = jnp.where(line == 3, (target & 127).astype(F32), rows)
    packed = dot_nt(rows.astype(BF16), slots)
    sums_out[9:10, :] = packed[0:1] + packed[1:2]
    sums_out[10:11, :] = packed[2:3] * 128.0 + packed[3:4]


def deal_body(sums_a, sums_b, sums_c, sums_d, out, scr):
    scr[...] = jnp.zeros(scr.shape, F32)
    scr[0:1, 128:640] = (sums_a[9:10, :] + sums_b[9:10, :]) + (sums_c[9:10, :] + sums_d[9:10, :])
    scr[1:2, 128:640] = sums_a[10:11, :]
    lead = 128 - 8 * (DMAX // 2)
    for q, (x, y) in enumerate(PATH):
        at = lead + 32 * q
        base = at // 128 * 128
        rolled = pltpu.roll(scr[:, base : base + 256], (256 - (at - base)) % 256, 1)[0:2, 0:128]
        for device in (2 * (4 * y + x), 2 * (4 * y + x) + 1):
            out[device] = rolled
            out[32 + device] = rolled


def finish_body(rates, again, sums_a, sums_b, sums_c, sums_d, inflow, energy_out):
    nb = again.shape[0]
    first_half = iota((24, 512), 0) < 12
    sums = (sums_a[...] + sums_b[...]) + (sums_c[...] + sums_d[...])
    m1 = sums[8:9, :]
    for pair in range(4):
        span = slice(pair * 24, pair * 24 + 24)
        mom = jnp.where(first_half, sums[2 * pair : 2 * pair + 1, :], sums[2 * pair + 1 : 2 * pair + 2, :])
        blank = inflow[span, :]
        for b in range(nb):
            alpha = rates[b : b + 1, :]
            beta = rates[nb + b : nb + b + 1, :]
            storage = rates[2 * nb + b : 2 * nb + b + 1, :]
            upstream = beta * again[b, span, :] + alpha * mom + storage * blank
            energy_out[b, span, :] = alpha * m1 + beta * upstream


def pack_body(where, table, thermal, label, sink, bulk, first_out, second_out):
    for number, out in ((6, first_out), (7, second_out)):
        start = where[number]
        for row in range(2):
            for t in range(TILES):
                at = pl.ds(start + t, 8, stride=TILES)
                out[0, row, t] = thermal[row, at, :]
                kinds = label[row, at, :]
                k = jnp.zeros((8, 128), F32)
                for mat in range(8):
                    k = jnp.where(kinds == mat, table[mat], k)
                out[1, row, t] = k
                out[2, row, t] = sink[row, at, :]
                out[3, row, t] = bulk[row, at, :]


def join_body(where, first, second, block_out, sems):
    swap = where[4]
    copies = [
        pltpu.make_async_copy(piece, block_out.at[:, pl.ds(2 * at, 2)], sems.at[number])
        for number, (piece, at) in enumerate(((first, swap), (second, 1 - swap)))
    ]
    for copy in copies:
        copy.start()
    for copy in copies:
        copy.wait()


def next_sublane(v):
    return pltpu.roll(v, 7, 0)


def last_sublane(v):
    return pltpu.roll(v, 1, 0)


def lane_ahead(v):
    return pltpu.roll(v, 127, 1)


def lane_behind(v):
    return pltpu.roll(v, 1, 1)


def assemble(core, lefts, own, rights, others, numbers, outs):
    for this, (before, after) in ((0, (lefts, others)), (1, (others, rights))):

        @pl.when(core == this)
        def _(before=before, after=after):
            for number, out in zip(numbers, outs):
                out[DMAX : DMAX + OWN] = own[number]
                for n, piece in enumerate(before):
                    at = DMAX - OWN * (n + 1)
                    out[at : at + OWN] = piece[number]
                for n, piece in enumerate(after):
                    at = DMAX + OWN * (n + 1)
                    out[at : at + OWN] = piece[number]


def faces_body(where, arrived, out, amounts, targets):
    start, core = where[1], where[5]
    for number, scr in ((0, amounts), (1, targets)):
        scr[:, 0:64] = arrived[:, number, :].T
    for o in range(OWNERS):
        at = pl.ds(pl.multiple_of(8 * o + 16 * core, 8), 8)
        slots = amounts[at, 0:64]
        amount = jnp.concatenate([slots[q : q + 1] for q in range(8)], axis=1)
        slots = targets[at, 0:64]
        target = jnp.concatenate([slots[q : q + 1] for q in range(8)], axis=1).astype(jnp.int32)
        y = ((target >> 7) & 127) - start
        inside = (y >= 0) & (y < WIN)
        s = (y * 37) >> 8
        place = jnp.where(inside, (target >> 14) * WIN + (y - TILES * s) * 8 + s, -1)
        hit = iota((2 * WIN, 512), 0) == place
        high = amount.astype(BF16).astype(F32)
        low = amount - high
        left = jnp.concatenate([jnp.where(hit, high, 0.0), jnp.where(hit, low, 0.0)], axis=0).astype(BF16)
        lanes = jnp.where(iota((128, 512), 0) == (target & 127), 1.0, 0.0).astype(BF16)
        got = dot_nt(left, lanes)
        out[2 * o : 2 * o + 2] = (got[: 2 * WIN] + got[2 * WIN :]).reshape(2, TILES, 8, 128)


def coefficients(where, k_in, faces, wx, wy, wz, wb, diag, rhs):
    first_row, start = where[0], where[1]
    shape = (8, 128)
    lane = iota(shape, 1)
    z_edge = jnp.where((lane == 0) | (lane == 127), 0.5, 0.0)
    z_half = jnp.where(lane == 127, 0.0, 0.5)
    b_half = jnp.where(lane == 0, 0.0, 0.5)
    last_half = jnp.where(iota(shape, 0) == 7, 0.0, 0.5)

    def link(row):
        return jnp.where((row >= 0) & (row < 127), 0.5, 0.0).astype(F32)

    def one(i):
        row = first_row + i
        after, before = link(row), link(row - 1)
        at_end = jnp.where((row == 0) | (row == 127), 0.5, 0.0).astype(F32)
        up, down = jnp.minimum(i + 1, EXT - 1), jnp.maximum(i - 1, 0)
        ks = [k_in[i, t] for t in range(TILES)]
        ys = [0.5 * (ks[t] + ks[t + 1]) for t in range(TILES - 1)]
        ys.append(last_half * (ks[TILES - 1] + next_sublane(ks[0])))
        for t in range(TILES):
            k = ks[t]
            column = TILES * iota(shape, 0) + (start + t)
            edge = z_edge + at_end + jnp.where((column == 0) | (column == 127), 0.5, 0.0)
            x_after = after * (k + k_in[up, t])
            x_before = before * (k + k_in[down, t])
            z_after = z_half * (k + lane_ahead(k))
            z_before = b_half * (k + lane_behind(k))
            y_before = ys[t - 1] if t else last_sublane(ys[TILES - 1])
            wx[i, t] = x_after
            wy[i, t] = ys[t]
            wz[i, t] = z_after
            wb[i, t] = z_before
            links = (x_after + x_before) + (ys[t] + y_before) + (z_after + z_before)
            diag[i, t] = (diag[i, t] + edge * k) + links
            rhs[i, t] = rhs[i, t] + faces[i, t]

    def four(n, _):
        for q in range(4):
            one(4 * n + q)
        return 0

    lax.fori_loop(0, EXT // 4, four, 0)


def steps(depth, rates, first, x_even, x_odd, d, wx, wy, wz, wb, diag, rhs):
    shift = DMAX - depth

    def rows(i, count, c1, c2, old, new):
        columns = [[old[i - 1 + q, t] for q in range(count + 2)] for t in (TILES - 1, 0)]
        before = [last_sublane(columns[0][q + 1]) for q in range(count)]
        after_end = [next_sublane(columns[1][q + 1]) for q in range(count)]
        y_before = [last_sublane(wy[i + q, TILES - 1]) for q in range(count)]
        here = columns[1]
        for t in range(TILES):
            ahead = [old[i - 1 + q, t + 1] for q in range(count + 2)] if t < TILES - 1 else None
            x_before = wx[i - 1, t]
            for q in range(count):
                v = here[q + 1]
                y_here, x_here = wy[i + q, t], wx[i + q, t]
                total = rhs[i + q, t] - diag[i + q, t] * v
                total = total + (x_here * here[q + 2] + x_before * here[q])
                total = total + (y_here * (ahead[q + 1] if ahead else after_end[q]) + y_before[q] * before[q])
                total = total + (wz[i + q, t] * lane_ahead(v) + wb[i + q, t] * lane_behind(v))
                step = c2 * total + c1 * d[i + q, t]
                d[i + q, t] = step
                new[i + q, t] = v + step
                before[q], y_before[q], x_before = v, y_here, x_here
            here = ahead

    def one(k, old, new):
        c1, c2 = rates[first + k, 0], rates[first + k, 1]
        low = shift + k + 1
        count = OWN + 2 * (depth - 1 - k)

        def several(n, _):
            rows(low + BODY * n, BODY, c1, c2, old, new)
            return 0

        bodies = count // BODY
        lax.fori_loop(0, bodies, several, 0)
        for tail in (2, 4, 6):

            @pl.when(count % BODY == tail)
            def _(tail=tail):
                rows(low + BODY * bodies, tail, c1, c2, old, new)

    def both(n, _):
        one(2 * n, x_even, x_odd)
        one(2 * n + 1, x_odd, x_even)
        return 0

    lax.fori_loop(0, depth // 2, both, 0)


def first_round_body(where, rates, *refs):
    own, near, far, third, other_own, other_near, other_far, faces = refs[:8]
    out, wx, wy, wz, wb, diag, rhs, xa, xb, d = refs[8:]
    mine = (near, far, third)
    assemble(
        where[5], mine, own, mine, (other_own, other_near, other_far), (0, 1, 2, 3), (xa, xb, diag, rhs)
    )
    coefficients(where, xb, faces, wx, wy, wz, wb, diag, rhs)
    d[...] = jnp.zeros(d.shape, F32)
    steps(DMAX, rates, 0, xa, xb, d, wx, wy, wz, wb, diag, rhs)
    for number, ref in ((0, xa), (1, d)):
        out[number] = ref[DMAX : DMAX + OWN]


def last_round_body(where, rates, wx, wy, wz, wb, diag, rhs, own, near, far, other_own, other_near, *rest):
    out, xa, xb, d = rest
    assemble(where[5], (near, far), own, (near, far), (other_own, other_near), (0, 1), (xa, d))
    steps(LATER, rates, DMAX, xa, xb, d, wx, wy, wz, wb, diag, rhs)
    offset = where[2]
    for j in range(16):
        y = offset + j
        s = (y * 37) >> 8
        t = y - TILES * s
        for row in range(OWN):
            out[row, j : j + 1, :] = xa[DMAX + row, t, pl.ds(s, 1), :]


def place_body(where, *refs):
    out = refs[4]
    core, band, half = where[5], where[8], where[9]
    for n in range(4):
        source = (band + (4 - n)) % 4
        for other in range(2):
            block = 4 * ((half + core + other) % 2) + source
            out[:, pl.ds(pl.multiple_of(16 * block, 16), 16), :] = refs[n][other, pl.ds(2 * core, 2)]


def on_device(
    phonon_deviation,
    thermal_field,
    bulk_generation,
    ambient_coupling,
    substance_label,
    material_conductance_table,
    mode_specific_warmth,
    mode_lifetime,
    mode_velocity_ratio,
    angular_cosine_factor,
    region_mesh_node,
    upstream_neighbour,
    interior_local_node,
    boundary_orientation,
    neighbour_partition,
    exterior_local_node,
):
    nb, nd, cells = phonon_deviation.shape
    tile = lax.axis_index("space")
    band = lax.axis_index("band")
    half = tile // 32
    plane = half * 4 + band
    other = (plane + 4) % 8
    chip = (tile % 32) // 2
    order = jnp.int32(0)
    for q, (x, y) in enumerate(PATH):
        order = jnp.where(chip == 4 * y + x, q, order)
    place = 2 * order + tile % 2
    stays = tile % 2 == 0

    def start_of(z):
        return jnp.clip(16 * z - 20, 0, 128 - WIN)

    start = start_of(plane)
    where = jnp.stack(
        [
            4 * place - DMAX,
            start,
            16 * plane - start,
            band * nb,
            jnp.where(place // 16 == half, 0, 1),
            tile % 2,
            jnp.where(stays, start, start_of(other)),
            jnp.where(stays, start_of(other), start),
            band,
            half,
        ]
    ).astype(jnp.int32)
    ext = sds(EXT, TILES, 8, 128)

    pack_shape = sds(4, 2, TILES, 8, 128)
    first, second = call(
        pack_body, [pack_shape, pack_shape], ins=[IN_SMEM, IN_SMEM] + [IN_VMEM] * 4, moved=3 << 20,
        grant=VMEM_MOST,
    )(where, material_conductance_table, thermal_field, substance_label, ambient_coupling, bulk_generation)
    first, second, where = lax.optimization_barrier((first, second, where))
    got_first = lax.ppermute(first, BOTH, chip_perm((0, 1)))
    got_second = lax.ppermute(second, BOTH, chip_perm((1, 0)))

    again, sums, inflow, rates = call(
        transport_body,
        [sds(nb, nd, cells), sds(11, cells), sds(nd, cells), sds(3 * nb, cells)],
        ins=[IN_SMEM] * 4 + [IN_VMEM] * 9,
        scratch=[pltpu.VMEM((nd, cells), F32), pltpu.VMEM((8, 128), F32)],
        flops=2 * 1600 * 512 * 512 * 4,
        moved=4 << 20,
        grant=VMEM_MOST,
    )(
        where,
        mode_specific_warmth,
        mode_lifetime,
        mode_velocity_ratio,
        phonon_deviation,
        thermal_field.reshape(256, 128),
        region_mesh_node.reshape(1, -1),
        upstream_neighbour,
        interior_local_node.reshape(1, -1),
        boundary_orientation.reshape(1, -1),
        neighbour_partition.reshape(1, -1),
        exterior_local_node.reshape(1, -1),
        angular_cosine_factor,
    )
    shares = [sums] + [
        lax.ppermute(sums, "band", [(i, (i + turn) % 4) for i in range(4)]) for turn in (1, 2, 3)
    ]

    packets = call(
        deal_body,
        sds(64, 2, 128),
        ins=[IN_VMEM] * 4,
        scratch=[pltpu.VMEM((8, 768), F32)],
        moved=1 << 18,
    )(*shares)

    packets, got_first, got_second = lax.optimization_barrier((packets, got_first, got_second))
    block = call(
        join_body,
        sds(4, OWN, TILES, 8, 128),
        ins=[IN_SMEM, ANYWHERE, ANYWHERE],
        scratch=[pltpu.SemaphoreType.DMA((2,))],
        moved=2 << 20,
        space=pl.ANY,
    )(where, got_first, got_second)
    packets, block = lax.optimization_barrier((packets, block))
    near = lax.ppermute(block, BOTH, NEXT)
    far = lax.ppermute(block, BOTH, SECOND)
    third = lax.ppermute(block, BOTH, THIRD)
    other_own = lax.ppermute(block, BOTH, SIBLING)
    arrived = lax.all_to_all(packets, "space", split_axis=0, concat_axis=0, tiled=True)
    near, far, third, other_own, arrived = lax.optimization_barrier((near, far, third, other_own, arrived))
    other_near = lax.ppermute(near, BOTH, SIBLING)
    other_far = lax.ppermute(far, BOTH, SIBLING)
    faces = call(
        faces_body,
        ext,
        ins=[IN_SMEM, IN_VMEM],
        scratch=[pltpu.VMEM((128, 128), F32)] * 2,
        flops=1 << 30,
        moved=1 << 20,
    )(where, arrived)

    factors = jnp.array(chebyshev_table(ITERS), F32)
    work = 25 * DMAX * (OWN + DMAX) * 8192
    scratch = [pltpu.VMEM((EXT, TILES, 8, 128), F32)] * 3
    state, *operator = call(
        first_round_body,
        [sds(2, OWN, TILES, 8, 128)] + [ext] * 6,
        ins=[IN_SMEM] * 2 + [IN_VMEM] * 8,
        scratch=scratch,
        flops=work,
        moved=8 << 20,
    )(where, factors, block, near, far, third, other_own, other_near, other_far, faces)
    near = lax.ppermute(state, BOTH, NEXT)
    far = lax.ppermute(state, BOTH, SECOND)
    other_own = lax.ppermute(state, BOTH, SIBLING)
    energy = call(
        finish_body,
        sds(nb, nd, cells),
        ins=[IN_VMEM] * 7,
        flops=8 * nb * nd * cells,
        moved=3 << 20,
    )(rates, again, *shares, inflow)
    near, far, other_own, energy = lax.optimization_barrier((near, far, other_own, energy))
    other_near = lax.ppermute(near, BOTH, SIBLING)
    state = call(
        last_round_body,
        sds(OWN, 16, 128),
        ins=[IN_SMEM] * 2 + [IN_VMEM] * 11,
        scratch=scratch,
        flops=work,
        moved=8 << 20,
    )(where, factors, *operator, state, near, far, other_own, other_near)

    rows = lax.ppermute(state, BOTH, [(b, a) for a, b in chip_perm((0, 1))])
    rows = jnp.stack([rows, lax.ppermute(rows, BOTH, SIBLING)])
    pieces = [rows] + [
        lax.ppermute(rows, "band", [(i, (i + turn) % 4) for i in range(4)]) for turn in (1, 2, 3)
    ]
    temperature = call(place_body, sds(2, 128, 128), ins=[IN_SMEM] + [IN_VMEM] * 4, moved=1 << 18)(
        where, *pieces
    )
    return temperature, energy


def solution(mesh):
    return jax.shard_map(
        on_device,
        mesh=mesh,
        in_specs=(
            P("band", None, "space"),
            P("space", None, None),
            P("space", None, None),
            P("space", None, None),
            P("space", None, None),
            P(),
            P(),
            P(),
            P(),
            P(),
            P("space"),
            P(None, "space"),
            P("space"),
            P("space"),
            P("space", None),
            P("space"),
        ),
        out_specs=(P("space", None, None), P("band", None, "space")),
        check_vma=False,
    )
```

```python
import jax
import jax.numpy as jnp
from jax import lax
from jax.experimental import pallas as pl
from jax.experimental.pallas import tpu as pltpu
from jax.sharding import PartitionSpec as P

ITERS = 20
BOTH = ("space", "band")
F32 = jnp.float32
BF16 = jnp.bfloat16
VMEM_BYTES = 24 * 1024 * 1024
VMEM_MOST = 56 * 1024 * 1024

DMAX = 8
LATER = ITERS - 2 * DMAX
OWN = 4
EXT = OWN + 2 * DMAX
BODY = 8
OWNERS = EXT // 2
TILES = 7
WIN = 8 * TILES

lowest = 0.5
highest = 50.0


def chebyshev_table(count):
    centre = (highest + lowest) / 2.0
    spread = (highest - lowest) / 2.0
    ratio = centre / spread
    rho_prev = 1.0 / ratio
    table = [(0.0, 1.0 / centre)]
    for number in range(1, count):
        rho_next = 1.0 / (2.0 * ratio - rho_prev)
        table.append((rho_next * rho_prev, 2.0 * rho_next / spread))
        rho_prev = rho_next
    return table


PATH = (
    (3, 0), (2, 0), (2, 1), (3, 1), (3, 2), (3, 3), (2, 3), (2, 2),
    (1, 1), (1, 0), (0, 0), (0, 1), (0, 2), (1, 2), (1, 3), (0, 3),
)


def spot_of(m):
    x, y = PATH[m // 2]
    return (y * 4 + x) * 2 + m % 2


def flat(z, spot):
    return ((z // 4) * 32 + spot) * 4 + z % 4


def along(move):
    return [
        (flat(z, spot_of(m)), flat(z, spot_of(move(m))))
        for z in range(8)
        for m in range(32)
        if 0 <= move(m) < 32
    ]


NEXT = along(lambda m: m + 1 if m % 2 else m - 1)
SECOND = along(lambda m: m - 2 if m % 2 else m + 2)
SIBLING = along(lambda m: m ^ 1)


def chip_perm(cores):
    pairs = []
    for z in range(8):
        for chip in range(16):
            place = spot_of(chip + 16 * (z // 4))
            for core, target in zip(cores, (z, (z + 4) % 8)):
                pairs.append((flat(z, 2 * chip + core), flat(target, place)))
    return pairs


def call(body, outs, *, ins, scratch=(), flops=0, moved=0, space=pltpu.VMEM, grant=VMEM_BYTES):
    return pl.pallas_call(
        body,
        out_shape=outs,
        in_specs=ins,
        out_specs=jax.tree.map(lambda _: pl.BlockSpec(memory_space=space), outs),
        scratch_shapes=list(scratch),
        compiler_params=pltpu.CompilerParams(vmem_limit_bytes=grant),
        cost_estimate=pl.CostEstimate(flops=flops, bytes_accessed=moved, transcendentals=0),
    )


IN_VMEM = pl.BlockSpec(memory_space=pltpu.VMEM)
IN_SMEM = pl.BlockSpec(memory_space=pltpu.SMEM)
ANYWHERE = pl.BlockSpec(memory_space=pl.ANY)


def sds(*shape):
    return jax.ShapeDtypeStruct(shape, F32)


def halves(values):
    high = values.astype(BF16)
    low = (values - high.astype(F32)).astype(BF16)
    return high, low


def dot(a, b):
    return jnp.dot(a, b, preferred_element_type=F32)


def dot_nt(a, b):
    return lax.dot_general(a, b, (((1,), (1,)), ((), ())), preferred_element_type=F32)


def iota(shape, axis):
    return lax.broadcasted_iota(jnp.int32, shape, axis)


def full(value, width=128):
    return jnp.full((1, width), value, F32)


def wide(row):
    return jnp.concatenate([row] * 4, axis=1)


def transport_body(
    where, warmth, lifetime, velocity, phonon, field, node, upwind, behind, side, owners, beyond, cosines,
    again_out, sums_out, inflow_out, rates_out, vscr, cscr,
):
    nb, nd, _ = phonon.shape
    first_band = where[3]

    capacity, sum_alpha, sum_ab, carry = full(0.0), full(0.0), full(0.0), full(0.0)
    for b in range(warmth.shape[0]):
        storage, speed, weight = full(warmth[b]), full(velocity[b]), 1.0 / full(lifetime[b])
        scale = 1.0 / (speed + weight)
        alpha, beta = storage * weight * scale, speed * scale
        capacity = capacity + storage * weight
        sum_alpha = sum_alpha + alpha
        sum_ab = sum_ab + alpha * beta
        carry = carry + alpha * weight
    unit = 1.0 / (nd * capacity)
    carry, sum_alpha, sum_ab = wide(carry / capacity), wide(sum_alpha), wide(sum_ab)
    alphas, betas, stores, means = [], [], [], []
    for b in range(nb):
        storage = full(warmth[first_band + b])
        speed, weight = full(velocity[first_band + b]), 1.0 / full(lifetime[first_band + b])
        scale = 1.0 / (speed + weight)
        alphas.append(wide(storage * weight * scale))
        betas.append(wide(speed * scale))
        stores.append(wide(storage))
        means.append(wide(weight * unit))
        rates_out[b : b + 1, :] = alphas[b]
        rates_out[nb + b : nb + b + 1, :] = betas[b]
        rates_out[2 * nb + b : 2 * nb + b + 1, :] = stores[b]

    cell = node[...]
    rows_hot = jnp.where(iota((256, 512), 0) == (cell >> 7), 1.0, 0.0).astype(BF16)
    turned = field[...].T
    high, low = halves(turned)
    picked = dot(high, rows_hot) + dot(low, rows_hot)
    patch = jnp.sum(jnp.where(iota((128, 512), 0) == (cell & 127), picked, 0.0), axis=0, keepdims=True)

    m0 = jnp.zeros((1, 512), F32)
    for b in range(nb):
        m0 = m0 + means[b] * jnp.sum(phonon[b], axis=0, keepdims=True)
    m0h, m0l = halves(m0)
    m0_rows = jnp.where(
        iota((16, 512), 0) == 0, m0h.astype(F32), jnp.where(iota((16, 512), 0) == 1, m0l.astype(F32), 0.0)
    ).astype(BF16)

    first_half = iota((24, 512), 0) < 12
    mid_first = iota((1, 8, 512), 1) < 4
    share = jnp.zeros((1, 512), F32)
    for pair in range(4):
        hots, blanks = [], []
        for odd in range(2):
            source = upwind[2 * pair + odd : 2 * pair + odd + 1, :]
            hots.append(jnp.where(iota((512, 512), 0) == source, 1.0, 0.0).astype(BF16))
            blanks.append(jnp.where(source < 0, patch, 0.0))
        inflow = jnp.where(first_half, blanks[0], blanks[1])
        inflow_out[pair * 24 : pair * 24 + 24, :] = inflow

        def gather(values, extra):
            parts = []
            moms = []
            for odd in range(2):
                chunk = values[:, 8 * odd : 8 * odd + 16, :].reshape(nb * 16, 512)
                h, l = halves(chunk)
                pieces = [h, l] + ([m0_rows] if extra else [])
                got = dot(jnp.concatenate(pieces, axis=0), hots[odd])
                parts.append((got[: nb * 16] + got[nb * 16 : nb * 32]).reshape(nb, 16, 512))
                if extra:
                    moms.append(got[nb * 32 : nb * 32 + 1] + got[nb * 32 + 1 : nb * 32 + 2])
            a, b = parts
            middle = jnp.where(mid_first, a[:, 8:16], b[:, 0:8])
            return jnp.concatenate([a[:, 0:8], middle, b[:, 8:16]], axis=1), moms

        first, moms = gather(phonon[:, pair * 24 : pair * 24 + 24, :], True)
        for odd in range(2):
            sums_out[2 * pair + odd : 2 * pair + odd + 1, :] = moms[odd]
        ups = []
        for b in range(nb):
            up = first[b] + stores[b] * inflow
            share = share + (means[b] * betas[b]) * jnp.sum(up, axis=0, keepdims=True)
            ups.append(up[None])
        second, _ = gather(jnp.concatenate(ups, axis=0), False)
        again_out[:, pair * 24 : pair * 24 + 24, :] = second
        total = jnp.zeros((24, 512), F32)
        for b in range(nb):
            total = total + (betas[b] * betas[b]) * second[b] + (betas[b] * stores[b]) * inflow
        vscr[pair * 24 : pair * 24 + 24, :] = total + sum_ab * jnp.where(first_half, moms[0], moms[1])

    m1 = carry * m0 + share
    sums_out[8:9, :] = m1
    field_sum = vscr[...] + sum_alpha * m1
    cscr[...] = jnp.zeros((8, 128), F32)
    cscr[0:6, 0:96] = cosines[...]
    by_side = jnp.dot(
        cscr[:, 0:96], field_sum, precision=lax.Precision.HIGHEST, preferred_element_type=F32
    )

    hot = jnp.where(iota((512, 256), 0) == behind[...], 1.0, 0.0).astype(BF16)
    h, l = halves(by_side)
    at_face = dot(jnp.concatenate([h.astype(F32), l.astype(F32)], axis=0).astype(BF16), hot)
    at_face = at_face[0:8] + at_face[8:16]
    flux = jnp.sum(jnp.where(iota((8, 256), 0) == side[...], at_face, 0.0), axis=0, keepdims=True)
    owner_row = owners[...]
    column = jnp.broadcast_to(owner_row.astype(F32), (128, 256)).T
    column = jnp.concatenate([column, column], axis=1)
    same = (column == owner_row.astype(F32)) & (iota((256, 256), 0) < iota((256, 256), 1))
    place = jnp.sum(jnp.where(same, 1.0, 0.0), axis=0, keepdims=True).astype(jnp.int32)
    slot = owner_row * 8 + place
    slots = jnp.where(iota((512, 256), 0) == slot, 1.0, 0.0).astype(BF16)
    h, l = halves(flux)
    line = iota((16, 256), 0)
    target = beyond[...]
    rows = jnp.where(line == 0, h.astype(F32), 0.0)
    rows = jnp.where(line == 1, l.astype(F32), rows)
    rows = jnp.where(line == 2, (target >> 7).astype(F32), rows)
    rows = jnp.where(line == 3, (target & 127).astype(F32), rows)
    packed = dot_nt(rows.astype(BF16), slots)
    sums_out[9:10, :] = packed[0:1] + packed[1:2]
    sums_out[10:11, :] = packed[2:3] * 128.0 + packed[3:4]


def deal_body(sums_a, sums_b, sums_c, sums_d, out, scr):
    scr[...] = jnp.zeros(scr.shape, F32)
    scr[0:1, 128:640] = (sums_a[9:10, :] + sums_b[9:10, :]) + (sums_c[9:10, :] + sums_d[9:10, :])
    scr[1:2, 128:640] = sums_a[10:11, :]
    lead = 128 - 8 * (DMAX // 2)
    for q, (x, y) in enumerate(PATH):
        at = lead + 32 * q
        base = at // 128 * 128
        rolled = pltpu.roll(scr[:, base : base + 256], (256 - (at - base)) % 256, 1)[0:2, 0:128]
        for device in (2 * (4 * y + x), 2 * (4 * y + x) + 1):
            out[device] = rolled
            out[32 + device] = rolled


def finish_body(rates, again, sums_a, sums_b, sums_c, sums_d, inflow, energy_out):
    nb = again.shape[0]
    first_half = iota((24, 512), 0) < 12
    sums = (sums_a[...] + sums_b[...]) + (sums_c[...] + sums_d[...])
    m1 = sums[8:9, :]
    for pair in range(4):
        span = slice(pair * 24, pair * 24 + 24)
        mom = jnp.where(first_half, sums[2 * pair : 2 * pair + 1, :], sums[2 * pair + 1 : 2 * pair + 2, :])
        blank = inflow[span, :]
        for b in range(nb):
            alpha = rates[b : b + 1, :]
            beta = rates[nb + b : nb + b + 1, :]
            storage = rates[2 * nb + b : 2 * nb + b + 1, :]
            upstream = beta * again[b, span, :] + alpha * mom + storage * blank
            energy_out[b, span, :] = alpha * m1 + beta * upstream


def pack_body(where, table, thermal, label, sink, bulk, first_out, second_out):
    for number, out in ((6, first_out), (7, second_out)):
        start = where[number]
        for row in range(2):
            for t in range(TILES):
                at = pl.ds(start + t, 8, stride=TILES)
                out[0, row, t] = thermal[row, at, :]
                kinds = label[row, at, :]
                k = jnp.zeros((8, 128), F32)
                for mat in range(8):
                    k = jnp.where(kinds == mat, table[mat], k)
                out[1, row, t] = k
                out[2, row, t] = sink[row, at, :]
                out[3, row, t] = bulk[row, at, :]


def join_body(where, first, second, block_out, sems):
    swap = where[4]
    copies = [
        pltpu.make_async_copy(piece, block_out.at[:, pl.ds(2 * at, 2)], sems.at[number])
        for number, (piece, at) in enumerate(((first, swap), (second, 1 - swap)))
    ]
    for copy in copies:
        copy.start()
    for copy in copies:
        copy.wait()


def next_sublane(v):
    return pltpu.roll(v, 7, 0)


def last_sublane(v):
    return pltpu.roll(v, 1, 0)


def lane_ahead(v):
    return pltpu.roll(v, 127, 1)


def lane_behind(v):
    return pltpu.roll(v, 1, 1)


def assemble(core, lefts, own, rights, others, numbers, outs):
    for this, (before, after) in ((0, (lefts, others)), (1, (others, rights))):

        @pl.when(core == this)
        def _(before=before, after=after):
            for number, out in zip(numbers, outs):
                out[DMAX : DMAX + OWN] = own[number]
                for n, piece in enumerate(before):
                    at = DMAX - OWN * (n + 1)
                    out[at : at + OWN] = piece[number]
                for n, piece in enumerate(after):
                    at = DMAX + OWN * (n + 1)
                    out[at : at + OWN] = piece[number]


def faces_body(where, arrived, out, amounts, targets):
    start, core = where[1], where[5]
    for number, scr in ((0, amounts), (1, targets)):
        scr[:, 0:64] = arrived[:, number, :].T
    for o in range(OWNERS):
        at = pl.ds(pl.multiple_of(8 * o + 16 * core, 8), 8)
        slots = amounts[at, 0:64]
        amount = jnp.concatenate([slots[q : q + 1] for q in range(8)], axis=1)
        slots = targets[at, 0:64]
        target = jnp.concatenate([slots[q : q + 1] for q in range(8)], axis=1).astype(jnp.int32)
        y = ((target >> 7) & 127) - start
        inside = (y >= 0) & (y < WIN)
        s = (y * 37) >> 8
        place = jnp.where(inside, (target >> 14) * WIN + (y - TILES * s) * 8 + s, -1)
        hit = iota((2 * WIN, 512), 0) == place
        high = amount.astype(BF16).astype(F32)
        low = amount - high
        left = jnp.concatenate([jnp.where(hit, high, 0.0), jnp.where(hit, low, 0.0)], axis=0).astype(BF16)
        lanes = jnp.where(iota((128, 512), 0) == (target & 127), 1.0, 0.0).astype(BF16)
        got = dot_nt(left, lanes)
        out[2 * o : 2 * o + 2] = (got[: 2 * WIN] + got[2 * WIN :]).reshape(2, TILES, 8, 128)


def coefficients(where, k_in, faces, wx, wy, wz, wb, diag, rhs):
    first_row, start = where[0], where[1]
    shape = (8, 128)
    lane = iota(shape, 1)
    z_edge = jnp.where((lane == 0) | (lane == 127), 0.5, 0.0)
    z_half = jnp.where(lane == 127, 0.0, 0.5)
    b_half = jnp.where(lane == 0, 0.0, 0.5)
    last_half = jnp.where(iota(shape, 0) == 7, 0.0, 0.5)

    def link(row):
        return jnp.where((row >= 0) & (row < 127), 0.5, 0.0).astype(F32)

    def one(i):
        row = first_row + i
        after, before = link(row), link(row - 1)
        at_end = jnp.where((row == 0) | (row == 127), 0.5, 0.0).astype(F32)
        up, down = jnp.minimum(i + 1, EXT - 1), jnp.maximum(i - 1, 0)
        ks = [k_in[i, t] for t in range(TILES)]
        ys = [0.5 * (ks[t] + ks[t + 1]) for t in range(TILES - 1)]
        ys.append(last_half * (ks[TILES - 1] + next_sublane(ks[0])))
        for t in range(TILES):
            k = ks[t]
            column = TILES * iota(shape, 0) + (start + t)
            edge = z_edge + at_end + jnp.where((column == 0) | (column == 127), 0.5, 0.0)
            x_after = after * (k + k_in[up, t])
            x_before = before * (k + k_in[down, t])
            z_after = z_half * (k + lane_ahead(k))
            z_before = b_half * (k + lane_behind(k))
            y_before = ys[t - 1] if t else last_sublane(ys[TILES - 1])
            wx[i, t] = x_after
            wy[i, t] = ys[t]
            wz[i, t] = z_after
            wb[i, t] = z_before
            links = (x_after + x_before) + (ys[t] + y_before) + (z_after + z_before)
            diag[i, t] = (diag[i, t] + edge * k) + links
            rhs[i, t] = rhs[i, t] + faces[i, t]

    def four(n, _):
        for q in range(4):
            one(4 * n + q)
        return 0

    lax.fori_loop(0, EXT // 4, four, 0)


def steps(depth, rates, first, x_even, x_odd, d, wx, wy, wz, wb, diag, rhs):
    shift = DMAX - depth

    def rows(i, count, c1, c2, old, new):
        columns = [[old[i - 1 + q, t] for q in range(count + 2)] for t in (TILES - 1, 0)]
        before = [last_sublane(columns[0][q + 1]) for q in range(count)]
        after_end = [next_sublane(columns[1][q + 1]) for q in range(count)]
        y_before = [last_sublane(wy[i + q, TILES - 1]) for q in range(count)]
        here = columns[1]
        for t in range(TILES):
            ahead = [old[i - 1 + q, t + 1] for q in range(count + 2)] if t < TILES - 1 else None
            x_before = wx[i - 1, t]
            for q in range(count):
                v = here[q + 1]
                y_here, x_here = wy[i + q, t], wx[i + q, t]
                total = rhs[i + q, t] - diag[i + q, t] * v
                total = total + (x_here * here[q + 2] + x_before * here[q])
                total = total + (y_here * (ahead[q + 1] if ahead else after_end[q]) + y_before[q] * before[q])
                total = total + (wz[i + q, t] * lane_ahead(v) + wb[i + q, t] * lane_behind(v))
                step = c2 * total + c1 * d[i + q, t]
                d[i + q, t] = step
                new[i + q, t] = v + step
                before[q], y_before[q], x_before = v, y_here, x_here
            here = ahead

    def one(k, old, new):
        c1, c2 = rates[first + k, 0], rates[first + k, 1]
        low = shift + k + 1
        count = OWN + 2 * (depth - 1 - k)

        def several(n, _):
            rows(low + BODY * n, BODY, c1, c2, old, new)
            return 0

        bodies = count // BODY
        lax.fori_loop(0, bodies, several, 0)
        for tail in (2, 4, 6):

            @pl.when(count % BODY == tail)
            def _(tail=tail):
                rows(low + BODY * bodies, tail, c1, c2, old, new)

    def both(n, _):
        one(2 * n, x_even, x_odd)
        one(2 * n + 1, x_odd, x_even)
        return 0

    lax.fori_loop(0, depth // 2, both, 0)


def first_round_body(where, rates, *refs):
    own, near, far, other_own, other_near, faces = refs[:6]
    out, wx, wy, wz, wb, diag, rhs, xa, xb, d = refs[6:]
    assemble(
        where[5], (near, far), own, (near, far), (other_own, other_near), (0, 1, 2, 3), (xa, xb, diag, rhs)
    )
    coefficients(where, xb, faces, wx, wy, wz, wb, diag, rhs)
    d[...] = jnp.zeros(d.shape, F32)
    steps(DMAX, rates, 0, xa, xb, d, wx, wy, wz, wb, diag, rhs)
    for number, ref in ((0, xa), (1, d)):
        out[number] = ref[DMAX : DMAX + OWN]


def middle_round_body(where, rates, wx, wy, wz, wb, diag, rhs, own, near, far, other_own, other_near, *rest):
    out, xa, xb, d = rest
    assemble(where[5], (near, far), own, (near, far), (other_own, other_near), (0, 1), (xa, d))
    steps(DMAX, rates, DMAX, xa, xb, d, wx, wy, wz, wb, diag, rhs)
    for number, ref in ((0, xa), (1, d)):
        out[number] = ref[DMAX : DMAX + OWN]


def last_round_body(where, rates, wx, wy, wz, wb, diag, rhs, own, near, other_own, *rest):
    out, xa, xb, d = rest
    assemble(where[5], (near,), own, (near,), (other_own,), (0, 1), (xa, d))
    steps(LATER, rates, 2 * DMAX, xa, xb, d, wx, wy, wz, wb, diag, rhs)
    offset = where[2]
    for j in range(16):
        y = offset + j
        s = (y * 37) >> 8
        t = y - TILES * s
        for row in range(OWN):
            out[row, j : j + 1, :] = xa[DMAX + row, t, pl.ds(s, 1), :]


def place_body(where, *refs):
    out = refs[4]
    core, band, half = where[5], where[8], where[9]
    for n in range(4):
        source = (band + (4 - n)) % 4
        for other in range(2):
            block = 4 * ((half + core + other) % 2) + source
            out[:, pl.ds(pl.multiple_of(16 * block, 16), 16), :] = refs[n][other, pl.ds(2 * core, 2)]


def on_device(
    phonon_deviation,
    thermal_field,
    bulk_generation,
    ambient_coupling,
    substance_label,
    material_conductance_table,
    mode_specific_warmth,
    mode_lifetime,
    mode_velocity_ratio,
    angular_cosine_factor,
    region_mesh_node,
    upstream_neighbour,
    interior_local_node,
    boundary_orientation,
    neighbour_partition,
    exterior_local_node,
):
    nb, nd, cells = phonon_deviation.shape
    tile = lax.axis_index("space")
    band = lax.axis_index("band")
    half = tile // 32
    plane = half * 4 + band
    other = (plane + 4) % 8
    chip = (tile % 32) // 2
    order = jnp.int32(0)
    for q, (x, y) in enumerate(PATH):
        order = jnp.where(chip == 4 * y + x, q, order)
    place = 2 * order + tile % 2
    stays = tile % 2 == 0

    def start_of(z):
        return jnp.clip(16 * z - 20, 0, 128 - WIN)

    start = start_of(plane)
    where = jnp.stack(
        [
            4 * place - DMAX,
            start,
            16 * plane - start,
            band * nb,
            jnp.where(place // 16 == half, 0, 1),
            tile % 2,
            jnp.where(stays, start, start_of(other)),
            jnp.where(stays, start_of(other), start),
            band,
            half,
        ]
    ).astype(jnp.int32)
    ext = sds(EXT, TILES, 8, 128)

    pack_shape = sds(4, 2, TILES, 8, 128)
    first, second = call(
        pack_body, [pack_shape, pack_shape], ins=[IN_SMEM, IN_SMEM] + [IN_VMEM] * 4, moved=3 << 20,
        grant=VMEM_MOST,
    )(where, material_conductance_table, thermal_field, substance_label, ambient_coupling, bulk_generation)
    first, second, where = lax.optimization_barrier((first, second, where))
    got_first = lax.ppermute(first, BOTH, chip_perm((0, 1)))
    got_second = lax.ppermute(second, BOTH, chip_perm((1, 0)))

    again, sums, inflow, rates = call(
        transport_body,
        [sds(nb, nd, cells), sds(11, cells), sds(nd, cells), sds(3 * nb, cells)],
        ins=[IN_SMEM] * 4 + [IN_VMEM] * 9,
        scratch=[pltpu.VMEM((nd, cells), F32), pltpu.VMEM((8, 128), F32)],
        flops=2 * 1600 * 512 * 512 * 4,
        moved=4 << 20,
        grant=VMEM_MOST,
    )(
        where,
        mode_specific_warmth,
        mode_lifetime,
        mode_velocity_ratio,
        phonon_deviation,
        thermal_field.reshape(256, 128),
        region_mesh_node.reshape(1, -1),
        upstream_neighbour,
        interior_local_node.reshape(1, -1),
        boundary_orientation.reshape(1, -1),
        neighbour_partition.reshape(1, -1),
        exterior_local_node.reshape(1, -1),
        angular_cosine_factor,
    )
    shares = [sums] + [
        lax.ppermute(sums, "band", [(i, (i + turn) % 4) for i in range(4)]) for turn in (1, 2, 3)
    ]

    packets = call(
        deal_body,
        sds(64, 2, 128),
        ins=[IN_VMEM] * 4,
        scratch=[pltpu.VMEM((8, 768), F32)],
        moved=1 << 18,
    )(*shares)

    packets, got_first, got_second = lax.optimization_barrier((packets, got_first, got_second))
    block = call(
        join_body,
        sds(4, OWN, TILES, 8, 128),
        ins=[IN_SMEM, ANYWHERE, ANYWHERE],
        scratch=[pltpu.SemaphoreType.DMA((2,))],
        moved=2 << 20,
        space=pl.ANY,
    )(where, got_first, got_second)
    packets, block = lax.optimization_barrier((packets, block))
    near = lax.ppermute(block, BOTH, NEXT)
    far = lax.ppermute(block, BOTH, SECOND)
    other_own = lax.ppermute(block, BOTH, SIBLING)
    arrived = lax.all_to_all(packets, "space", split_axis=0, concat_axis=0, tiled=True)
    near, far, other_own, arrived = lax.optimization_barrier((near, far, other_own, arrived))
    other_near = lax.ppermute(near, BOTH, SIBLING)
    faces = call(
        faces_body,
        ext,
        ins=[IN_SMEM, IN_VMEM],
        scratch=[pltpu.VMEM((128, 128), F32)] * 2,
        flops=1 << 30,
        moved=1 << 20,
    )(where, arrived)

    factors = jnp.array(chebyshev_table(ITERS), F32)
    work = 25 * DMAX * (OWN + DMAX) * 8192
    scratch = [pltpu.VMEM((EXT, TILES, 8, 128), F32)] * 3
    state, *operator = call(
        first_round_body,
        [sds(2, OWN, TILES, 8, 128)] + [ext] * 6,
        ins=[IN_SMEM] * 2 + [IN_VMEM] * 6,
        scratch=scratch,
        flops=work,
        moved=8 << 20,
    )(where, factors, block, near, far, other_own, other_near, faces)
    near = lax.ppermute(state, BOTH, NEXT)
    far = lax.ppermute(state, BOTH, SECOND)
    other_own = lax.ppermute(state, BOTH, SIBLING)
    energy = call(
        finish_body,
        sds(nb, nd, cells),
        ins=[IN_VMEM] * 7,
        flops=8 * nb * nd * cells,
        moved=3 << 20,
    )(rates, again, *shares, inflow)
    near, far, other_own, energy = lax.optimization_barrier((near, far, other_own, energy))
    other_near = lax.ppermute(near, BOTH, SIBLING)
    state = call(
        middle_round_body,
        sds(2, OWN, TILES, 8, 128),
        ins=[IN_SMEM] * 2 + [IN_VMEM] * 11,
        scratch=scratch,
        flops=work,
        moved=8 << 20,
    )(where, factors, *operator, state, near, far, other_own, other_near)
    near = lax.ppermute(state, BOTH, NEXT)
    other_own = lax.ppermute(state, BOTH, SIBLING)
    state = call(
        last_round_body,
        sds(OWN, 16, 128),
        ins=[IN_SMEM] * 2 + [IN_VMEM] * 9,
        scratch=scratch,
        flops=work,
        moved=8 << 20,
    )(where, factors, *operator, state, near, other_own)

    rows = lax.ppermute(state, BOTH, [(b, a) for a, b in chip_perm((0, 1))])
    rows = jnp.stack([rows, lax.ppermute(rows, BOTH, SIBLING)])
    pieces = [rows] + [
        lax.ppermute(rows, "band", [(i, (i + turn) % 4) for i in range(4)]) for turn in (1, 2, 3)
    ]
    temperature = call(place_body, sds(2, 128, 128), ins=[IN_SMEM] + [IN_VMEM] * 4, moved=1 << 18)(
        where, *pieces
    )
    return temperature, energy


def solution(mesh):
    return jax.shard_map(
        on_device,
        mesh=mesh,
        in_specs=(
            P("band", None, "space"),
            P("space", None, None),
            P("space", None, None),
            P("space", None, None),
            P("space", None, None),
            P(),
            P(),
            P(),
            P(),
            P(),
            P("space"),
            P(None, "space"),
            P("space"),
            P("space"),
            P("space", None),
            P("space"),
        ),
        out_specs=(P("space", None, None), P("band", None, "space")),
        check_vma=False,
    )
```

```python
import jax
import jax.numpy as jnp
from jax import lax
from jax.experimental import pallas as pl
from jax.experimental.pallas import tpu as pltpu
from jax.sharding import PartitionSpec as P

ITERS = 20
BOTH = ("space", "band")
F32 = jnp.float32
BF16 = jnp.bfloat16
VMEM_BYTES = 24 * 1024 * 1024
VMEM_MOST = 56 * 1024 * 1024

DMAX = 12
LATER = ITERS - DMAX
OWN = 4
EXT = OWN + 2 * DMAX
BODY = 8
OWNERS = EXT // 2
TILES = 7
WIN = 8 * TILES

lowest = 0.5
highest = 50.0


def chebyshev_table(count):
    centre = (highest + lowest) / 2.0
    spread = (highest - lowest) / 2.0
    ratio = centre / spread
    rho_prev = 1.0 / ratio
    table = [(0.0, 1.0 / centre)]
    for number in range(1, count):
        rho_next = 1.0 / (2.0 * ratio - rho_prev)
        table.append((rho_next * rho_prev, 2.0 * rho_next / spread))
        rho_prev = rho_next
    return table


PATH = (
    (3, 0), (2, 0), (2, 1), (3, 1), (3, 2), (3, 3), (2, 3), (2, 2),
    (1, 1), (1, 0), (0, 0), (0, 1), (0, 2), (1, 2), (1, 3), (0, 3),
)


def spot_of(m):
    x, y = PATH[m // 2]
    return (y * 4 + x) * 2 + m % 2


def flat(z, spot):
    return ((z // 4) * 32 + spot) * 4 + z % 4


def along(move):
    return [
        (flat(z, spot_of(m)), flat(z, spot_of(move(m))))
        for z in range(8)
        for m in range(32)
        if 0 <= move(m) < 32
    ]


NEXT = along(lambda m: m + 1 if m % 2 else m - 1)
SECOND = along(lambda m: m - 2 if m % 2 else m + 2)
THIRD = along(lambda m: m + 3 if m % 2 else m - 3)
SIBLING = along(lambda m: m ^ 1)
ACROSS = along(lambda m: m + 2 if m % 2 else m - 2)


def chip_perm(cores):
    pairs = []
    for z in range(8):
        for chip in range(16):
            place = spot_of(chip + 16 * (z // 4))
            for core, target in zip(cores, (z, (z + 4) % 8)):
                pairs.append((flat(z, 2 * chip + core), flat(target, place)))
    return pairs


def call(body, outs, *, ins, scratch=(), flops=0, moved=0, space=pltpu.VMEM, grant=VMEM_BYTES):
    return pl.pallas_call(
        body,
        out_shape=outs,
        in_specs=ins,
        out_specs=jax.tree.map(lambda _: pl.BlockSpec(memory_space=space), outs),
        scratch_shapes=list(scratch),
        compiler_params=pltpu.CompilerParams(vmem_limit_bytes=grant),
        cost_estimate=pl.CostEstimate(flops=flops, bytes_accessed=moved, transcendentals=0),
    )


IN_VMEM = pl.BlockSpec(memory_space=pltpu.VMEM)
IN_SMEM = pl.BlockSpec(memory_space=pltpu.SMEM)
ANYWHERE = pl.BlockSpec(memory_space=pl.ANY)


def sds(*shape):
    return jax.ShapeDtypeStruct(shape, F32)


def halves(values):
    high = values.astype(BF16)
    low = (values - high.astype(F32)).astype(BF16)
    return high, low


def dot(a, b):
    return jnp.dot(a, b, preferred_element_type=F32)


def dot_nt(a, b):
    return lax.dot_general(a, b, (((1,), (1,)), ((), ())), preferred_element_type=F32)


def iota(shape, axis):
    return lax.broadcasted_iota(jnp.int32, shape, axis)


def full(value, width=128):
    return jnp.full((1, width), value, F32)


def wide(row):
    return jnp.concatenate([row] * 4, axis=1)


def transport_body(
    where, warmth, lifetime, velocity, phonon, field, node, upwind, behind, side, owners, beyond, cosines,
    again_out, sums_out, inflow_out, rates_out, vscr, cscr,
):
    nb, nd, _ = phonon.shape
    first_band = where[3]

    capacity, sum_alpha, sum_ab, carry = full(0.0), full(0.0), full(0.0), full(0.0)
    for b in range(warmth.shape[0]):
        storage, speed, weight = full(warmth[b]), full(velocity[b]), 1.0 / full(lifetime[b])
        scale = 1.0 / (speed + weight)
        alpha, beta = storage * weight * scale, speed * scale
        capacity = capacity + storage * weight
        sum_alpha = sum_alpha + alpha
        sum_ab = sum_ab + alpha * beta
        carry = carry + alpha * weight
    unit = 1.0 / (nd * capacity)
    carry, sum_alpha, sum_ab = wide(carry / capacity), wide(sum_alpha), wide(sum_ab)
    alphas, betas, stores, means = [], [], [], []
    for b in range(nb):
        storage = full(warmth[first_band + b])
        speed, weight = full(velocity[first_band + b]), 1.0 / full(lifetime[first_band + b])
        scale = 1.0 / (speed + weight)
        alphas.append(wide(storage * weight * scale))
        betas.append(wide(speed * scale))
        stores.append(wide(storage))
        means.append(wide(weight * unit))
        rates_out[b : b + 1, :] = alphas[b]
        rates_out[nb + b : nb + b + 1, :] = betas[b]
        rates_out[2 * nb + b : 2 * nb + b + 1, :] = stores[b]

    cell = node[...]
    rows_hot = jnp.where(iota((256, 512), 0) == (cell >> 7), 1.0, 0.0).astype(BF16)
    turned = field[...].T
    high, low = halves(turned)
    picked = dot(high, rows_hot) + dot(low, rows_hot)
    patch = jnp.sum(jnp.where(iota((128, 512), 0) == (cell & 127), picked, 0.0), axis=0, keepdims=True)

    m0 = jnp.zeros((1, 512), F32)
    for b in range(nb):
        m0 = m0 + means[b] * jnp.sum(phonon[b], axis=0, keepdims=True)
    m0h, m0l = halves(m0)
    m0_rows = jnp.where(
        iota((16, 512), 0) == 0, m0h.astype(F32), jnp.where(iota((16, 512), 0) == 1, m0l.astype(F32), 0.0)
    ).astype(BF16)

    first_half = iota((24, 512), 0) < 12
    mid_first = iota((1, 8, 512), 1) < 4
    share = jnp.zeros((1, 512), F32)
    for pair in range(4):
        hots, blanks = [], []
        for odd in range(2):
            source = upwind[2 * pair + odd : 2 * pair + odd + 1, :]
            hots.append(jnp.where(iota((512, 512), 0) == source, 1.0, 0.0).astype(BF16))
            blanks.append(jnp.where(source < 0, patch, 0.0))
        inflow = jnp.where(first_half, blanks[0], blanks[1])
        inflow_out[pair * 24 : pair * 24 + 24, :] = inflow

        def gather(values, extra):
            parts = []
            moms = []
            for odd in range(2):
                chunk = values[:, 8 * odd : 8 * odd + 16, :].reshape(nb * 16, 512)
                h, l = halves(chunk)
                pieces = [h, l] + ([m0_rows] if extra else [])
                got = dot(jnp.concatenate(pieces, axis=0), hots[odd])
                parts.append((got[: nb * 16] + got[nb * 16 : nb * 32]).reshape(nb, 16, 512))
                if extra:
                    moms.append(got[nb * 32 : nb * 32 + 1] + got[nb * 32 + 1 : nb * 32 + 2])
            a, b = parts
            middle = jnp.where(mid_first, a[:, 8:16], b[:, 0:8])
            return jnp.concatenate([a[:, 0:8], middle, b[:, 8:16]], axis=1), moms

        first, moms = gather(phonon[:, pair * 24 : pair * 24 + 24, :], True)
        for odd in range(2):
            sums_out[2 * pair + odd : 2 * pair + odd + 1, :] = moms[odd]
        ups = []
        for b in range(nb):
            up = first[b] + stores[b] * inflow
            share = share + (means[b] * betas[b]) * jnp.sum(up, axis=0, keepdims=True)
            ups.append(up[None])
        second, _ = gather(jnp.concatenate(ups, axis=0), False)
        again_out[:, pair * 24 : pair * 24 + 24, :] = second
        total = jnp.zeros((24, 512), F32)
        for b in range(nb):
            total = total + (betas[b] * betas[b]) * second[b] + (betas[b] * stores[b]) * inflow
        vscr[pair * 24 : pair * 24 + 24, :] = total + sum_ab * jnp.where(first_half, moms[0], moms[1])

    m1 = carry * m0 + share
    sums_out[8:9, :] = m1
    field_sum = vscr[...] + sum_alpha * m1
    cscr[...] = jnp.zeros((8, 128), F32)
    cscr[0:6, 0:96] = cosines[...]
    by_side = jnp.dot(
        cscr[:, 0:96], field_sum, precision=lax.Precision.HIGHEST, preferred_element_type=F32
    )

    hot = jnp.where(iota((512, 256), 0) == behind[...], 1.0, 0.0).astype(BF16)
    h, l = halves(by_side)
    at_face = dot(jnp.concatenate([h.astype(F32), l.astype(F32)], axis=0).astype(BF16), hot)
    at_face = at_face[0:8] + at_face[8:16]
    flux = jnp.sum(jnp.where(iota((8, 256), 0) == side[...], at_face, 0.0), axis=0, keepdims=True)
    owner_row = owners[...]
    column = jnp.broadcast_to(owner_row.astype(F32), (128, 256)).T
    column = jnp.concatenate([column, column], axis=1)
    same = (column == owner_row.astype(F32)) & (iota((256, 256), 0) < iota((256, 256), 1))
    place = jnp.sum(jnp.where(same, 1.0, 0.0), axis=0, keepdims=True).astype(jnp.int32)
    slot = owner_row * 8 + place
    slots = jnp.where(iota((512, 256), 0) == slot, 1.0, 0.0).astype(BF16)
    h, l = halves(flux)
    line = iota((16, 256), 0)
    target = beyond[...]
    rows = jnp.where(line == 0, h.astype(F32), 0.0)
    rows = jnp.where(line == 1, l.astype(F32), rows)
    rows = jnp.where(line == 2, (target >> 7).astype(F32), rows)
    rows = jnp.where(line == 3, (target & 127).astype(F32), rows)
    packed = dot_nt(rows.astype(BF16), slots)
    sums_out[9:10, :] = packed[0:1] + packed[1:2]
    sums_out[10:11, :] = packed[2:3] * 128.0 + packed[3:4]


def deal_body(sums_a, sums_b, sums_c, sums_d, out, scr):
    scr[...] = jnp.zeros(scr.shape, F32)
    scr[0:1, 128:640] = (sums_a[9:10, :] + sums_b[9:10, :]) + (sums_c[9:10, :] + sums_d[9:10, :])
    scr[1:2, 128:640] = sums_a[10:11, :]
    lead = 128 - 8 * (DMAX // 2)
    for q, (x, y) in enumerate(PATH):
        at = lead + 32 * q
        base = at // 128 * 128
        rolled = pltpu.roll(scr[:, base : base + 256], (256 - (at - base)) % 256, 1)[0:2, 0:128]
        for device in (2 * (4 * y + x), 2 * (4 * y + x) + 1):
            out[device] = rolled
            out[32 + device] = rolled


def finish_body(rates, again, sums_a, sums_b, sums_c, sums_d, inflow, energy_out):
    nb = again.shape[0]
    first_half = iota((24, 512), 0) < 12
    sums = (sums_a[...] + sums_b[...]) + (sums_c[...] + sums_d[...])
    m1 = sums[8:9, :]
    for pair in range(4):
        span = slice(pair * 24, pair * 24 + 24)
        mom = jnp.where(first_half, sums[2 * pair : 2 * pair + 1, :], sums[2 * pair + 1 : 2 * pair + 2, :])
        blank = inflow[span, :]
        for b in range(nb):
            alpha = rates[b : b + 1, :]
            beta = rates[nb + b : nb + b + 1, :]
            storage = rates[2 * nb + b : 2 * nb + b + 1, :]
            upstream = beta * again[b, span, :] + alpha * mom + storage * blank
            energy_out[b, span, :] = alpha * m1 + beta * upstream


def pack_body(where, table, thermal, label, sink, bulk, first_out, second_out):
    for number, out in ((6, first_out), (7, second_out)):
        start = where[number]
        for row in range(2):
            for t in range(TILES):
                at = pl.ds(start + t, 8, stride=TILES)
                out[0, row, t] = thermal[row, at, :]
                kinds = label[row, at, :]
                k = jnp.zeros((8, 128), F32)
                for mat in range(8):
                    k = jnp.where(kinds == mat, table[mat], k)
                out[1, row, t] = k
                out[2, row, t] = sink[row, at, :]
                out[3, row, t] = bulk[row, at, :]


def join_body(where, first, second, block_out, sems):
    swap = where[4]
    copies = [
        pltpu.make_async_copy(piece, block_out.at[:, pl.ds(2 * at, 2)], sems.at[number])
        for number, (piece, at) in enumerate(((first, swap), (second, 1 - swap)))
    ]
    for copy in copies:
        copy.start()
    for copy in copies:
        copy.wait()


def next_sublane(v):
    return pltpu.roll(v, 7, 0)


def last_sublane(v):
    return pltpu.roll(v, 1, 0)


def lane_ahead(v):
    return pltpu.roll(v, 127, 1)


def lane_behind(v):
    return pltpu.roll(v, 1, 1)


def assemble(core, lefts, own, rights, others, numbers, outs):
    for this, (before, after) in ((0, (lefts, others)), (1, (others, rights))):

        @pl.when(core == this)
        def _(before=before, after=after):
            for number, out in zip(numbers, outs):
                out[DMAX : DMAX + OWN] = own[number]
                for n, piece in enumerate(before):
                    at = DMAX - OWN * (n + 1)
                    out[at : at + OWN] = piece[number]
                for n, piece in enumerate(after):
                    at = DMAX + OWN * (n + 1)
                    out[at : at + OWN] = piece[number]


def faces_body(where, arrived, out, amounts, targets):
    start, core = where[1], where[5]
    for number, scr in ((0, amounts), (1, targets)):
        scr[:, 0:64] = arrived[:, number, :].T
    for o in range(OWNERS):
        at = pl.ds(pl.multiple_of(8 * o + 16 * core, 8), 8)
        slots = amounts[at, 0:64]
        amount = jnp.concatenate([slots[q : q + 1] for q in range(8)], axis=1)
        slots = targets[at, 0:64]
        target = jnp.concatenate([slots[q : q + 1] for q in range(8)], axis=1).astype(jnp.int32)
        y = ((target >> 7) & 127) - start
        inside = (y >= 0) & (y < WIN)
        s = (y * 37) >> 8
        place = jnp.where(inside, (target >> 14) * WIN + (y - TILES * s) * 8 + s, -1)
        hit = iota((2 * WIN, 512), 0) == place
        high = amount.astype(BF16).astype(F32)
        low = amount - high
        left = jnp.concatenate([jnp.where(hit, high, 0.0), jnp.where(hit, low, 0.0)], axis=0).astype(BF16)
        lanes = jnp.where(iota((128, 512), 0) == (target & 127), 1.0, 0.0).astype(BF16)
        got = dot_nt(left, lanes)
        out[2 * o : 2 * o + 2] = (got[: 2 * WIN] + got[2 * WIN :]).reshape(2, TILES, 8, 128)


def coefficients(where, k_in, faces, wx, wy, wz, wb, diag, rhs):
    first_row, start = where[0], where[1]
    shape = (8, 128)
    lane = iota(shape, 1)
    z_edge = jnp.where((lane == 0) | (lane == 127), 0.5, 0.0)
    z_half = jnp.where(lane == 127, 0.0, 0.5)
    b_half = jnp.where(lane == 0, 0.0, 0.5)
    last_half = jnp.where(iota(shape, 0) == 7, 0.0, 0.5)

    def link(row):
        return jnp.where((row >= 0) & (row < 127), 0.5, 0.0).astype(F32)

    def one(i):
        row = first_row + i
        after, before = link(row), link(row - 1)
        at_end = jnp.where((row == 0) | (row == 127), 0.5, 0.0).astype(F32)
        up, down = jnp.minimum(i + 1, EXT - 1), jnp.maximum(i - 1, 0)
        ks = [k_in[i, t] for t in range(TILES)]
        ys = [0.5 * (ks[t] + ks[t + 1]) for t in range(TILES - 1)]
        ys.append(last_half * (ks[TILES - 1] + next_sublane(ks[0])))
        for t in range(TILES):
            k = ks[t]
            column = TILES * iota(shape, 0) + (start + t)
            edge = z_edge + at_end + jnp.where((column == 0) | (column == 127), 0.5, 0.0)
            x_after = after * (k + k_in[up, t])
            x_before = before * (k + k_in[down, t])
            z_after = z_half * (k + lane_ahead(k))
            z_before = b_half * (k + lane_behind(k))
            y_before = ys[t - 1] if t else last_sublane(ys[TILES - 1])
            wx[i, t] = x_after
            wy[i, t] = ys[t]
            wz[i, t] = z_after
            wb[i, t] = z_before
            links = (x_after + x_before) + (ys[t] + y_before) + (z_after + z_before)
            diag[i, t] = (diag[i, t] + edge * k) + links
            rhs[i, t] = rhs[i, t] + faces[i, t]

    def four(n, _):
        for q in range(4):
            one(4 * n + q)
        return 0

    lax.fori_loop(0, EXT // 4, four, 0)


def steps(depth, rates, first, x_even, x_odd, d, wx, wy, wz, wb, diag, rhs):
    shift = DMAX - depth

    def rows(i, count, c1, c2, old, new):
        columns = [[old[i - 1 + q, t] for q in range(count + 2)] for t in (TILES - 1, 0)]
        before = [last_sublane(columns[0][q + 1]) for q in range(count)]
        after_end = [next_sublane(columns[1][q + 1]) for q in range(count)]
        y_before = [last_sublane(wy[i + q, TILES - 1]) for q in range(count)]
        here = columns[1]
        for t in range(TILES):
            ahead = [old[i - 1 + q, t + 1] for q in range(count + 2)] if t < TILES - 1 else None
            x_before = wx[i - 1, t]
            for q in range(count):
                v = here[q + 1]
                y_here, x_here = wy[i + q, t], wx[i + q, t]
                total = rhs[i + q, t] - diag[i + q, t] * v
                total = total + (x_here * here[q + 2] + x_before * here[q])
                total = total + (y_here * (ahead[q + 1] if ahead else after_end[q]) + y_before[q] * before[q])
                total = total + (wz[i + q, t] * lane_ahead(v) + wb[i + q, t] * lane_behind(v))
                step = c2 * total + c1 * d[i + q, t]
                d[i + q, t] = step
                new[i + q, t] = v + step
                before[q], y_before[q], x_before = v, y_here, x_here
            here = ahead

    def one(k, old, new):
        c1, c2 = rates[first + k, 0], rates[first + k, 1]
        low = shift + k + 1
        count = OWN + 2 * (depth - 1 - k)

        def several(n, _):
            rows(low + BODY * n, BODY, c1, c2, old, new)
            return 0

        bodies = count // BODY
        lax.fori_loop(0, bodies, several, 0)
        for tail in (2, 4, 6):

            @pl.when(count % BODY == tail)
            def _(tail=tail):
                rows(low + BODY * bodies, tail, c1, c2, old, new)

    def both(n, _):
        one(2 * n, x_even, x_odd)
        one(2 * n + 1, x_odd, x_even)
        return 0

    lax.fori_loop(0, depth // 2, both, 0)


def first_round_body(where, rates, *refs):
    own, near, far, third, other_own, other_near, other_far, faces = refs[:8]
    out, wx, wy, wz, wb, diag, rhs, xa, xb, d = refs[8:]
    mine = (near, far, third)
    assemble(
        where[5], mine, own, mine, (other_own, other_near, other_far), (0, 1, 2, 3), (xa, xb, diag, rhs)
    )
    coefficients(where, xb, faces, wx, wy, wz, wb, diag, rhs)
    d[...] = jnp.zeros(d.shape, F32)
    steps(DMAX, rates, 0, xa, xb, d, wx, wy, wz, wb, diag, rhs)
    for number, ref in ((0, xa), (1, d)):
        out[number] = ref[DMAX : DMAX + OWN]


def last_round_body(where, rates, wx, wy, wz, wb, diag, rhs, own, near, far, other_own, other_near, *rest):
    out, xa, xb, d = rest
    assemble(where[5], (near, far), own, (near, far), (other_own, other_near), (0, 1), (xa, d))
    steps(LATER, rates, DMAX, xa, xb, d, wx, wy, wz, wb, diag, rhs)
    offset = where[2]
    for j in range(16):
        y = offset + j
        s = (y * 37) >> 8
        t = y - TILES * s
        for row in range(OWN):
            out[row, j : j + 1, :] = xa[DMAX + row, t, pl.ds(s, 1), :]


def place_body(where, *refs):
    out = refs[4]
    core, band, half = where[5], where[8], where[9]
    for n in range(4):
        source = (band + (4 - n)) % 4
        for other in range(2):
            block = 4 * ((half + core + other) % 2) + source
            out[:, pl.ds(pl.multiple_of(16 * block, 16), 16), :] = refs[n][other, pl.ds(2 * core, 2)]


def on_device(
    phonon_deviation,
    thermal_field,
    bulk_generation,
    ambient_coupling,
    substance_label,
    material_conductance_table,
    mode_specific_warmth,
    mode_lifetime,
    mode_velocity_ratio,
    angular_cosine_factor,
    region_mesh_node,
    upstream_neighbour,
    interior_local_node,
    boundary_orientation,
    neighbour_partition,
    exterior_local_node,
):
    nb, nd, cells = phonon_deviation.shape
    tile = lax.axis_index("space")
    band = lax.axis_index("band")
    half = tile // 32
    plane = half * 4 + band
    other = (plane + 4) % 8
    chip = (tile % 32) // 2
    order = jnp.int32(0)
    for q, (x, y) in enumerate(PATH):
        order = jnp.where(chip == 4 * y + x, q, order)
    place = 2 * order + tile % 2
    stays = tile % 2 == 0

    def start_of(z):
        return jnp.clip(16 * z - 20, 0, 128 - WIN)

    start = start_of(plane)
    where = jnp.stack(
        [
            4 * place - DMAX,
            start,
            16 * plane - start,
            band * nb,
            jnp.where(place // 16 == half, 0, 1),
            tile % 2,
            jnp.where(stays, start, start_of(other)),
            jnp.where(stays, start_of(other), start),
            band,
            half,
        ]
    ).astype(jnp.int32)
    ext = sds(EXT, TILES, 8, 128)

    pack_shape = sds(4, 2, TILES, 8, 128)
    first, second = call(
        pack_body, [pack_shape, pack_shape], ins=[IN_SMEM, IN_SMEM] + [IN_VMEM] * 4, moved=3 << 20,
        grant=VMEM_MOST,
    )(where, material_conductance_table, thermal_field, substance_label, ambient_coupling, bulk_generation)
    first, second, where = lax.optimization_barrier((first, second, where))
    got_first = lax.ppermute(first, BOTH, chip_perm((0, 1)))
    got_second = lax.ppermute(second, BOTH, chip_perm((1, 0)))

    again, sums, inflow, rates = call(
        transport_body,
        [sds(nb, nd, cells), sds(11, cells), sds(nd, cells), sds(3 * nb, cells)],
        ins=[IN_SMEM] * 4 + [IN_VMEM] * 9,
        scratch=[pltpu.VMEM((nd, cells), F32), pltpu.VMEM((8, 128), F32)],
        flops=2 * 1600 * 512 * 512 * 4,
        moved=4 << 20,
        grant=VMEM_MOST,
    )(
        where,
        mode_specific_warmth,
        mode_lifetime,
        mode_velocity_ratio,
        phonon_deviation,
        thermal_field.reshape(256, 128),
        region_mesh_node.reshape(1, -1),
        upstream_neighbour,
        interior_local_node.reshape(1, -1),
        boundary_orientation.reshape(1, -1),
        neighbour_partition.reshape(1, -1),
        exterior_local_node.reshape(1, -1),
        angular_cosine_factor,
    )
    shares = [sums] + [
        lax.ppermute(sums, "band", [(i, (i + turn) % 4) for i in range(4)]) for turn in (1, 2, 3)
    ]

    packets = call(
        deal_body,
        sds(64, 2, 128),
        ins=[IN_VMEM] * 4,
        scratch=[pltpu.VMEM((8, 768), F32)],
        moved=1 << 18,
    )(*shares)

    packets, got_first, got_second = lax.optimization_barrier((packets, got_first, got_second))
    block = call(
        join_body,
        sds(4, OWN, TILES, 8, 128),
        ins=[IN_SMEM, ANYWHERE, ANYWHERE],
        scratch=[pltpu.SemaphoreType.DMA((2,))],
        moved=2 << 20,
        space=pl.ANY,
    )(where, got_first, got_second)
    packets, block = lax.optimization_barrier((packets, block))
    near = lax.ppermute(block, BOTH, NEXT)
    far = lax.ppermute(block, BOTH, SECOND)
    third = lax.ppermute(block, BOTH, THIRD)
    other_own = lax.ppermute(block, BOTH, SIBLING)
    arrived = lax.all_to_all(packets, "space", split_axis=0, concat_axis=0, tiled=True)
    near, far, third, other_own, arrived = lax.optimization_barrier((near, far, third, other_own, arrived))
    other_near = lax.ppermute(near, BOTH, SIBLING)
    other_far = lax.ppermute(far, BOTH, SIBLING)
    faces = call(
        faces_body,
        ext,
        ins=[IN_SMEM, IN_VMEM],
        scratch=[pltpu.VMEM((128, 128), F32)] * 2,
        flops=1 << 30,
        moved=1 << 20,
    )(where, arrived)

    factors = jnp.array(chebyshev_table(ITERS), F32)
    work = 25 * DMAX * (OWN + DMAX) * 8192
    scratch = [pltpu.VMEM((EXT, TILES, 8, 128), F32)] * 3
    state, *operator = call(
        first_round_body,
        [sds(2, OWN, TILES, 8, 128)] + [ext] * 6,
        ins=[IN_SMEM] * 2 + [IN_VMEM] * 8,
        scratch=scratch,
        flops=work,
        moved=8 << 20,
    )(where, factors, block, near, far, third, other_own, other_near, other_far, faces)
    near = lax.ppermute(state, BOTH, NEXT)
    far = lax.ppermute(state, BOTH, SECOND)
    other_own = lax.ppermute(state, BOTH, SIBLING)
    other_near = lax.ppermute(state, BOTH, ACROSS)
    energy = call(
        finish_body,
        sds(nb, nd, cells),
        ins=[IN_VMEM] * 7,
        flops=8 * nb * nd * cells,
        moved=3 << 20,
    )(rates, again, *shares, inflow)
    near, far, other_own, other_near, energy = lax.optimization_barrier(
        (near, far, other_own, other_near, energy)
    )
    state = call(
        last_round_body,
        sds(OWN, 16, 128),
        ins=[IN_SMEM] * 2 + [IN_VMEM] * 11,
        scratch=scratch,
        flops=work,
        moved=8 << 20,
    )(where, factors, *operator, state, near, far, other_own, other_near)

    rows = lax.ppermute(state, BOTH, [(b, a) for a, b in chip_perm((0, 1))])
    rows = jnp.stack([rows, lax.ppermute(rows, BOTH, SIBLING)])
    pieces = [rows] + [
        lax.ppermute(rows, "band", [(i, (i + turn) % 4) for i in range(4)]) for turn in (1, 2, 3)
    ]
    temperature = call(place_body, sds(2, 128, 128), ins=[IN_SMEM] + [IN_VMEM] * 4, moved=1 << 18)(
        where, *pieces
    )
    return temperature, energy


def solution(mesh):
    return jax.shard_map(
        on_device,
        mesh=mesh,
        in_specs=(
            P("band", None, "space"),
            P("space", None, None),
            P("space", None, None),
            P("space", None, None),
            P("space", None, None),
            P(),
            P(),
            P(),
            P(),
            P(),
            P("space"),
            P(None, "space"),
            P("space"),
            P("space"),
            P("space", None),
            P("space"),
        ),
        out_specs=(P("space", None, None), P("band", None, "space")),
        check_vma=False,
    )
```

```python
import jax
import jax.numpy as jnp
from jax import lax
from jax.experimental import pallas as pl
from jax.experimental.pallas import tpu as pltpu
from jax.sharding import PartitionSpec as P

ITERS = 20
BOTH = ("space", "band")
F32 = jnp.float32
BF16 = jnp.bfloat16
VMEM_BYTES = 24 * 1024 * 1024
VMEM_MOST = 56 * 1024 * 1024

DMAX = 12
LATER = ITERS - DMAX
OWN = 4
EXT = OWN + 2 * DMAX
BODY = 12
OWNERS = EXT // 2
TILES = 7
WIN = 8 * TILES

lowest = 0.5
highest = 50.0


def chebyshev_table(count):
    centre = (highest + lowest) / 2.0
    spread = (highest - lowest) / 2.0
    ratio = centre / spread
    rho_prev = 1.0 / ratio
    table = [(0.0, 1.0 / centre)]
    for number in range(1, count):
        rho_next = 1.0 / (2.0 * ratio - rho_prev)
        table.append((rho_next * rho_prev, 2.0 * rho_next / spread))
        rho_prev = rho_next
    return table


PATH = (
    (3, 0), (2, 0), (2, 1), (3, 1), (3, 2), (3, 3), (2, 3), (2, 2),
    (1, 1), (1, 0), (0, 0), (0, 1), (0, 2), (1, 2), (1, 3), (0, 3),
)


def spot_of(m):
    x, y = PATH[m // 2]
    return (y * 4 + x) * 2 + m % 2


def flat(z, spot):
    return ((z // 4) * 32 + spot) * 4 + z % 4


def along(move):
    return [
        (flat(z, spot_of(m)), flat(z, spot_of(move(m))))
        for z in range(8)
        for m in range(32)
        if 0 <= move(m) < 32
    ]


NEXT = along(lambda m: m + 1 if m % 2 else m - 1)
SECOND = along(lambda m: m - 2 if m % 2 else m + 2)
THIRD = along(lambda m: m + 3 if m % 2 else m - 3)
SIBLING = along(lambda m: m ^ 1)


def chip_perm(cores):
    pairs = []
    for z in range(8):
        for chip in range(16):
            place = spot_of(chip + 16 * (z // 4))
            for core, target in zip(cores, (z, (z + 4) % 8)):
                pairs.append((flat(z, 2 * chip + core), flat(target, place)))
    return pairs


def call(body, outs, *, ins, scratch=(), flops=0, moved=0, space=pltpu.VMEM, grant=VMEM_BYTES):
    return pl.pallas_call(
        body,
        out_shape=outs,
        in_specs=ins,
        out_specs=jax.tree.map(lambda _: pl.BlockSpec(memory_space=space), outs),
        scratch_shapes=list(scratch),
        compiler_params=pltpu.CompilerParams(vmem_limit_bytes=grant),
        cost_estimate=pl.CostEstimate(flops=flops, bytes_accessed=moved, transcendentals=0),
    )


IN_VMEM = pl.BlockSpec(memory_space=pltpu.VMEM)
IN_SMEM = pl.BlockSpec(memory_space=pltpu.SMEM)
ANYWHERE = pl.BlockSpec(memory_space=pl.ANY)


def sds(*shape):
    return jax.ShapeDtypeStruct(shape, F32)


def halves(values):
    high = values.astype(BF16)
    low = (values - high.astype(F32)).astype(BF16)
    return high, low


def dot(a, b):
    return jnp.dot(a, b, preferred_element_type=F32)


def dot_nt(a, b):
    return lax.dot_general(a, b, (((1,), (1,)), ((), ())), preferred_element_type=F32)


def iota(shape, axis):
    return lax.broadcasted_iota(jnp.int32, shape, axis)


def full(value, width=128):
    return jnp.full((1, width), value, F32)


def wide(row):
    return jnp.concatenate([row] * 4, axis=1)


def transport_body(
    where, warmth, lifetime, velocity, phonon, field, node, upwind, behind, side, owners, beyond, cosines,
    again_out, sums_out, inflow_out, rates_out, vscr, cscr,
):
    nb, nd, _ = phonon.shape
    first_band = where[3]

    capacity, sum_alpha, sum_ab, carry = full(0.0), full(0.0), full(0.0), full(0.0)
    for b in range(warmth.shape[0]):
        storage, speed, weight = full(warmth[b]), full(velocity[b]), 1.0 / full(lifetime[b])
        scale = 1.0 / (speed + weight)
        alpha, beta = storage * weight * scale, speed * scale
        capacity = capacity + storage * weight
        sum_alpha = sum_alpha + alpha
        sum_ab = sum_ab + alpha * beta
        carry = carry + alpha * weight
    unit = 1.0 / (nd * capacity)
    carry, sum_alpha, sum_ab = wide(carry / capacity), wide(sum_alpha), wide(sum_ab)
    alphas, betas, stores, means = [], [], [], []
    for b in range(nb):
        storage = full(warmth[first_band + b])
        speed, weight = full(velocity[first_band + b]), 1.0 / full(lifetime[first_band + b])
        scale = 1.0 / (speed + weight)
        alphas.append(wide(storage * weight * scale))
        betas.append(wide(speed * scale))
        stores.append(wide(storage))
        means.append(wide(weight * unit))
        rates_out[b : b + 1, :] = alphas[b]
        rates_out[nb + b : nb + b + 1, :] = betas[b]
        rates_out[2 * nb + b : 2 * nb + b + 1, :] = stores[b]

    cell = node[...]
    rows_hot = jnp.where(iota((256, 512), 0) == (cell >> 7), 1.0, 0.0).astype(BF16)
    turned = field[...].T
    high, low = halves(turned)
    picked = dot(high, rows_hot) + dot(low, rows_hot)
    patch = jnp.sum(jnp.where(iota((128, 512), 0) == (cell & 127), picked, 0.0), axis=0, keepdims=True)

    m0 = jnp.zeros((1, 512), F32)
    for b in range(nb):
        m0 = m0 + means[b] * jnp.sum(phonon[b], axis=0, keepdims=True)
    m0h, m0l = halves(m0)
    m0_rows = jnp.where(
        iota((16, 512), 0) == 0, m0h.astype(F32), jnp.where(iota((16, 512), 0) == 1, m0l.astype(F32), 0.0)
    ).astype(BF16)

    first_half = iota((24, 512), 0) < 12
    mid_first = iota((1, 8, 512), 1) < 4
    share = jnp.zeros((1, 512), F32)
    for pair in range(4):
        hots, blanks = [], []
        for odd in range(2):
            source = upwind[2 * pair + odd : 2 * pair + odd + 1, :]
            hots.append(jnp.where(iota((512, 512), 0) == source, 1.0, 0.0).astype(BF16))
            blanks.append(jnp.where(source < 0, patch, 0.0))
        inflow = jnp.where(first_half, blanks[0], blanks[1])
        inflow_out[pair * 24 : pair * 24 + 24, :] = inflow

        def gather(values, extra):
            parts = []
            moms = []
            for odd in range(2):
                chunk = values[:, 8 * odd : 8 * odd + 16, :].reshape(nb * 16, 512)
                h, l = halves(chunk)
                pieces = [h, l] + ([m0_rows] if extra else [])
                got = dot(jnp.concatenate(pieces, axis=0), hots[odd])
                parts.append((got[: nb * 16] + got[nb * 16 : nb * 32]).reshape(nb, 16, 512))
                if extra:
                    moms.append(got[nb * 32 : nb * 32 + 1] + got[nb * 32 + 1 : nb * 32 + 2])
            a, b = parts
            middle = jnp.where(mid_first, a[:, 8:16], b[:, 0:8])
            return jnp.concatenate([a[:, 0:8], middle, b[:, 8:16]], axis=1), moms

        first, moms = gather(phonon[:, pair * 24 : pair * 24 + 24, :], True)
        for odd in range(2):
            sums_out[2 * pair + odd : 2 * pair + odd + 1, :] = moms[odd]
        ups = []
        for b in range(nb):
            up = first[b] + stores[b] * inflow
            share = share + (means[b] * betas[b]) * jnp.sum(up, axis=0, keepdims=True)
            ups.append(up[None])
        second, _ = gather(jnp.concatenate(ups, axis=0), False)
        again_out[:, pair * 24 : pair * 24 + 24, :] = second
        total = jnp.zeros((24, 512), F32)
        for b in range(nb):
            total = total + (betas[b] * betas[b]) * second[b] + (betas[b] * stores[b]) * inflow
        vscr[pair * 24 : pair * 24 + 24, :] = total + sum_ab * jnp.where(first_half, moms[0], moms[1])

    m1 = carry * m0 + share
    sums_out[8:9, :] = m1
    field_sum = vscr[...] + sum_alpha * m1
    cscr[...] = jnp.zeros((8, 128), F32)
    cscr[0:6, 0:96] = cosines[...]
    by_side = jnp.dot(
        cscr[:, 0:96], field_sum, precision=lax.Precision.HIGHEST, preferred_element_type=F32
    )

    hot = jnp.where(iota((512, 256), 0) == behind[...], 1.0, 0.0).astype(BF16)
    h, l = halves(by_side)
    at_face = dot(jnp.concatenate([h.astype(F32), l.astype(F32)], axis=0).astype(BF16), hot)
    at_face = at_face[0:8] + at_face[8:16]
    flux = jnp.sum(jnp.where(iota((8, 256), 0) == side[...], at_face, 0.0), axis=0, keepdims=True)
    owner_row = owners[...]
    column = jnp.broadcast_to(owner_row.astype(F32), (128, 256)).T
    column = jnp.concatenate([column, column], axis=1)
    same = (column == owner_row.astype(F32)) & (iota((256, 256), 0) < iota((256, 256), 1))
    place = jnp.sum(jnp.where(same, 1.0, 0.0), axis=0, keepdims=True).astype(jnp.int32)
    slot = owner_row * 8 + place
    slots = jnp.where(iota((512, 256), 0) == slot, 1.0, 0.0).astype(BF16)
    h, l = halves(flux)
    line = iota((16, 256), 0)
    target = beyond[...]
    rows = jnp.where(line == 0, h.astype(F32), 0.0)
    rows = jnp.where(line == 1, l.astype(F32), rows)
    rows = jnp.where(line == 2, (target >> 7).astype(F32), rows)
    rows = jnp.where(line == 3, (target & 127).astype(F32), rows)
    packed = dot_nt(rows.astype(BF16), slots)
    sums_out[9:10, :] = packed[0:1] + packed[1:2]
    sums_out[10:11, :] = packed[2:3] * 128.0 + packed[3:4]


def deal_body(sums_a, sums_b, sums_c, sums_d, out, scr):
    scr[...] = jnp.zeros(scr.shape, F32)
    scr[0:1, 128:640] = (sums_a[9:10, :] + sums_b[9:10, :]) + (sums_c[9:10, :] + sums_d[9:10, :])
    scr[1:2, 128:640] = sums_a[10:11, :]
    lead = 128 - 8 * (DMAX // 2)
    for q, (x, y) in enumerate(PATH):
        at = lead + 32 * q
        base = at // 128 * 128
        rolled = pltpu.roll(scr[:, base : base + 256], (256 - (at - base)) % 256, 1)[0:2, 0:128]
        for device in (2 * (4 * y + x), 2 * (4 * y + x) + 1):
            out[device] = rolled
            out[32 + device] = rolled


def finish_body(rates, again, sums_a, sums_b, sums_c, sums_d, inflow, energy_out):
    nb = again.shape[0]
    first_half = iota((24, 512), 0) < 12
    sums = (sums_a[...] + sums_b[...]) + (sums_c[...] + sums_d[...])
    m1 = sums[8:9, :]
    for pair in range(4):
        span = slice(pair * 24, pair * 24 + 24)
        mom = jnp.where(first_half, sums[2 * pair : 2 * pair + 1, :], sums[2 * pair + 1 : 2 * pair + 2, :])
        blank = inflow[span, :]
        for b in range(nb):
            alpha = rates[b : b + 1, :]
            beta = rates[nb + b : nb + b + 1, :]
            storage = rates[2 * nb + b : 2 * nb + b + 1, :]
            upstream = beta * again[b, span, :] + alpha * mom + storage * blank
            energy_out[b, span, :] = alpha * m1 + beta * upstream


def pack_body(where, table, thermal, label, sink, bulk, first_out, second_out):
    for number, out in ((6, first_out), (7, second_out)):
        start = where[number]
        for row in range(2):
            for t in range(TILES):
                at = pl.ds(start + t, 8, stride=TILES)
                out[0, row, t] = thermal[row, at, :]
                kinds = label[row, at, :]
                k = jnp.zeros((8, 128), F32)
                for mat in range(8):
                    k = jnp.where(kinds == mat, table[mat], k)
                out[1, row, t] = k
                out[2, row, t] = sink[row, at, :]
                out[3, row, t] = bulk[row, at, :]


def join_body(where, first, second, block_out, sems):
    swap = where[4]
    copies = [
        pltpu.make_async_copy(piece, block_out.at[:, pl.ds(2 * at, 2)], sems.at[number])
        for number, (piece, at) in enumerate(((first, swap), (second, 1 - swap)))
    ]
    for copy in copies:
        copy.start()
    for copy in copies:
        copy.wait()


def next_sublane(v):
    return pltpu.roll(v, 7, 0)


def last_sublane(v):
    return pltpu.roll(v, 1, 0)


def lane_ahead(v):
    return pltpu.roll(v, 127, 1)


def lane_behind(v):
    return pltpu.roll(v, 1, 1)


def assemble(core, lefts, own, rights, others, numbers, outs):
    for this, (before, after) in ((0, (lefts, others)), (1, (others, rights))):

        @pl.when(core == this)
        def _(before=before, after=after):
            for number, out in zip(numbers, outs):
                out[DMAX : DMAX + OWN] = own[number]
                for n, piece in enumerate(before):
                    at = DMAX - OWN * (n + 1)
                    out[at : at + OWN] = piece[number]
                for n, piece in enumerate(after):
                    at = DMAX + OWN * (n + 1)
                    out[at : at + OWN] = piece[number]


def faces_body(where, arrived, out, amounts, targets):
    start, core = where[1], where[5]
    for number, scr in ((0, amounts), (1, targets)):
        scr[:, 0:64] = arrived[:, number, :].T
    for o in range(OWNERS):
        at = pl.ds(pl.multiple_of(8 * o + 16 * core, 8), 8)
        slots = amounts[at, 0:64]
        amount = jnp.concatenate([slots[q : q + 1] for q in range(8)], axis=1)
        slots = targets[at, 0:64]
        target = jnp.concatenate([slots[q : q + 1] for q in range(8)], axis=1).astype(jnp.int32)
        y = ((target >> 7) & 127) - start
        inside = (y >= 0) & (y < WIN)
        s = (y * 37) >> 8
        place = jnp.where(inside, (target >> 14) * WIN + (y - TILES * s) * 8 + s, -1)
        hit = iota((2 * WIN, 512), 0) == place
        high = amount.astype(BF16).astype(F32)
        low = amount - high
        left = jnp.concatenate([jnp.where(hit, high, 0.0), jnp.where(hit, low, 0.0)], axis=0).astype(BF16)
        lanes = jnp.where(iota((128, 512), 0) == (target & 127), 1.0, 0.0).astype(BF16)
        got = dot_nt(left, lanes)
        out[2 * o : 2 * o + 2] = (got[: 2 * WIN] + got[2 * WIN :]).reshape(2, TILES, 8, 128)


def coefficients(where, k_in, faces, wx, wy, wz, wb, diag, rhs):
    first_row, start = where[0], where[1]
    shape = (8, 128)
    lane = iota(shape, 1)
    z_edge = jnp.where((lane == 0) | (lane == 127), 0.5, 0.0)
    z_half = jnp.where(lane == 127, 0.0, 0.5)
    b_half = jnp.where(lane == 0, 0.0, 0.5)
    last_half = jnp.where(iota(shape, 0) == 7, 0.0, 0.5)

    def link(row):
        return jnp.where((row >= 0) & (row < 127), 0.5, 0.0).astype(F32)

    def one(i):
        row = first_row + i
        after, before = link(row), link(row - 1)
        at_end = jnp.where((row == 0) | (row == 127), 0.5, 0.0).astype(F32)
        up, down = jnp.minimum(i + 1, EXT - 1), jnp.maximum(i - 1, 0)
        ks = [k_in[i, t] for t in range(TILES)]
        ys = [0.5 * (ks[t] + ks[t + 1]) for t in range(TILES - 1)]
        ys.append(last_half * (ks[TILES - 1] + next_sublane(ks[0])))
        for t in range(TILES):
            k = ks[t]
            column = TILES * iota(shape, 0) + (start + t)
            edge = z_edge + at_end + jnp.where((column == 0) | (column == 127), 0.5, 0.0)
            x_after = after * (k + k_in[up, t])
            x_before = before * (k + k_in[down, t])
            z_after = z_half * (k + lane_ahead(k))
            z_before = b_half * (k + lane_behind(k))
            y_before = ys[t - 1] if t else last_sublane(ys[TILES - 1])
            wx[i, t] = x_after
            wy[i, t] = ys[t]
            wz[i, t] = z_after
            wb[i, t] = z_before
            links = (x_after + x_before) + (ys[t] + y_before) + (z_after + z_before)
            diag[i, t] = (diag[i, t] + edge * k) + links
            rhs[i, t] = rhs[i, t] + faces[i, t]

    def four(n, _):
        for q in range(4):
            one(4 * n + q)
        return 0

    lax.fori_loop(0, EXT // 4, four, 0)


def steps(depth, rates, first, x_even, x_odd, d, wx, wy, wz, wb, diag, rhs):
    shift = DMAX - depth

    def rows(i, count, c1, c2, old, new):
        columns = [[old[i - 1 + q, t] for q in range(count + 2)] for t in (TILES - 1, 0)]
        before = [last_sublane(columns[0][q + 1]) for q in range(count)]
        after_end = [next_sublane(columns[1][q + 1]) for q in range(count)]
        y_before = [last_sublane(wy[i + q, TILES - 1]) for q in range(count)]
        here = columns[1]
        for t in range(TILES):
            ahead = [old[i - 1 + q, t + 1] for q in range(count + 2)] if t < TILES - 1 else None
            x_before = wx[i - 1, t]
            for q in range(count):
                v = here[q + 1]
                y_here, x_here = wy[i + q, t], wx[i + q, t]
                total = rhs[i + q, t] - diag[i + q, t] * v
                total = total + (x_here * here[q + 2] + x_before * here[q])
                total = total + (y_here * (ahead[q + 1] if ahead else after_end[q]) + y_before[q] * before[q])
                total = total + (wz[i + q, t] * lane_ahead(v) + wb[i + q, t] * lane_behind(v))
                step = c2 * total + c1 * d[i + q, t]
                d[i + q, t] = step
                new[i + q, t] = v + step
                before[q], y_before[q], x_before = v, y_here, x_here
            here = ahead

    def one(k, old, new):
        c1, c2 = rates[first + k, 0], rates[first + k, 1]
        low = shift + k + 1
        count = OWN + 2 * (depth - 1 - k)

        def several(n, _):
            rows(low + BODY * n, BODY, c1, c2, old, new)
            return 0

        bodies = count // BODY
        lax.fori_loop(0, bodies, several, 0)
        for tail in range(2, BODY, 2):

            @pl.when(count % BODY == tail)
            def _(tail=tail):
                rows(low + BODY * bodies, tail, c1, c2, old, new)

    def both(n, _):
        one(2 * n, x_even, x_odd)
        one(2 * n + 1, x_odd, x_even)
        return 0

    lax.fori_loop(0, depth // 2, both, 0)


def first_round_body(where, rates, *refs):
    own, near, far, third, other_own, other_near, other_far, faces = refs[:8]
    out, wx, wy, wz, wb, diag, rhs, xa, xb, d = refs[8:]
    mine = (near, far, third)
    assemble(
        where[5], mine, own, mine, (other_own, other_near, other_far), (0, 1, 2, 3), (xa, xb, diag, rhs)
    )
    coefficients(where, xb, faces, wx, wy, wz, wb, diag, rhs)
    d[...] = jnp.zeros(d.shape, F32)
    steps(DMAX, rates, 0, xa, xb, d, wx, wy, wz, wb, diag, rhs)
    for number, ref in ((0, xa), (1, d)):
        out[number] = ref[DMAX : DMAX + OWN]


def last_round_body(where, rates, wx, wy, wz, wb, diag, rhs, own, near, far, other_own, other_near, *rest):
    out, xa, xb, d = rest
    assemble(where[5], (near, far), own, (near, far), (other_own, other_near), (0, 1), (xa, d))
    steps(LATER, rates, DMAX, xa, xb, d, wx, wy, wz, wb, diag, rhs)
    offset = where[2]
    for j in range(16):
        y = offset + j
        s = (y * 37) >> 8
        t = y - TILES * s
        for row in range(OWN):
            out[row, j : j + 1, :] = xa[DMAX + row, t, pl.ds(s, 1), :]


def place_body(where, *refs):
    out = refs[4]
    core, band, half = where[5], where[8], where[9]
    for n in range(4):
        source = (band + (4 - n)) % 4
        for other in range(2):
            block = 4 * ((half + core + other) % 2) + source
            out[:, pl.ds(pl.multiple_of(16 * block, 16), 16), :] = refs[n][other, pl.ds(2 * core, 2)]


def on_device(
    phonon_deviation,
    thermal_field,
    bulk_generation,
    ambient_coupling,
    substance_label,
    material_conductance_table,
    mode_specific_warmth,
    mode_lifetime,
    mode_velocity_ratio,
    angular_cosine_factor,
    region_mesh_node,
    upstream_neighbour,
    interior_local_node,
    boundary_orientation,
    neighbour_partition,
    exterior_local_node,
):
    nb, nd, cells = phonon_deviation.shape
    tile = lax.axis_index("space")
    band = lax.axis_index("band")
    half = tile // 32
    plane = half * 4 + band
    other = (plane + 4) % 8
    chip = (tile % 32) // 2
    order = jnp.int32(0)
    for q, (x, y) in enumerate(PATH):
        order = jnp.where(chip == 4 * y + x, q, order)
    place = 2 * order + tile % 2
    stays = tile % 2 == 0

    def start_of(z):
        return jnp.clip(16 * z - 20, 0, 128 - WIN)

    start = start_of(plane)
    where = jnp.stack(
        [
            4 * place - DMAX,
            start,
            16 * plane - start,
            band * nb,
            jnp.where(place // 16 == half, 0, 1),
            tile % 2,
            jnp.where(stays, start, start_of(other)),
            jnp.where(stays, start_of(other), start),
            band,
            half,
        ]
    ).astype(jnp.int32)
    ext = sds(EXT, TILES, 8, 128)

    pack_shape = sds(4, 2, TILES, 8, 128)
    first, second = call(
        pack_body, [pack_shape, pack_shape], ins=[IN_SMEM, IN_SMEM] + [IN_VMEM] * 4, moved=3 << 20,
        grant=VMEM_MOST,
    )(where, material_conductance_table, thermal_field, substance_label, ambient_coupling, bulk_generation)
    first, second, where = lax.optimization_barrier((first, second, where))
    got_first = lax.ppermute(first, BOTH, chip_perm((0, 1)))
    got_second = lax.ppermute(second, BOTH, chip_perm((1, 0)))

    again, sums, inflow, rates = call(
        transport_body,
        [sds(nb, nd, cells), sds(11, cells), sds(nd, cells), sds(3 * nb, cells)],
        ins=[IN_SMEM] * 4 + [IN_VMEM] * 9,
        scratch=[pltpu.VMEM((nd, cells), F32), pltpu.VMEM((8, 128), F32)],
        flops=2 * 1600 * 512 * 512 * 4,
        moved=4 << 20,
        grant=VMEM_MOST,
    )(
        where,
        mode_specific_warmth,
        mode_lifetime,
        mode_velocity_ratio,
        phonon_deviation,
        thermal_field.reshape(256, 128),
        region_mesh_node.reshape(1, -1),
        upstream_neighbour,
        interior_local_node.reshape(1, -1),
        boundary_orientation.reshape(1, -1),
        neighbour_partition.reshape(1, -1),
        exterior_local_node.reshape(1, -1),
        angular_cosine_factor,
    )
    shares = [sums] + [
        lax.ppermute(sums, "band", [(i, (i + turn) % 4) for i in range(4)]) for turn in (1, 2, 3)
    ]

    packets = call(
        deal_body,
        sds(64, 2, 128),
        ins=[IN_VMEM] * 4,
        scratch=[pltpu.VMEM((8, 768), F32)],
        moved=1 << 18,
    )(*shares)

    packets, got_first, got_second = lax.optimization_barrier((packets, got_first, got_second))
    block = call(
        join_body,
        sds(4, OWN, TILES, 8, 128),
        ins=[IN_SMEM, ANYWHERE, ANYWHERE],
        scratch=[pltpu.SemaphoreType.DMA((2,))],
        moved=2 << 20,
        space=pl.ANY,
    )(where, got_first, got_second)
    packets, block = lax.optimization_barrier((packets, block))
    near = lax.ppermute(block, BOTH, NEXT)
    far = lax.ppermute(block, BOTH, SECOND)
    third = lax.ppermute(block, BOTH, THIRD)
    other_own = lax.ppermute(block, BOTH, SIBLING)
    arrived = lax.all_to_all(packets, "space", split_axis=0, concat_axis=0, tiled=True)
    near, far, third, other_own, arrived = lax.optimization_barrier((near, far, third, other_own, arrived))
    other_near = lax.ppermute(near, BOTH, SIBLING)
    other_far = lax.ppermute(far, BOTH, SIBLING)
    faces = call(
        faces_body,
        ext,
        ins=[IN_SMEM, IN_VMEM],
        scratch=[pltpu.VMEM((128, 128), F32)] * 2,
        flops=1 << 30,
        moved=1 << 20,
    )(where, arrived)

    factors = jnp.array(chebyshev_table(ITERS), F32)
    work = 25 * DMAX * (OWN + DMAX) * 8192
    scratch = [pltpu.VMEM((EXT, TILES, 8, 128), F32)] * 3
    state, *operator = call(
        first_round_body,
        [sds(2, OWN, TILES, 8, 128)] + [ext] * 6,
        ins=[IN_SMEM] * 2 + [IN_VMEM] * 8,
        scratch=scratch,
        flops=work,
        moved=8 << 20,
    )(where, factors, block, near, far, third, other_own, other_near, other_far, faces)
    near = lax.ppermute(state, BOTH, NEXT)
    far = lax.ppermute(state, BOTH, SECOND)
    other_own = lax.ppermute(state, BOTH, SIBLING)
    energy = call(
        finish_body,
        sds(nb, nd, cells),
        ins=[IN_VMEM] * 7,
        flops=8 * nb * nd * cells,
        moved=3 << 20,
    )(rates, again, *shares, inflow)
    near, far, other_own, energy = lax.optimization_barrier((near, far, other_own, energy))
    other_near = lax.ppermute(near, BOTH, SIBLING)
    state = call(
        last_round_body,
        sds(OWN, 16, 128),
        ins=[IN_SMEM] * 2 + [IN_VMEM] * 11,
        scratch=scratch,
        flops=work,
        moved=8 << 20,
    )(where, factors, *operator, state, near, far, other_own, other_near)

    rows = lax.ppermute(state, BOTH, [(b, a) for a, b in chip_perm((0, 1))])
    rows = jnp.stack([rows, lax.ppermute(rows, BOTH, SIBLING)])
    pieces = [rows] + [
        lax.ppermute(rows, "band", [(i, (i + turn) % 4) for i in range(4)]) for turn in (1, 2, 3)
    ]
    temperature = call(place_body, sds(2, 128, 128), ins=[IN_SMEM] + [IN_VMEM] * 4, moved=1 << 18)(
        where, *pieces
    )
    return temperature, energy


def solution(mesh):
    return jax.shard_map(
        on_device,
        mesh=mesh,
        in_specs=(
            P("band", None, "space"),
            P("space", None, None),
            P("space", None, None),
            P("space", None, None),
            P("space", None, None),
            P(),
            P(),
            P(),
            P(),
            P(),
            P("space"),
            P(None, "space"),
            P("space"),
            P("space"),
            P("space", None),
            P("space"),
        ),
        out_specs=(P("space", None, None), P("band", None, "space")),
        check_vma=False,
    )
```
